512 devices in a mesh: pole: 8 (over y), row: 16 (over z, core), col: 4 (over x).
Axes of the slice: x: 4, y: 8, z: 8, core: 2. Of those that a mesh axis runs over, the one named last changes fastest.
Arguments:
- front_h: bfloat16 [4096, 4096], P(('row', 'col')), may hold values from -6 to 6
- front_s: bfloat16 [4096, 4096], P(('row', 'col')), may hold values from -6 to 6
- panel_h: bfloat16 [4096, 256], P('row'), may hold values from -6 to 6
- panel_s: bfloat16 [4096, 256], P('row'), may hold values from -4 to 4
- pivot_h: bfloat16 [256, 256], replicated, may hold values from -1.7 to 8.5, as said below
- pivot_s: bfloat16 [256, 256], replicated, may hold values from -0.1 to 1.5, as said below
- pole_shift: float32 [8, 2], P('pole'), may hold values from -0.5 to 1.5, as said below
- pole_weight: float32 [8, 2], P('pole'), may hold values from -6 to 6
- pattern: int32 [16, 16], replicated, may hold values 0 or 1
- ancestor_inverse: bfloat16 [8, 2, 16, 4, 64, 4096], P('pole', None, None, 'col', None, 'row'), may hold values from -0.09375 to 0.09375
Outputs:
- schur: bfloat16 [8, 2, 16, 4, 64, 4096], P('pole', None, None, 'col', None, 'row')
- density_rows: float32 [4096, 256], P(('row', 'col'), 'pole')
- density_pivot: float32 [256, 256], P(None, 'pole')
The draws below stay inside these ranges and needn't reach their ends.
Inputs may be any that keep to these rules, and one draw needn't show every extreme that they name: `pivot_h`: symmetric; each row's off-diagonal entries sum in magnitude to at most 6.6, the diagonal lies in 8 to 8.5. `pivot_s`: symmetric; each row's off-diagonal entries sum in magnitude to at most 0.33, the diagonal lies in 1 to 1.5. `pole_shift`: column 0 lies in -0.5 to 0.5, column 1 in 0.25 to 1.5.
All inputs are finite; a program needn't handle non-finite values.
Results may differ from the reference program's by a relative error of at most 0.0063.
Values may be sent and summed in bfloat16 or wider, within the bound.
No kernel may reach another device: no remote copies, remote signals or barrier semaphores. Data moves between devices by JAX's collectives and lax.ppermute only.
A program may use at most 64 MiB of HBM per device.

```python
import jax
import jax.numpy as jnp
from jax import lax

SUPER = 256
NEWTON = 4
POLES = 8
NB = 16
ORDER = 4096
STRIP = 64
N_ROW = 16
N_COL = 4


def banded_symmetric(key, diag_lo, diag_hi, reach, inner):
    first, second = jax.random.split(key)
    index = jnp.arange(SUPER)
    gap = jnp.abs(index[:, None] - index[None, :])
    sign = jnp.where(jax.random.uniform(first, (SUPER, SUPER)) < 0.5, -1.0, 1.0)
    raw = sign * jax.random.uniform(second, (SUPER, SUPER), jnp.float32, inner * reach, reach)
    upper = index[:, None] < index[None, :]
    symmetric = jnp.where(upper, raw, raw.T)
    band = jnp.where((gap >= 1) & (gap <= 2), symmetric, 0.0)
    diagonal = jax.random.uniform(first, (SUPER,), jnp.float32, diag_lo, diag_hi)
    return band + jnp.diag(diagonal)


def coherent_band(key, diag_lo, diag_hi, lowest, reach):
    first, second, third = jax.random.split(key, 3)
    index = jnp.arange(SUPER)
    gap = jnp.abs(index[:, None] - index[None, :])
    gauge = jnp.where(jax.random.uniform(first, (SUPER,)) < 0.5, -1.0, 1.0)
    raw = jax.random.uniform(second, (SUPER, SUPER), jnp.float32, lowest, reach)
    upper = index[:, None] < index[None, :]
    magnitude = jnp.where(upper, raw, raw.T)
    band = jnp.where((gap >= 1) & (gap <= 2), -gauge[:, None] * gauge[None, :] * magnitude, 0.0)
    diagonal = jax.random.uniform(third, (SUPER,), jnp.float32, diag_lo, diag_hi)
    return band + jnp.diag(diagonal)


def draw_pivot_h(key, part):
    key = jax.random.fold_in(key, 11)
    matrix = coherent_band(key, 8.0, 8.5, 1.4, 1.65)
    return matrix.astype(jnp.bfloat16)


def draw_pivot_s(key, part):
    key = jax.random.fold_in(key, 12)
    matrix = banded_symmetric(key, 1.0, 1.5, 0.08, -1.0)
    return matrix.astype(jnp.bfloat16)


def draw_pole_shift(key, part):
    key = jax.random.fold_in(key, 13)
    first, second = jax.random.split(key)
    real = jax.random.uniform(first, (POLES,), jnp.float32, -0.5, 0.5)
    imag = jax.random.uniform(second, (POLES,), jnp.float32, 0.25, 1.5)
    return jnp.stack([real, imag], axis=1)


def plant(drawn, rng, low, largest):
    dims = drawn.shape
    spot = [jax.random.randint(jax.random.fold_in(rng, axis), (), 0, dims[axis]) for axis in range(len(dims))]
    drawn = drawn.at[tuple(spot)].set(low)
    longest = dims.index(max(dims))
    spot[longest] = (spot[longest] + 1) % dims[longest]
    return drawn.at[tuple(spot)].set(largest)


def levels(stream_key, dims, shards, smallest, top_value):
    factor_of, own = 1.0, jax.random.fold_in(stream_key, 6)
    for axis_at, blocks in shards:
        draws = jnp.exp(jax.random.uniform(jax.random.fold_in(own, axis_at), (blocks,), jnp.float32, smallest / len(shards), top_value / len(shards)))
        factor_of = factor_of * jnp.repeat(draws, dims[axis_at] // blocks).reshape([-1 if axis == axis_at else 1 for axis in range(len(dims))])
    return factor_of


def normal_values(own_key, dims, spread, most, shards=(), kind=jnp.bfloat16):
    gain = levels(own_key, dims, shards, -0.22, 0.18) if shards else 1.0
    array = jax.random.normal(own_key, dims, jnp.float32) * spread * gain
    return jnp.minimum(jnp.maximum(array, -most), most).astype(kind)


def setup_inputs(seed: int = 0) -> dict:
    streams_of = jax.random.split(jax.random.key(seed), 11)
    front_h = normal_values(streams_of[0], (ORDER, ORDER), 1.0, 6.0, ((0, 64),))
    front_s = normal_values(streams_of[1], (ORDER, ORDER), 0.5, 6.0, ((0, 64),))
    panel_h = normal_values(streams_of[2], (ORDER, SUPER), 1.0, 6.0, ((0, 16),))
    panel_s = normal_values(streams_of[3], (ORDER, SUPER), 0.3, 4.0, ((0, 16),))
    pivot_h = draw_pivot_h(jax.random.fold_in(streams_of[10], 71), 0)
    pivot_s = draw_pivot_s(jax.random.fold_in(streams_of[10], 71), 0)
    pole_shift = draw_pole_shift(jax.random.fold_in(streams_of[10], 71), 0)
    pole_weight = normal_values(streams_of[7], (POLES, 2), 2.0, 6.0, ((0, 8),), jnp.float32)
    pattern = plant((jax.random.randint(streams_of[8], (NB, NB), 0, 2) < 1).astype(jnp.int32), jax.random.fold_in(streams_of[8], 1), 0, 1)
    ancestor_inverse = normal_values(streams_of[9], (POLES, 2, N_ROW, N_COL, STRIP, ORDER), ORDER ** -0.5, 0.09375, ((0, 8), (3, 4), (5, 16)))
    return {"front_h": front_h, "front_s": front_s, "panel_h": panel_h, "panel_s": panel_s, "pivot_h": pivot_h, "pivot_s": pivot_s, "pole_shift": pole_shift, "pole_weight": pole_weight, "pattern": pattern, "ancestor_inverse": ancestor_inverse}


highest = lax.Precision.HIGHEST


def complex_matmul(left_real, left_imag, right_real, right_imag):
    real = jnp.dot(left_real, right_real, precision=highest, preferred_element_type=jnp.float32) - jnp.dot(left_imag, right_imag, precision=highest, preferred_element_type=jnp.float32)
    imag = jnp.dot(left_real, right_imag, precision=highest, preferred_element_type=jnp.float32) + jnp.dot(left_imag, right_real, precision=highest, preferred_element_type=jnp.float32)
    return real, imag


def complex_einsum(form, left_real, left_imag, right_real, right_imag):
    real = jnp.einsum(form, left_real, right_real, precision=highest) - jnp.einsum(form, left_imag, right_imag, precision=highest)
    imag = jnp.einsum(form, left_real, right_imag, precision=highest) + jnp.einsum(form, left_imag, right_real, precision=highest)
    return real, imag


def invert_pivot(pivot_h, pivot_s, shift_real, shift_imag, sweeps):
    matrix_real = pivot_h.astype(jnp.float32) - shift_real * pivot_s.astype(jnp.float32)
    matrix_imag = -shift_imag * pivot_s.astype(jnp.float32)
    diag_real = jnp.diagonal(matrix_real)
    diag_imag = jnp.diagonal(matrix_imag)
    denom = diag_real * diag_real + diag_imag * diag_imag
    identity = jnp.eye(matrix_real.shape[0], dtype=jnp.float32)

    def advance(index, state):
        approx_real, approx_imag = state
        prod_real, prod_imag = complex_matmul(matrix_real, matrix_imag, approx_real, approx_imag)
        return complex_matmul(approx_real, approx_imag, 2.0 * identity - prod_real, -prod_imag)

    start = (jnp.diag(diag_real / denom), jnp.diag(-diag_imag / denom))
    return lax.fori_loop(0, sweeps, advance, start)


def reference(front_h, front_s, panel_h, panel_s, pivot_h, pivot_s, pole_shift, pole_weight, pattern, ancestor_inverse):
    block_mask = jnp.repeat(jnp.repeat(pattern.astype(jnp.float32), SUPER, axis=0), SUPER, axis=1)
    hamil = front_h.astype(jnp.float32)
    margin = front_s.astype(jnp.float32)
    panel_hf = panel_h.astype(jnp.float32)
    panel_sf = panel_s.astype(jnp.float32)
    density_rows = jnp.zeros((ORDER, SUPER), jnp.float32)
    density_pivot = jnp.zeros((SUPER, SUPER), jnp.float32)
    schur_list = []
    for pole in range(POLES):
        shift_real = pole_shift[pole, 0]
        shift_imag = pole_shift[pole, 1]
        weight_real = pole_weight[pole, 0]
        weight_imag = pole_weight[pole, 1]
        inv_real, inv_imag = invert_pivot(pivot_h, pivot_s, shift_real, shift_imag, NEWTON)
        coupling_real = (panel_hf - shift_real * panel_sf).astype(jnp.bfloat16).astype(jnp.float32)
        coupling_imag = (-shift_imag * panel_sf).astype(jnp.bfloat16).astype(jnp.float32)
        solved_real, solved_imag = complex_matmul(coupling_real, coupling_imag, inv_real, inv_imag)
        solved_real = solved_real.astype(jnp.bfloat16).astype(jnp.float32)
        solved_imag = solved_imag.astype(jnp.bfloat16).astype(jnp.float32)
        front_real = block_mask * (hamil - shift_real * margin)
        front_imag = block_mask * (-shift_imag * margin)
        update_real, update_imag = complex_einsum("gk,ik->gi", solved_real, solved_imag, coupling_real, coupling_imag)
        schur = jnp.stack([front_real - update_real, front_imag - update_imag]).astype(jnp.bfloat16)
        schur_list.append(schur.reshape(2, N_ROW, N_COL, STRIP, ORDER))
        ancestor = ancestor_inverse[pole].astype(jnp.float32).reshape(2, ORDER, ORDER)
        part_real, part_imag = complex_einsum("gi,gk->ik", ancestor[0], ancestor[1], solved_real, solved_imag)
        column_real = -part_real
        column_imag = -part_imag
        corr_real, corr_imag = complex_einsum("sk,sl->kl", solved_real, solved_imag, column_real, column_imag)
        block_real = inv_real - corr_real
        block_imag = inv_imag - corr_imag
        density_rows = density_rows + (weight_real * column_imag + weight_imag * column_real)
        density_pivot = density_pivot + (weight_real * block_imag + weight_imag * block_real)
    return jnp.stack(schur_list), density_rows, density_pivot
```

```python
import jax
import jax.numpy as jnp
from jax import lax
from jax.sharding import PartitionSpec as P

bf16 = jnp.bfloat16
f32 = jnp.float32


def block(real, imag):
    return jnp.concatenate(
        [jnp.concatenate([real, imag], axis=1), jnp.concatenate([-imag, real], axis=1)], axis=0
    )


def halves(wide):
    size = wide.shape[1] // 2
    return wide[:, :size], wide[:, size:]


def product(left, right):
    return jnp.dot(left, right, precision=lax.Precision.HIGH, preferred_element_type=f32)


def invert_pivot(pivot_h, pivot_s, shift_real, shift_imag):
    size = pivot_h.shape[0]
    margin = pivot_s.astype(f32)
    real = pivot_h.astype(f32) - shift_real * margin
    imag = -shift_imag * margin
    on_diag = jnp.eye(size, dtype=bool)
    diag_real = jnp.sum(jnp.where(on_diag, real, 0.0), axis=0)
    diag_imag = jnp.sum(jnp.where(on_diag, imag, 0.0), axis=0)
    denom = diag_real * diag_real + diag_imag * diag_imag
    inv_real, inv_imag = diag_real / denom, -diag_imag / denom
    err_real = jnp.where(on_diag, 0.0, imag * inv_imag - real * inv_real)
    err_imag = jnp.where(on_diag, 0.0, -(real * inv_imag + imag * inv_real))
    one = jnp.concatenate([on_diag.astype(f32), jnp.zeros((size, size), f32)], axis=1)
    err = jnp.concatenate([err_real, err_imag], axis=1)
    err2 = product(err, block(err_real, err_imag))
    square = block(*halves(err2))
    err3 = product(err, square)
    err4 = product(err2, square)
    first = one + err + err2 + err3
    fourth = block(*halves(err4))
    second = first + product(first, fourth)
    err8 = product(err4, fourth)
    total = second + product(second, block(*halves(err8)))
    sum_real, sum_imag = halves(total)
    scale_real, scale_imag = inv_real[:, None], inv_imag[:, None]
    return (
        scale_real * sum_real - scale_imag * sum_imag,
        scale_real * sum_imag + scale_imag * sum_real,
    )


def couple(rows_h, rows_s, shift_real, shift_imag):
    margin = rows_s.astype(f32)
    real = (rows_h.astype(f32) - shift_real * margin).astype(bf16)
    imag = (-shift_imag * margin).astype(bf16)
    return real, imag


def dot(left, right):
    return jnp.dot(left, right, preferred_element_type=f32)


def contract(left, right):
    return lax.dot_general(left, right, (((0,), (0,)), ((), ())), preferred_element_type=f32)


def split(value):
    high = value.astype(bf16)
    return high, (value - high.astype(f32)).astype(bf16)


def pack(member, col_count, pole_count):
    size = member.shape[0]
    width, piece = size // col_count, size // pole_count
    fold = 128 // width
    member = member.reshape(pole_count, fold, piece // fold, col_count, width)
    return member.transpose(0, 3, 2, 1, 4).reshape(pole_count * col_count, piece // fold, 128)


def unpack(member, width, piece):
    fold = 128 // width
    member = member.reshape(-1, piece // fold, fold, width)
    return member.transpose(2, 1, 0, 3).reshape(piece, -1)


def shards(
    front_h,
    front_s,
    panel_h,
    panel_s,
    pivot_h,
    pivot_s,
    pole_shift,
    pole_weight,
    pattern,
    ancestor_inverse,
):
    row_count = lax.axis_size("row")
    col_count = lax.axis_size("col")
    pole_count = lax.axis_size("pole")
    row_index = lax.axis_index("row")
    col_index = lax.axis_index("col")
    shift_real = pole_shift[0, 0]
    shift_imag = pole_shift[0, 1]
    weight_real = pole_weight[0, 0]
    weight_imag = pole_weight[0, 1]
    size = pivot_h.shape[0]
    width = size // col_count
    piece = size // pole_count
    half = width // 2
    order = row_count * width
    core = row_index % 2

    strip = lax.dynamic_slice_in_dim(jnp.stack([panel_h, panel_s]), col_index * width, width, axis=1)
    strip = strip.reshape(2, 2, half, size).transpose(1, 0, 2, 3)
    sent = jnp.broadcast_to(strip[None], (row_count // 2, 2, 2, half, size))
    far = lax.all_to_all(
        sent.reshape(row_count, 2, half, size), "row", split_axis=0, concat_axis=0, tiled=True
    )

    fronts = jnp.stack([front_h, front_s]).reshape(2, width, row_count, size).transpose(2, 0, 1, 3)
    fronts, _ = lax.optimization_barrier((fronts, far))
    tiles = lax.all_to_all(fronts, "row", split_axis=0, concat_axis=0, tiled=True)

    inv_real, inv_imag = invert_pivot(pivot_h, pivot_s, shift_real, shift_imag)
    inv_high, inv_low = split(block(inv_real, inv_imag))

    def solve(real, imag):
        wide = jnp.concatenate([real, imag], axis=1)
        return (dot(wide, inv_high) + dot(wide, inv_low)).astype(bf16)

    coupling_real, coupling_imag = couple(panel_h, panel_s, shift_real, shift_imag)
    solved = solve(coupling_real, coupling_imag)

    far_half = solve(
        *couple(
            far[:, 0].reshape(row_count * half, size),
            far[:, 1].reshape(row_count * half, size),
            shift_real,
            shift_imag,
        )
    )
    other = lax.ppermute(far_half, "row", [(i, i ^ 1) for i in range(row_count)])
    mine = far_half.reshape(row_count, 1, half, 2 * size)
    other = other.reshape(row_count, 1, half, 2 * size)
    far_solved = jnp.where(
        core == 0,
        jnp.concatenate([mine, other], axis=1),
        jnp.concatenate([other, mine], axis=1),
    ).reshape(order, 2 * size)

    far_real, far_imag = halves(far_solved)
    ancestor = ancestor_inverse.reshape(2 * order, size)
    part = contract(
        jnp.concatenate([far_solved, jnp.concatenate([-far_imag, far_real], axis=1)], axis=0),
        ancestor,
    )
    part_real, part_imag = part[:size], part[size:]
    rows_part = -(weight_real * part_imag + weight_imag * part_real)
    twin_part = -(weight_real * part_real - weight_imag * part_imag)
    solved_real, solved_imag = halves(solved)
    right = jnp.concatenate([solved_real, solved_imag], axis=0)
    left_high, left_low = split(jnp.concatenate([rows_part, twin_part], axis=1))
    correction = dot(left_high, right) + dot(left_low, right)
    pivot_part = (
        jnp.where(
            (row_index == 0) & (col_index == 0),
            weight_real * inv_imag + weight_imag * inv_real,
            0.0,
        ).T
        - correction
    )

    both = jnp.stack(
        [pack(rows_part, col_count, pole_count), pack(pivot_part, col_count, pole_count)], axis=1
    )
    both = lax.all_to_all(both, ("pole", "col"), split_axis=0, concat_axis=0, tiled=True)
    both = jnp.sum(both, axis=0)
    rows_out = unpack(both[:1, :, :], width, piece).T

    spread = jnp.broadcast_to(both[1][None], (row_count * col_count,) + both.shape[1:])
    spread = lax.all_to_all(spread, ("row", "col"), split_axis=0, concat_axis=0, tiled=True)
    spread = jnp.sum(spread.reshape((row_count, col_count) + both.shape[1:]), axis=0)
    pivot_out = unpack(spread, width, piece).T

    update = dot(far_solved, block(coupling_real.T, coupling_imag.T))
    mask = lax.dynamic_slice_in_dim(pattern, row_index, 1, axis=1).astype(f32)[:, :, None]
    hamil = tiles[:, 0].astype(f32)
    margin = tiles[:, 1].astype(f32)
    front_real = (mask * (hamil - shift_real * margin)).reshape(order, size)
    front_imag = (mask * (-shift_imag * margin)).reshape(order, size)
    update_real, update_imag = halves(update)
    schur = jnp.stack([front_real - update_real, front_imag - update_imag]).astype(bf16)
    schur = schur.reshape(1, 2, row_count, 1, width, size)
    return (schur, rows_out, pivot_out)


def solution(mesh):
    in_specs = (
        P(("row", "col"), None),
        P(("row", "col"), None),
        P("row", None),
        P("row", None),
        P(),
        P(),
        P("pole", None),
        P("pole", None),
        P(),
        P("pole", None, None, "col", None, "row"),
    )
    out_specs = (
        P("pole", None, None, "col", None, "row"),
        P(("row", "col"), "pole"),
        P(None, "pole"),
    )
    return jax.shard_map(shards, mesh=mesh, in_specs=in_specs, out_specs=out_specs, check_vma=False)
```

```python
import jax
import jax.numpy as jnp
from jax import lax
from jax.sharding import PartitionSpec as P

bf16 = jnp.bfloat16
f32 = jnp.float32


def block(real, imag):
    return jnp.concatenate(
        [jnp.concatenate([real, imag], axis=1), jnp.concatenate([-imag, real], axis=1)], axis=0
    )


def halves(wide):
    size = wide.shape[1] // 2
    return wide[:, :size], wide[:, size:]


def product(left, right):
    return jnp.dot(left, right, precision=lax.Precision.HIGH, preferred_element_type=f32)


def invert_pivot(pivot_h, pivot_s, shift_real, shift_imag):
    size = pivot_h.shape[0]
    margin = pivot_s.astype(f32)
    real = pivot_h.astype(f32) - shift_real * margin
    imag = -shift_imag * margin
    on_diag = jnp.eye(size, dtype=bool)
    diag_real = jnp.sum(jnp.where(on_diag, real, 0.0), axis=0)
    diag_imag = jnp.sum(jnp.where(on_diag, imag, 0.0), axis=0)
    denom = diag_real * diag_real + diag_imag * diag_imag
    inv_real, inv_imag = diag_real / denom, -diag_imag / denom
    err_real = jnp.where(on_diag, 0.0, imag * inv_imag - real * inv_real)
    err_imag = jnp.where(on_diag, 0.0, -(real * inv_imag + imag * inv_real))
    one = jnp.concatenate([on_diag.astype(f32), jnp.zeros((size, size), f32)], axis=1)
    err = jnp.concatenate([err_real, err_imag], axis=1)
    err2 = product(err, block(err_real, err_imag))
    square = block(*halves(err2))
    err3 = product(err, square)
    err4 = product(err2, square)
    first = one + err + err2 + err3
    fourth = block(*halves(err4))
    second = first + product(first, fourth)
    err8 = product(err4, fourth)
    total = second + product(second, block(*halves(err8)))
    sum_real, sum_imag = halves(total)
    scale_real, scale_imag = inv_real[:, None], inv_imag[:, None]
    return (
        scale_real * sum_real - scale_imag * sum_imag,
        scale_real * sum_imag + scale_imag * sum_real,
    )


def couple(rows_h, rows_s, shift_real, shift_imag):
    margin = rows_s.astype(f32)
    real = (rows_h.astype(f32) - shift_real * margin).astype(bf16)
    imag = (-shift_imag * margin).astype(bf16)
    return real, imag


def dot(left, right):
    return jnp.dot(left, right, preferred_element_type=f32)


def contract(left, right):
    return lax.dot_general(left, right, (((0,), (0,)), ((), ())), preferred_element_type=f32)


def split(value):
    high = lax.reduce_precision(value, 8, 7)
    return high.astype(bf16), (value - high).astype(bf16)


def pack(member, col_count, pole_count):
    size = member.shape[0]
    width, piece = size // col_count, size // pole_count
    fold = 128 // width
    member = member.reshape(pole_count, fold, piece // fold, col_count, width)
    return member.transpose(0, 3, 2, 1, 4).reshape(pole_count * col_count, piece // fold, 128)


def unpack(member, width, piece):
    fold = 128 // width
    member = member.reshape(-1, piece // fold, fold, width)
    return member.transpose(2, 1, 0, 3).reshape(piece, -1)


def shards(
    front_h,
    front_s,
    panel_h,
    panel_s,
    pivot_h,
    pivot_s,
    pole_shift,
    pole_weight,
    pattern,
    ancestor_inverse,
):
    row_count = lax.axis_size("row")
    col_count = lax.axis_size("col")
    pole_count = lax.axis_size("pole")
    row_index = lax.axis_index("row")
    col_index = lax.axis_index("col")
    shift_real = pole_shift[0, 0]
    shift_imag = pole_shift[0, 1]
    weight_real = pole_weight[0, 0]
    weight_imag = pole_weight[0, 1]
    size = pivot_h.shape[0]
    width = size // col_count
    piece = size // pole_count
    half = width // 2
    order = row_count * width
    core = row_index % 2

    strip = lax.dynamic_slice_in_dim(jnp.stack([panel_h, panel_s]), col_index * width, width, axis=1)
    strip = strip.reshape(2, 2, half, size).transpose(1, 0, 2, 3)
    sent = jnp.broadcast_to(strip[None], (row_count // 2, 2, 2, half, size))
    sent = sent.reshape(row_count, 2 * half, size)
    share = width // pole_count
    fronts = lax.dynamic_slice_in_dim(
        jnp.stack([front_h, front_s]), lax.axis_index("pole") * share, share, axis=1
    )
    fronts = fronts.reshape(2, share, row_count, size).transpose(2, 0, 1, 3)
    sent = jnp.concatenate([sent, fronts.reshape(row_count, 2 * share, size)], axis=1)
    received = lax.all_to_all(sent, "row", split_axis=0, concat_axis=0, tiled=True)
    far = received[:, : 2 * half].reshape(row_count, 2, half, size)
    tiles = lax.all_gather(received[:, 2 * half :], "pole", axis=0, tiled=False)
    tiles = tiles.reshape(pole_count, row_count, 2, share, size).transpose(1, 2, 0, 3, 4)
    tiles = tiles.reshape(row_count, 2, width, size)

    inv_real, inv_imag = invert_pivot(pivot_h, pivot_s, shift_real, shift_imag)
    inv_high, inv_low = split(block(inv_real, inv_imag))

    def solve(real, imag):
        wide = jnp.concatenate([real, imag], axis=1)
        return (dot(wide, inv_high) + dot(wide, inv_low)).astype(bf16)

    coupling_real, coupling_imag = couple(panel_h, panel_s, shift_real, shift_imag)
    solved = solve(coupling_real, coupling_imag)

    far_half = solve(
        *couple(
            far[:, 0].reshape(row_count * half, size),
            far[:, 1].reshape(row_count * half, size),
            shift_real,
            shift_imag,
        )
    )
    other = lax.ppermute(far_half, "row", [(i, i ^ 1) for i in range(row_count)])
    mine = far_half.reshape(row_count, 1, half, 2 * size)
    other = other.reshape(row_count, 1, half, 2 * size)
    far_solved = jnp.where(
        core == 0,
        jnp.concatenate([mine, other], axis=1),
        jnp.concatenate([other, mine], axis=1),
    ).reshape(order, 2 * size)

    far_real, far_imag = halves(far_solved)
    ancestor = ancestor_inverse.reshape(2 * order, size)
    part = contract(
        jnp.concatenate([far_solved, jnp.concatenate([-far_imag, far_real], axis=1)], axis=0),
        ancestor,
    )
    part_real, part_imag = part[:size], part[size:]
    rows_part = -(weight_real * part_imag + weight_imag * part_real)
    twin_part = -(weight_real * part_real - weight_imag * part_imag)
    solved_real, solved_imag = halves(solved)
    right = jnp.concatenate([solved_real, solved_imag], axis=0)
    left_high, left_low = split(jnp.concatenate([rows_part, twin_part], axis=1))
    correction = dot(left_high, right) + dot(left_low, right)
    pivot_part = (
        jnp.where(
            (row_index == 0) & (col_index == 0),
            weight_real * inv_imag + weight_imag * inv_real,
            0.0,
        ).T
        - correction
    )

    both = jnp.stack(
        [pack(rows_part, col_count, pole_count), pack(pivot_part, col_count, pole_count)], axis=1
    )
    both = lax.all_to_all(both, ("pole", "col"), split_axis=0, concat_axis=0, tiled=True)
    both = jnp.sum(both, axis=0)
    rows_out = unpack(both[:1, :, :], width, piece).T

    spread = jnp.broadcast_to(both[1][None], (row_count * col_count,) + both.shape[1:])
    spread = lax.all_to_all(spread, ("row", "col"), split_axis=0, concat_axis=0, tiled=True)
    spread = jnp.sum(spread.reshape((row_count, col_count) + both.shape[1:]), axis=0)
    pivot_out = unpack(spread, width, piece).T

    update = dot(far_solved, block(coupling_real.T, coupling_imag.T))
    mask = lax.dynamic_slice_in_dim(pattern, row_index, 1, axis=1).astype(f32)[:, :, None]
    hamil = tiles[:, 0].astype(f32)
    margin = tiles[:, 1].astype(f32)
    front_real = (mask * (hamil - shift_real * margin)).reshape(order, size)
    front_imag = (mask * (-shift_imag * margin)).reshape(order, size)
    update_real, update_imag = halves(update)
    schur = jnp.stack([front_real - update_real, front_imag - update_imag]).astype(bf16)
    schur = schur.reshape(1, 2, row_count, 1, width, size)
    return (schur, rows_out, pivot_out)


def solution(mesh):
    in_specs = (
        P(("row", "col"), None),
        P(("row", "col"), None),
        P("row", None),
        P("row", None),
        P(),
        P(),
        P("pole", None),
        P("pole", None),
        P(),
        P("pole", None, None, "col", None, "row"),
    )
    out_specs = (
        P("pole", None, None, "col", None, "row"),
        P(("row", "col"), "pole"),
        P(None, "pole"),
    )
    return jax.shard_map(shards, mesh=mesh, in_specs=in_specs, out_specs=out_specs, check_vma=False)
```

```python
import functools

import jax
import jax.numpy as jnp
from jax import lax
from jax.experimental import pallas as pl
from jax.experimental.pallas import tpu as pltpu
from jax.sharding import PartitionSpec as P

bf16 = jnp.bfloat16
f32 = jnp.float32
VMEM = pl.BlockSpec(memory_space=pltpu.VMEM)
SMEM = pl.BlockSpec(memory_space=pltpu.SMEM)


def call(body, outs, ins, flops, name):
    moved = sum(x.size * x.dtype.itemsize for x in list(ins) + list(outs))
    return pl.pallas_call(
        body,
        out_shape=outs,
        in_specs=[SMEM if x.size <= 256 else VMEM for x in ins],
        out_specs=[VMEM] * len(outs),
        compiler_params=pltpu.CompilerParams(vmem_limit_bytes=40 * 2**20),
        cost_estimate=pl.CostEstimate(flops=flops, bytes_accessed=moved, transcendentals=0),
        name=name,
    )(*ins)


def shape(*dims, dtype=bf16):
    return jax.ShapeDtypeStruct(dims, dtype)


def dot(left, right):
    return jnp.dot(left, right, preferred_element_type=f32)


def contract(left, right, axis_left, axis_right):
    dims = (((axis_left,), (axis_right,)), ((), ()))
    return lax.dot_general(left, right, dims, preferred_element_type=f32)


def split(value):
    high = value.astype(bf16)
    return high, (value - high.astype(f32)).astype(bf16)


def product(left, right):
    return dot(left[0], right[0]) + (dot(left[0], right[1]) + dot(left[1], right[0]))


def block(wide):
    size = wide.shape[1] // 2
    real, imag = wide[:, :size], wide[:, size:]
    return jnp.concatenate([wide, jnp.concatenate([-imag, real], axis=1)], axis=0)


def both_of(pair, form):
    return form(pair[0]), form(pair[1])


def couple(rows_h, rows_s, shift_real, shift_imag):
    margin = rows_s.astype(f32)
    real = (rows_h.astype(f32) - shift_real * margin).astype(bf16)
    imag = (-shift_imag * margin).astype(bf16)
    return real, imag


def invert_body(
    shift, weight, pivot_h, pivot_s, panel_h, panel_s, inverse, right, wide, base
):
    size = pivot_h.shape[0]
    shift_real, shift_imag = shift[0, 0], shift[0, 1]
    margin = pivot_s[...].astype(f32)
    real = pivot_h[...].astype(f32) - shift_real * margin
    imag = -shift_imag * margin
    on_diag = lax.broadcasted_iota(jnp.int32, (size, size), 0) == lax.broadcasted_iota(
        jnp.int32, (size, size), 1
    )

    def scales(axis):
        diag_real = jnp.sum(jnp.where(on_diag, real, 0.0), axis=axis, keepdims=True)
        diag_imag = jnp.sum(jnp.where(on_diag, imag, 0.0), axis=axis, keepdims=True)
        denom = diag_real * diag_real + diag_imag * diag_imag
        return diag_real / denom, -diag_imag / denom

    col_real, col_imag = scales(0)
    err_real = jnp.where(on_diag, 0.0, imag * col_imag - real * col_real)
    err_imag = jnp.where(on_diag, 0.0, -(real * col_imag + imag * col_real))
    one = jnp.concatenate([jnp.where(on_diag, 1.0, 0.0), jnp.zeros((size, size), f32)], axis=1)
    err = jnp.concatenate([err_real, err_imag], axis=1)
    err_pair = split(err)
    err2 = product(err_pair, both_of(err_pair, block))
    err2_pair = split(err2)
    square = both_of(err2_pair, block)
    err3 = product(err_pair, square)
    err4_pair = split(product(err2_pair, square))
    first = one + err + err2 + err3
    fourth = both_of(err4_pair, block)
    second = first + product(split(first), fourth)
    err8_pair = split(product(err4_pair, fourth))
    total = second + product(split(second), both_of(err8_pair, block))
    sum_real, sum_imag = total[:, :size], total[:, size:]
    row_real, row_imag = scales(1)
    inv_real = row_real * sum_real - row_imag * sum_imag
    inv_imag = row_real * sum_imag + row_imag * sum_real
    inv_pair = both_of(split(jnp.concatenate([inv_real, inv_imag], axis=1)), block)
    inverse[0] = inv_pair[0]
    inverse[1] = inv_pair[1]
    first_device = (lax.axis_index("row") == 0) & (lax.axis_index("col") == 0)
    density = weight[0, 0] * inv_imag + weight[0, 1] * inv_real
    base[...] = jnp.where(first_device, density.T, 0.0)
    coupling_real, coupling_imag = couple(panel_h[...], panel_s[...], shift_real, shift_imag)
    coupling = jnp.concatenate([coupling_real, coupling_imag], axis=1)
    solved = (dot(coupling, inv_pair[0]) + dot(coupling, inv_pair[1])).astype(bf16)
    right[:size] = solved[:, :size]
    right[size:] = solved[:, size:]
    wide[:size] = jnp.concatenate([coupling_real, -coupling_imag], axis=1)
    wide[size:] = jnp.concatenate([coupling_imag, coupling_real], axis=1)


def solve_body(shift, received, inverse, solved):
    strips, twice, size = received.shape
    half = twice // 2
    rows_h = received[:, :half].reshape(strips * half, size)
    rows_s = received[:, half:].reshape(strips * half, size)
    coupling = jnp.concatenate(couple(rows_h, rows_s, shift[0, 0], shift[0, 1]), axis=1)
    solved[...] = (dot(coupling, inverse[0]) + dot(coupling, inverse[1])).astype(bf16)


def ordered(mine, other):
    low = lax.rem(lax.axis_index("row"), 2) == 0
    return jnp.where(low, mine, other), jnp.where(low, other, mine)


def fold(member, out, at):
    pieces = out.shape[0]
    half = out.shape[1] // 2
    cols = 2 * member.shape[1] // 128
    low_lane = lax.broadcasted_iota(jnp.int32, (half, 128), 1) < 64
    for pole in range(pieces // cols):
        for pair in range(cols // 2):
            rows = pole * 2 * half
            top = member[rows : rows + half, pair * 128 : pair * 128 + 128]
            bottom = member[rows + half : rows + 2 * half, pair * 128 : pair * 128 + 128]
            even = jnp.where(low_lane, top, pltpu.roll(bottom, 64, 1))
            odd = jnp.where(low_lane, pltpu.roll(top, 64, 1), bottom)
            out[pole * cols + 2 * pair, at : at + half] = even
            out[pole * cols + 2 * pair + 1, at : at + half] = odd


def column_body(weight, mine, other, ancestor, right, base, out, far):
    strips, half = ancestor.shape[1], ancestor.shape[2] // 2
    size = ancestor.shape[3]
    wide = mine.shape[1]
    top, bottom = ordered(mine[...], other[...])
    far[:, :half] = top.reshape(strips, half, wide)
    far[:, half:] = bottom.reshape(strips, half, wide)
    rows = far[...].reshape(strips * 2 * half, wide)
    by_real = contract(rows, ancestor[0].reshape(strips * 2 * half, size), 0, 0)
    by_imag = contract(rows, ancestor[1].reshape(strips * 2 * half, size), 0, 0)
    part_real = by_real[:size] - by_imag[size:]
    part_imag = by_real[size:] + by_imag[:size]
    weight_real, weight_imag = weight[0, 0], weight[0, 1]
    density = -(weight_real * part_imag + weight_imag * part_real)
    twin = -(weight_real * part_real - weight_imag * part_imag)
    high, low = split(jnp.concatenate([density, twin], axis=1))
    pivot = base[...] - (dot(high, right[...]) + dot(low, right[...]))
    fold(density, out, 0)
    fold(pivot, out, out.shape[1] // 2)


def strips_body(front_h, front_s, kept, given):
    size = kept.shape[3]
    core = lax.rem(lax.axis_index("row"), 2)
    for chip in range(kept.shape[0]):
        own = pl.ds(pl.multiple_of((2 * chip + core) * size, size), size)
        far = pl.ds(pl.multiple_of((2 * chip + 1 - core) * size, size), size)
        kept[chip, 0] = front_h[:, own]
        kept[chip, 1] = front_s[:, own]
        given[chip, 0] = front_h[:, far]
        given[chip, 1] = front_s[:, far]


def blocks_body(kept, swapped, *outs):
    chips = kept.shape[0]
    chip = lax.rem(lax.axis_index("row"), 2 * chips) // 2
    for step, out in enumerate(outs):
        to = lax.rem(chip + step, chips)
        low, high = ordered(kept[to], swapped[to])
        out[0] = low
        out[1] = high


def schur_body(shift, pattern, mine, other, wide, *refs):
    blocks, out = refs[:-1], refs[-1]
    chips = len(blocks)
    half = blocks[0].shape[2] // 2
    size = blocks[0].shape[3]
    shift_real, shift_imag = shift[0, 0], shift[0, 1]
    row = lax.axis_index("row")
    for step, tiles in enumerate(blocks):
        chip = lax.rem(row // 2 + chips - step, chips)
        at = pl.ds(pl.multiple_of(chip * 2 * half, 2 * half), 2 * half)
        low, high = ordered(mine[at, :], other[at, :])
        solved = jnp.concatenate([low[:half], high[:half], low[half:], high[half:]], axis=0)
        update = contract(solved, wide[...], 1, 1)
        for core in range(2):
            strip = 2 * chip + core
            mask = pattern[strip, row].astype(f32)
            rows = slice(core * 2 * half, (core + 1) * 2 * half)
            margin = mask * tiles[core, 1].astype(f32)
            real = mask * tiles[core, 0].astype(f32) - shift_real * margin
            out[0, strip] = (real - update[rows, :size]).astype(bf16)
            out[1, strip] = (-shift_imag * margin - update[rows, size:]).astype(bf16)


def unfold(member, width, piece):
    times = 128 // width
    member = member.reshape(-1, piece // times, times, width)
    return member.transpose(2, 1, 0, 3).reshape(piece, -1)


def shards(
    front_h,
    front_s,
    panel_h,
    panel_s,
    pivot_h,
    pivot_s,
    pole_shift,
    pole_weight,
    pattern,
    ancestor_inverse,
):
    row_count = lax.axis_size("row")
    col_count = lax.axis_size("col")
    pole_count = lax.axis_size("pole")
    col_index = lax.axis_index("col")
    size = pivot_h.shape[0]
    width = size // col_count
    piece = size // pole_count
    half = width // 2
    chips = row_count // 2
    neighbour = [(i, i ^ 1) for i in range(row_count)]

    strip = lax.dynamic_slice_in_dim(jnp.stack([panel_h, panel_s]), col_index * width, width, axis=1)
    strip = strip.reshape(2, 2, half, size).transpose(1, 0, 2, 3)
    sent = jnp.broadcast_to(strip[None], (chips, 2, 2, half, size))
    sent = sent.reshape(row_count, 2 * half, size)
    received = lax.all_to_all(sent, "row", split_axis=0, concat_axis=0, tiled=True)

    kept, given = call(
        strips_body,
        [shape(chips, 2, width, size)] * 2,
        [front_h, front_s],
        0,
        "front_strips",
    )
    swapped = lax.ppermute(given, "row", neighbour)

    inverse, right, wide, base = call(
        invert_body,
        [
            shape(2, 2 * size, 2 * size),
            shape(2 * size, size),
            shape(2 * size, 2 * size),
            shape(size, size, dtype=f32),
        ],
        [pole_shift, pole_weight, pivot_h, pivot_s, panel_h, panel_s],
        6 * 4 * 3 * 2 * size**3,
        "pivot_inverse",
    )
    (mine,) = call(
        solve_body,
        [shape(row_count * half, 2 * size)],
        [pole_shift, received, inverse],
        2 * 8 * row_count * half * size * size,
        "solved_rows",
    )
    other = lax.ppermute(mine, "row", neighbour)

    ancestor = ancestor_inverse.reshape(2, row_count, width, size)
    (both,) = pl.pallas_call(
        column_body,
        out_shape=[shape(pole_count * col_count, piece, 128, dtype=f32)],
        in_specs=[SMEM] + [VMEM] * 5,
        out_specs=[VMEM],
        scratch_shapes=[pltpu.VMEM((row_count, width, 2 * size), bf16)],
        compiler_params=pltpu.CompilerParams(vmem_limit_bytes=40 * 2**20),
        cost_estimate=pl.CostEstimate(
            flops=8 * row_count * width * size * size, bytes_accessed=4 * 2**20, transcendentals=0
        ),
        name="column",
    )(pole_weight, mine, other, ancestor, right, base)

    kept, swapped, both = lax.optimization_barrier((kept, swapped, both))
    blocks = call(
        blocks_body,
        [shape(2, 2, width, size)] * chips,
        [kept, swapped],
        0,
        "front_blocks",
    )
    arrived = list(blocks[:1]) + [
        lax.ppermute(
            blocks[step], "row", [(i, (i + 2 * step) % row_count) for i in range(row_count)]
        )
        for step in range(1, chips)
    ]

    both = lax.all_to_all(both, ("pole", "col"), split_axis=0, concat_axis=0, tiled=True)
    both = jnp.sum(both, axis=0).reshape(2, piece // 2, 128)
    rows_out = unfold(both[:1], width, piece).T

    spread = jnp.broadcast_to(both[1][None], (row_count * col_count,) + both.shape[1:])
    spread = lax.all_to_all(spread, ("row", "col"), split_axis=0, concat_axis=0, tiled=True)
    spread = jnp.sum(spread.reshape((row_count, col_count) + both.shape[1:]), axis=0)
    pivot_out = unfold(spread, width, piece).T

    (schur,) = call(
        schur_body,
        [shape(2, row_count, width, size)],
        [pole_shift, pattern, mine, other, wide, *arrived],
        8 * row_count * width * size * size,
        "schur",
    )
    return (schur.reshape(1, 2, row_count, 1, width, size), rows_out, pivot_out)


def solution(mesh):
    in_specs = (
        P(("row", "col"), None),
        P(("row", "col"), None),
        P("row", None),
        P("row", None),
        P(),
        P(),
        P("pole", None),
        P("pole", None),
        P(),
        P("pole", None, None, "col", None, "row"),
    )
    out_specs = (
        P("pole", None, None, "col", None, "row"),
        P(("row", "col"), "pole"),
        P(None, "pole"),
    )
    return jax.shard_map(shards, mesh=mesh, in_specs=in_specs, out_specs=out_specs, check_vma=False)
```

```python
import functools

import jax
import jax.numpy as jnp
from jax import lax
from jax.experimental import pallas as pl
from jax.experimental.pallas import tpu as pltpu
from jax.sharding import PartitionSpec as P

bf16 = jnp.bfloat16
f32 = jnp.float32
VMEM = pl.BlockSpec(memory_space=pltpu.VMEM)
SMEM = pl.BlockSpec(memory_space=pltpu.SMEM)


def call(body, outs, ins, flops, name):
    moved = sum(x.size * x.dtype.itemsize for x in list(ins) + list(outs))
    return pl.pallas_call(
        body,
        out_shape=outs,
        in_specs=[SMEM if x.size <= 256 else VMEM for x in ins],
        out_specs=[VMEM] * len(outs),
        compiler_params=pltpu.CompilerParams(vmem_limit_bytes=40 * 2**20),
        cost_estimate=pl.CostEstimate(flops=flops, bytes_accessed=moved, transcendentals=0),
        name=name,
    )(*ins)


def shape(*dims, dtype=bf16):
    return jax.ShapeDtypeStruct(dims, dtype)


def dot(left, right):
    return jnp.dot(left, right, preferred_element_type=f32)


def contract(left, right, axis_left, axis_right):
    dims = (((axis_left,), (axis_right,)), ((), ()))
    return lax.dot_general(left, right, dims, preferred_element_type=f32)


def split(value):
    high = value.astype(bf16)
    return high, (value - high.astype(f32)).astype(bf16)


def product(left, right):
    return dot(left[0], right[0]) + (dot(left[0], right[1]) + dot(left[1], right[0]))


def block(wide):
    size = wide.shape[1] // 2
    real, imag = wide[:, :size], wide[:, size:]
    return jnp.concatenate([wide, jnp.concatenate([-imag, real], axis=1)], axis=0)


def both_of(pair, form):
    return form(pair[0]), form(pair[1])


def couple(rows_h, rows_s, shift_real, shift_imag):
    margin = rows_s.astype(f32)
    real = (rows_h.astype(f32) - shift_real * margin).astype(bf16)
    imag = (-shift_imag * margin).astype(bf16)
    return real, imag


def invert_body(
    shift, weight, pivot_h, pivot_s, panel_h, panel_s, inverse, right, wide, base
):
    size = pivot_h.shape[0]
    shift_real, shift_imag = shift[0, 0], shift[0, 1]
    margin = pivot_s[...].astype(f32)
    real = pivot_h[...].astype(f32) - shift_real * margin
    imag = -shift_imag * margin
    on_diag = lax.broadcasted_iota(jnp.int32, (size, size), 0) == lax.broadcasted_iota(
        jnp.int32, (size, size), 1
    )

    def scales(axis):
        diag_real = jnp.sum(jnp.where(on_diag, real, 0.0), axis=axis, keepdims=True)
        diag_imag = jnp.sum(jnp.where(on_diag, imag, 0.0), axis=axis, keepdims=True)
        denom = diag_real * diag_real + diag_imag * diag_imag
        return diag_real / denom, -diag_imag / denom

    col_real, col_imag = scales(0)
    err_real = jnp.where(on_diag, 0.0, imag * col_imag - real * col_real)
    err_imag = jnp.where(on_diag, 0.0, -(real * col_imag + imag * col_real))
    one = jnp.concatenate([jnp.where(on_diag, 1.0, 0.0), jnp.zeros((size, size), f32)], axis=1)
    err = jnp.concatenate([err_real, err_imag], axis=1)
    err_pair = split(err)
    err2 = product(err_pair, both_of(err_pair, block))
    err2_pair = split(err2)
    square = both_of(err2_pair, block)
    err3 = product(err_pair, square)
    err4_pair = split(product(err2_pair, square))
    first = one + err + err2 + err3
    fourth = both_of(err4_pair, block)
    second = first + product(split(first), fourth)
    err8_pair = split(product(err4_pair, fourth))
    total = second + product(split(second), both_of(err8_pair, block))
    sum_real, sum_imag = total[:, :size], total[:, size:]
    row_real, row_imag = scales(1)
    inv_real = row_real * sum_real - row_imag * sum_imag
    inv_imag = row_real * sum_imag + row_imag * sum_real
    inv_pair = both_of(split(jnp.concatenate([inv_real, inv_imag], axis=1)), block)
    inverse[0] = inv_pair[0]
    inverse[1] = inv_pair[1]
    first_device = (lax.axis_index("row") == 0) & (lax.axis_index("col") == 0)
    density = weight[0, 0] * inv_imag + weight[0, 1] * inv_real
    base[...] = jnp.where(first_device, density.T, 0.0)
    coupling_real, coupling_imag = couple(panel_h[...], panel_s[...], shift_real, shift_imag)
    coupling = jnp.concatenate([coupling_real, coupling_imag], axis=1)
    solved = (dot(coupling, inv_pair[0]) + dot(coupling, inv_pair[1])).astype(bf16)
    right[:size] = solved[:, :size]
    right[size:] = solved[:, size:]
    wide[:size] = jnp.concatenate([coupling_real, -coupling_imag], axis=1)
    wide[size:] = jnp.concatenate([coupling_imag, coupling_real], axis=1)


def pack_body(panel_h, panel_s, front_h, front_s, out, panels, fronts, sems):
    half = panels.shape[1] // 2
    share, size = fronts.shape[0], out.shape[2]
    pole = lax.axis_index("pole")
    shares = panels.shape[1] // share
    at = pl.ds(pl.multiple_of(lax.axis_index("col") * 2 * half, 2 * half), 2 * half)
    of = pl.ds(pl.multiple_of(lax.rem(pole, shares) * share, share), share)
    copy_h = pltpu.make_async_copy(panel_h.at[at], panels.at[0], sems.at[0])
    copy_s = pltpu.make_async_copy(panel_s.at[at], panels.at[1], sems.at[1])
    share_h = pltpu.make_async_copy(front_h.at[of], fronts, sems.at[2])
    share_s = pltpu.make_async_copy(front_s.at[of], fronts, sems.at[2])
    copy_h.start()
    copy_s.start()
    pl.when(pole < shares)(share_h.start)
    pl.when(pole >= shares)(share_s.start)
    copy_h.wait()
    copy_s.wait()
    share_h.wait()
    for row in range(out.shape[0]):
        core = row % 2
        out[row, :half] = panels[0, core * half : (core + 1) * half]
        out[row, half : 2 * half] = panels[1, core * half : (core + 1) * half]
        out[row, 2 * half :] = fronts[:, row * size : (row + 1) * size]


def solve_body(shift, received, inverse, solved, share):
    strips, rows, size = received.shape
    half = solved.shape[0] // strips
    rows_h = received[:, :half].reshape(strips * half, size)
    rows_s = received[:, half : 2 * half].reshape(strips * half, size)
    coupling = jnp.concatenate(couple(rows_h, rows_s, shift[0, 0], shift[0, 1]), axis=1)
    solved[...] = (dot(coupling, inverse[0]) + dot(coupling, inverse[1])).astype(bf16)
    share[...] = received[:, 2 * half :]


def ordered(mine, other):
    low = lax.rem(lax.axis_index("row"), 2) == 0
    return jnp.where(low, mine, other), jnp.where(low, other, mine)


def fold(member, out, at):
    pieces = out.shape[0]
    half = out.shape[1] // 2
    cols = 2 * member.shape[1] // 128
    low_lane = lax.broadcasted_iota(jnp.int32, (half, 128), 1) < 64
    for pole in range(pieces // cols):
        for pair in range(cols // 2):
            rows = pole * 2 * half
            top = member[rows : rows + half, pair * 128 : pair * 128 + 128]
            bottom = member[rows + half : rows + 2 * half, pair * 128 : pair * 128 + 128]
            even = jnp.where(low_lane, top, pltpu.roll(bottom, 64, 1))
            odd = jnp.where(low_lane, pltpu.roll(top, 64, 1), bottom)
            out[pole * cols + 2 * pair, at : at + half] = even
            out[pole * cols + 2 * pair + 1, at : at + half] = odd


def column_body(weight, mine, other, ancestor, right, base, out, far):
    strips, half = ancestor.shape[1], ancestor.shape[2] // 2
    size = ancestor.shape[3]
    wide = mine.shape[1]
    top, bottom = ordered(mine[...], other[...])
    far[:, :half] = top.reshape(strips, half, wide)
    far[:, half:] = bottom.reshape(strips, half, wide)
    rows = far[...].reshape(strips * 2 * half, wide)
    by_real = contract(rows, ancestor[0].reshape(strips * 2 * half, size), 0, 0)
    by_imag = contract(rows, ancestor[1].reshape(strips * 2 * half, size), 0, 0)
    part_real = by_real[:size] - by_imag[size:]
    part_imag = by_real[size:] + by_imag[:size]
    weight_real, weight_imag = weight[0, 0], weight[0, 1]
    density = -(weight_real * part_imag + weight_imag * part_real)
    twin = -(weight_real * part_real - weight_imag * part_imag)
    high, low = split(jnp.concatenate([density, twin], axis=1))
    pivot = base[...] - (dot(high, right[...]) + dot(low, right[...]))
    fold(density, out, 0)
    fold(pivot, out, out.shape[1] // 2)


def sums_body(parts, spread, rows):
    half, width = parts.shape[1] // 2, rows.shape[1]
    total = jnp.sum(parts[...], axis=0)
    rows[:half] = total[:half, :width]
    rows[half:] = total[:half, width:]
    spread[...] = jnp.broadcast_to(total[None, half:], spread.shape)


def pivot_body(parts, out):
    half = parts.shape[1]
    width = 64
    cols = out.shape[1] // width
    total = jnp.sum(parts[...].reshape(-1, cols, half, 128), axis=0)
    for index in range(128 // width):
        lanes = slice(index * width, (index + 1) * width)
        strips = [total[col][:, lanes] for col in range(cols)]
        out[index * half : (index + 1) * half] = jnp.concatenate(strips, axis=1)


def schur_body(shift, pattern, mine, other, wide, *refs):
    shares, out, front = refs[:-2], refs[-2], refs[-1]
    poles, strips, share, size = front.shape
    pole = lax.axis_index("pole")
    row = lax.axis_index("row")
    for step, member in enumerate(shares):
        front[lax.rem(pole + poles - step, poles)] = member[...]
    shift_real, shift_imag = shift[0, 0], shift[0, 1]
    half = mine.shape[0] // strips
    top, bottom = ordered(mine[...], other[...])
    for strip in range(strips):
        rows = slice(strip * half, (strip + 1) * half)
        solved = jnp.concatenate([top[rows], bottom[rows]], axis=0)
        update = contract(solved, wide[...], 1, 1)
        mask = pattern[strip, row].astype(f32)
        for part in range(poles // 2):
            at = slice(part * share, (part + 1) * share)
            margin = mask * front[poles // 2 + part, strip].astype(f32)
            real = mask * front[part, strip].astype(f32) - shift_real * margin
            out[0, strip, at] = (real - update[at, :size]).astype(bf16)
            out[1, strip, at] = (-shift_imag * margin - update[at, size:]).astype(bf16)


def shards(
    front_h,
    front_s,
    panel_h,
    panel_s,
    pivot_h,
    pivot_s,
    pole_shift,
    pole_weight,
    pattern,
    ancestor_inverse,
):
    row_count = lax.axis_size("row")
    col_count = lax.axis_size("col")
    pole_count = lax.axis_size("pole")
    col_index = lax.axis_index("col")
    size = pivot_h.shape[0]
    width = size // col_count
    piece = size // pole_count
    half = width // 2
    neighbour = [(i, i ^ 1) for i in range(row_count)]

    share = 2 * width // pole_count
    params = pltpu.CompilerParams(vmem_limit_bytes=40 * 2**20)

    (sent,) = pl.pallas_call(
        pack_body,
        out_shape=[shape(row_count, width + share, size)],
        in_specs=[pl.BlockSpec(memory_space=pl.ANY)] * 4,
        out_specs=[VMEM],
        scratch_shapes=[
            pltpu.VMEM((2, width, size), bf16),
            pltpu.VMEM((share, row_count * size), bf16),
            pltpu.SemaphoreType.DMA((3,)),
        ],
        compiler_params=params,
        cost_estimate=pl.CostEstimate(flops=0, bytes_accessed=2**20, transcendentals=0),
        name="pack",
    )(panel_h, panel_s, front_h, front_s)
    received = lax.all_to_all(sent, "row", split_axis=0, concat_axis=0, tiled=True)

    inverse, right, wide, base = call(
        invert_body,
        [
            shape(2, 2 * size, 2 * size),
            shape(2 * size, size),
            shape(2 * size, 2 * size),
            shape(size, size, dtype=f32),
        ],
        [pole_shift, pole_weight, pivot_h, pivot_s, panel_h, panel_s],
        6 * 4 * 3 * 2 * size**3,
        "pivot_inverse",
    )
    mine, shared = call(
        solve_body,
        [shape(row_count * half, 2 * size), shape(row_count, share, size)],
        [pole_shift, received, inverse],
        2 * 8 * row_count * half * size * size,
        "solved_rows",
    )
    other = lax.ppermute(mine, "row", neighbour)

    ancestor = ancestor_inverse.reshape(2, row_count, width, size)
    (both,) = pl.pallas_call(
        column_body,
        out_shape=[shape(pole_count * col_count, piece, 128, dtype=f32)],
        in_specs=[SMEM] + [VMEM] * 5,
        out_specs=[VMEM],
        scratch_shapes=[pltpu.VMEM((row_count, width, 2 * size), bf16)],
        compiler_params=pltpu.CompilerParams(vmem_limit_bytes=40 * 2**20),
        cost_estimate=pl.CostEstimate(
            flops=8 * row_count * width * size * size, bytes_accessed=4 * 2**20, transcendentals=0
        ),
        name="column",
    )(pole_weight, mine, other, ancestor, right, base)

    shared, both = lax.optimization_barrier((shared, both))
    onward = [(i, (i + 1) % pole_count) for i in range(pole_count)]
    back = [(i, (i - 1) % pole_count) for i in range(pole_count)]
    shares = {0: shared}

    def go_round(steps):
        for step in steps:
            shares[step + 1] = lax.ppermute(shares[step], "pole", onward)
            if step + 1 < pole_count // 2:
                before = shares[(pole_count - step) % pole_count]
                shares[pole_count - step - 1] = lax.ppermute(before, "pole", back)

    go_round(range(2))
    both = lax.all_to_all(both, ("pole", "col"), split_axis=0, concat_axis=0, tiled=True)
    spread, rows_out = call(
        sums_body,
        [
            shape(row_count * col_count, piece // 2, 128, dtype=f32),
            shape(piece, width, dtype=f32),
        ],
        [both],
        0,
        "sums",
    )
    spread, shares[2], shares[pole_count - 2] = lax.optimization_barrier(
        (spread, shares[2], shares[pole_count - 2])
    )
    go_round(range(2, pole_count // 2))
    spread = lax.all_to_all(spread, ("row", "col"), split_axis=0, concat_axis=0, tiled=True)
    (pivot_out,) = call(pivot_body, [shape(piece, size, dtype=f32)], [spread], 0, "pivot")

    (schur,) = pl.pallas_call(
        schur_body,
        out_shape=[shape(2, row_count, width, size)],
        in_specs=[SMEM] * 2 + [VMEM] * (3 + pole_count),
        out_specs=[VMEM],
        scratch_shapes=[pltpu.VMEM((pole_count, row_count, share, size), bf16)],
        compiler_params=params,
        cost_estimate=pl.CostEstimate(
            flops=8 * row_count * width * size * size, bytes_accessed=4 * 2**20, transcendentals=0
        ),
        name="schur",
    )(pole_shift, pattern, mine, other, wide, *[shares[step] for step in range(pole_count)])
    return (schur.reshape(1, 2, row_count, 1, width, size), rows_out.T, pivot_out.T)


def solution(mesh):
    in_specs = (
        P(("row", "col"), None),
        P(("row", "col"), None),
        P("row", None),
        P("row", None),
        P(),
        P(),
        P("pole", None),
        P("pole", None),
        P(),
        P("pole", None, None, "col", None, "row"),
    )
    out_specs = (
        P("pole", None, None, "col", None, "row"),
        P(("row", "col"), "pole"),
        P(None, "pole"),
    )
    return jax.shard_map(shards, mesh=mesh, in_specs=in_specs, out_specs=out_specs, check_vma=False)
```

```python
import functools

import jax
import jax.numpy as jnp
from jax import lax
from jax.experimental import pallas as pl
from jax.experimental.pallas import tpu as pltpu
from jax.sharding import PartitionSpec as P

bf16 = jnp.bfloat16
f32 = jnp.float32
VMEM = pl.BlockSpec(memory_space=pltpu.VMEM)
SMEM = pl.BlockSpec(memory_space=pltpu.SMEM)


def call(body, outs, ins, flops, name, grant=16):
    moved = sum(x.size * x.dtype.itemsize for x in list(ins) + list(outs))
    return pl.pallas_call(
        body,
        out_shape=outs,
        in_specs=[SMEM if x.size <= 256 else VMEM for x in ins],
        out_specs=[VMEM] * len(outs),
        compiler_params=pltpu.CompilerParams(vmem_limit_bytes=grant * 2**20),
        cost_estimate=pl.CostEstimate(flops=flops, bytes_accessed=moved, transcendentals=0),
        name=name,
    )(*ins)


def shape(*dims, dtype=bf16):
    return jax.ShapeDtypeStruct(dims, dtype)


def dot(left, right):
    return jnp.dot(left, right, preferred_element_type=f32)


def contract(left, right, axis_left, axis_right):
    dims = (((axis_left,), (axis_right,)), ((), ()))
    return lax.dot_general(left, right, dims, preferred_element_type=f32)


def split(value):
    high = value.astype(bf16)
    return high, (value - high.astype(f32)).astype(bf16)


def product(left, right):
    return dot(left[0], right[0]) + (dot(left[0], right[1]) + dot(left[1], right[0]))


def block(wide):
    size = wide.shape[1] // 2
    real, imag = wide[:, :size], wide[:, size:]
    return jnp.concatenate([wide, jnp.concatenate([-imag, real], axis=1)], axis=0)


def both_of(pair, form):
    return form(pair[0]), form(pair[1])


def couple(rows_h, rows_s, shift_real, shift_imag):
    margin = rows_s.astype(f32)
    real = (rows_h.astype(f32) - shift_real * margin).astype(bf16)
    imag = (-shift_imag * margin).astype(bf16)
    return real, imag


def invert_body(shift, pivot_h, pivot_s, inverse):
    size = pivot_h.shape[0]
    shift_real, shift_imag = shift[0, 0], shift[0, 1]
    margin = pivot_s[...].astype(f32)
    real = pivot_h[...].astype(f32) - shift_real * margin
    imag = -shift_imag * margin
    on_diag = lax.broadcasted_iota(jnp.int32, (size, size), 0) == lax.broadcasted_iota(
        jnp.int32, (size, size), 1
    )

    def scales(axis):
        diag_real = jnp.sum(jnp.where(on_diag, real, 0.0), axis=axis, keepdims=True)
        diag_imag = jnp.sum(jnp.where(on_diag, imag, 0.0), axis=axis, keepdims=True)
        denom = diag_real * diag_real + diag_imag * diag_imag
        return diag_real / denom, -diag_imag / denom

    col_real, col_imag = scales(0)
    err_real = jnp.where(on_diag, 0.0, imag * col_imag - real * col_real)
    err_imag = jnp.where(on_diag, 0.0, -(real * col_imag + imag * col_real))
    one = jnp.concatenate([jnp.where(on_diag, 1.0, 0.0), jnp.zeros((size, size), f32)], axis=1)
    err = jnp.concatenate([err_real, err_imag], axis=1)
    err_pair = split(err)
    err2 = product(err_pair, both_of(err_pair, block))
    err2_pair = split(err2)
    square = both_of(err2_pair, block)
    err3 = product(err_pair, square)
    err4_pair = split(product(err2_pair, square))
    first = one + err + err2 + err3
    fourth = both_of(err4_pair, block)
    second = first + product(split(first), fourth)
    err8_pair = split(product(err4_pair, fourth))
    total = second + product(split(second), both_of(err8_pair, block))
    sum_real, sum_imag = total[:, :size], total[:, size:]
    row_real, row_imag = scales(1)
    inv_real = row_real * sum_real - row_imag * sum_imag
    inv_imag = row_real * sum_imag + row_imag * sum_real
    inverse[0], inverse[1] = split(jnp.concatenate([inv_real, inv_imag], axis=1))


def solve(rows_h, rows_s, shift, inverse):
    coupling = jnp.concatenate(couple(rows_h, rows_s, shift[0, 0], shift[0, 1]), axis=1)
    return (dot(coupling, block(inverse[0])) + dot(coupling, block(inverse[1]))).astype(bf16)


def local_body(shift, weight, panel_h, panel_s, inverse, right, base):
    size = panel_h.shape[1]
    solved = solve(panel_h[...], panel_s[...], shift, inverse)
    right[:size] = solved[:, :size]
    right[size:] = solved[:, size:]
    whole = inverse[0].astype(f32) + inverse[1].astype(f32)
    density = weight[0, 0] * whole[:, size:] + weight[0, 1] * whole[:, :size]
    first_device = (lax.axis_index("row") == 0) & (lax.axis_index("col") == 0)
    base[...] = jnp.where(first_device, density.T, 0.0)


def pack_body(panel_h, panel_s, front_h, front_s, out, panels, fronts, sems):
    half = panels.shape[1] // 2
    share, size = fronts.shape[1], out.shape[2]
    shares = panels.shape[1] // share
    at = pl.ds(pl.multiple_of(lax.axis_index("col") * 2 * half, 2 * half), 2 * half)
    of = pl.ds(pl.multiple_of(lax.rem(lax.axis_index("pole"), shares) * share, share), share)
    copies = [
        pltpu.make_async_copy(panel_h.at[at], panels.at[0], sems.at[0]),
        pltpu.make_async_copy(panel_s.at[at], panels.at[1], sems.at[1]),
        pltpu.make_async_copy(front_h.at[of], fronts.at[0], sems.at[2]),
        pltpu.make_async_copy(front_s.at[of], fronts.at[1], sems.at[3]),
    ]
    for copy in copies:
        copy.start()
    for copy in copies:
        copy.wait()
    for row in range(out.shape[0]):
        core = row % 2
        for part in range(2):
            low = part * half
            out[row, low : low + half] = panels[part, core * half : (core + 1) * half]
            low = 2 * half + part * share
            out[row, low : low + share] = fronts[part, :, row * size : (row + 1) * size]


def solve_body(shift, received, inverse, solved, share):
    strips, rows, size = received.shape
    half = solved.shape[0] // strips
    rows_h = received[:, :half].reshape(strips * half, size)
    rows_s = received[:, half : 2 * half].reshape(strips * half, size)
    solved[...] = solve(rows_h, rows_s, shift, inverse)
    share[...] = received[:, 2 * half :]


def ordered(mine, other):
    low = lax.rem(lax.axis_index("row"), 2) == 0
    return jnp.where(low, mine, other), jnp.where(low, other, mine)


def fold(member, out, at):
    pieces = out.shape[0]
    half = out.shape[1] // 2
    cols = 2 * member.shape[1] // 128
    low_lane = lax.broadcasted_iota(jnp.int32, (half, 128), 1) < 64
    for pole in range(pieces // cols):
        for pair in range(cols // 2):
            rows = pole * 2 * half
            top = member[rows : rows + half, pair * 128 : pair * 128 + 128]
            bottom = member[rows + half : rows + 2 * half, pair * 128 : pair * 128 + 128]
            even = jnp.where(low_lane, top, pltpu.roll(bottom, 64, 1))
            odd = jnp.where(low_lane, pltpu.roll(top, 64, 1), bottom)
            out[pole * cols + 2 * pair, at : at + half] = even
            out[pole * cols + 2 * pair + 1, at : at + half] = odd


def column_body(weight, mine, other, ancestor, right, base, out, far):
    strips, half = ancestor.shape[1], ancestor.shape[2] // 2
    size = ancestor.shape[3]
    wide = mine.shape[1]
    top, bottom = ordered(mine[...], other[...])
    far[:, :half] = top.reshape(strips, half, wide)
    far[:, half:] = bottom.reshape(strips, half, wide)
    rows = far[...].reshape(strips * 2 * half, wide)
    by_real = contract(rows, ancestor[0].reshape(strips * 2 * half, size), 0, 0)
    by_imag = contract(rows, ancestor[1].reshape(strips * 2 * half, size), 0, 0)
    part_real = by_real[:size] - by_imag[size:]
    part_imag = by_real[size:] + by_imag[:size]
    weight_real, weight_imag = weight[0, 0], weight[0, 1]
    density = -(weight_real * part_imag + weight_imag * part_real)
    twin = -(weight_real * part_real - weight_imag * part_imag)
    high, low = split(jnp.concatenate([density, twin], axis=1))
    pivot = base[...] - (dot(high, right[...]) + dot(low, right[...]))
    fold(density, out, 0)
    fold(pivot, out, out.shape[1] // 2)


def sums_body(parts, spread, rows):
    half, width = parts.shape[1] // 2, rows.shape[1]
    total = jnp.sum(parts[...], axis=0)
    rows[:half] = total[:half, :width]
    rows[half:] = total[:half, width:]
    spread[...] = jnp.broadcast_to(total[None, half:], spread.shape)


def pivot_body(parts, out):
    half = parts.shape[1]
    width = 64
    cols = out.shape[1] // width
    total = jnp.sum(parts[...].reshape(-1, cols, half, 128), axis=0)
    for index in range(128 // width):
        lanes = slice(index * width, (index + 1) * width)
        strips = [total[col][:, lanes] for col in range(cols)]
        out[index * half : (index + 1) * half] = jnp.concatenate(strips, axis=1)


def update_body(shift, panel_h, panel_s, mine, other, out):
    strips, rows = out.shape[0], out.shape[1] * out.shape[2]
    half = mine.shape[0] // strips
    group = 4
    top, bottom = ordered(mine[...], other[...])
    real, imag = couple(panel_h[...], panel_s[...], shift[0, 0], shift[0, 1])
    wide = jnp.concatenate(
        [jnp.concatenate([real, -imag], axis=1), jnp.concatenate([imag, real], axis=1)], axis=0
    )
    for first in range(0, strips, group):
        solved = jnp.concatenate(
            [
                member[strip * half : (strip + 1) * half]
                for strip in range(first, first + group)
                for member in (top, bottom)
            ],
            axis=0,
        )
        update = contract(solved, wide, 1, 1)
        out[first : first + group] = update.reshape((group,) + out.shape[1:])


def schur_body(shift, pattern, update, *refs):
    shares, out = refs[:-1], refs[-1]
    strips, count, share, size = out.shape[1:]
    pole = lax.axis_index("pole")
    row = lax.axis_index("row")
    shift_real, shift_imag = shift[0, 0], shift[0, 1]
    for step, member in enumerate(shares):
        at = lax.rem(pole + count - step, count)
        for strip in range(strips):
            mask = pattern[strip, row].astype(f32)
            margin = mask * member[strip, share:].astype(f32)
            real = mask * member[strip, :share].astype(f32) - shift_real * margin
            out[0, strip, at] = (real - update[strip, at, :, :size]).astype(bf16)
            out[1, strip, at] = (-shift_imag * margin - update[strip, at, :, size:]).astype(bf16)


def shards(
    front_h,
    front_s,
    panel_h,
    panel_s,
    pivot_h,
    pivot_s,
    pole_shift,
    pole_weight,
    pattern,
    ancestor_inverse,
):
    row_count = lax.axis_size("row")
    col_count = lax.axis_size("col")
    pole_count = lax.axis_size("pole")
    col_index = lax.axis_index("col")
    size = pivot_h.shape[0]
    width = size // col_count
    piece = size // pole_count
    half = width // 2
    neighbour = [(i, i ^ 1) for i in range(row_count)]

    quarters = 4
    share = width // quarters

    (sent,) = pl.pallas_call(
        pack_body,
        out_shape=[shape(row_count, width + 2 * share, size)],
        in_specs=[pl.BlockSpec(memory_space=pl.ANY)] * 4,
        out_specs=[VMEM],
        scratch_shapes=[
            pltpu.VMEM((2, width, size), bf16),
            pltpu.VMEM((2, share, row_count * size), bf16),
            pltpu.SemaphoreType.DMA((4,)),
        ],
        cost_estimate=pl.CostEstimate(flops=0, bytes_accessed=2**20, transcendentals=0),
        name="pack",
    )(panel_h, panel_s, front_h, front_s)
    received = lax.all_to_all(sent, "row", split_axis=0, concat_axis=0, tiled=True)

    (inverse,) = call(
        invert_body,
        [shape(2, size, 2 * size)],
        [pole_shift, pivot_h, pivot_s],
        6 * 4 * 3 * 2 * size**3,
        "pivot_inverse",
    )
    mine, shared = call(
        solve_body,
        [shape(row_count * half, 2 * size), shape(row_count, 2 * share, size)],
        [pole_shift, received, inverse],
        2 * 8 * row_count * half * size * size,
        "solved_rows",
    )
    other = lax.ppermute(mine, "row", neighbour)
    right, base = call(
        local_body,
        [shape(2 * size, size), shape(size, size, dtype=f32)],
        [pole_shift, pole_weight, panel_h, panel_s, inverse],
        2 * 8 * size**3,
        "local_rows",
    )

    ancestor = ancestor_inverse.reshape(2, row_count, width, size)
    (both,) = pl.pallas_call(
        column_body,
        out_shape=[shape(pole_count * col_count, piece, 128, dtype=f32)],
        in_specs=[SMEM] + [VMEM] * 5,
        out_specs=[VMEM],
        scratch_shapes=[pltpu.VMEM((row_count, width, 2 * size), bf16)],
        compiler_params=pltpu.CompilerParams(vmem_limit_bytes=16 * 2**20),
        cost_estimate=pl.CostEstimate(
            flops=8 * row_count * width * size * size, bytes_accessed=4 * 2**20, transcendentals=0
        ),
        name="column",
    )(pole_weight, mine, other, ancestor, right, base)

    both = lax.all_to_all(both, ("pole", "col"), split_axis=0, concat_axis=0, tiled=True)
    spread, rows_out = call(
        sums_body,
        [
            shape(row_count * col_count, piece // 2, 128, dtype=f32),
            shape(piece, width, dtype=f32),
        ],
        [both],
        0,
        "sums",
    )
    shared, spread = lax.optimization_barrier((shared, spread))
    spread = lax.all_to_all(spread, ("row", "col"), split_axis=0, concat_axis=0, tiled=True)
    (pivot_out,) = call(pivot_body, [shape(piece, size, dtype=f32)], [spread], 0, "pivot")

    onward = [(i, (i + 1) % pole_count) for i in range(pole_count)]
    back = [(i, (i - 1) % pole_count) for i in range(pole_count)]
    before = lax.ppermute(shared, "pole", onward)
    after = lax.ppermute(shared, "pole", back)
    second = lax.ppermute(before, "pole", onward)

    (update,) = call(
        update_body,
        [shape(row_count, quarters, share, 2 * size, dtype=f32)],
        [pole_shift, panel_h, panel_s, mine, other],
        8 * row_count * width * size * size,
        "update",
    )
    (schur,) = call(
        schur_body,
        [shape(2, row_count, quarters, share, size)],
        [pole_shift, pattern, update, shared, before, second, after],
        0,
        "schur",
    )
    return (schur.reshape(1, 2, row_count, 1, width, size), rows_out.T, pivot_out.T)


def solution(mesh):
    in_specs = (
        P(("row", "col"), None),
        P(("row", "col"), None),
        P("row", None),
        P("row", None),
        P(),
        P(),
        P("pole", None),
        P("pole", None),
        P(),
        P("pole", None, None, "col", None, "row"),
    )
    out_specs = (
        P("pole", None, None, "col", None, "row"),
        P(("row", "col"), "pole"),
        P(None, "pole"),
    )
    return jax.shard_map(shards, mesh=mesh, in_specs=in_specs, out_specs=out_specs, check_vma=False)
```

```python
import functools

import jax
import jax.numpy as jnp
from jax import lax
from jax.experimental import pallas as pl
from jax.experimental.pallas import tpu as pltpu
from jax.sharding import PartitionSpec as P

bf16 = jnp.bfloat16
f32 = jnp.float32
VMEM = pl.BlockSpec(memory_space=pltpu.VMEM)
SMEM = pl.BlockSpec(memory_space=pltpu.SMEM)


def call(body, outs, ins, flops, name, grant=16):
    moved = sum(x.size * x.dtype.itemsize for x in list(ins) + list(outs))
    return pl.pallas_call(
        body,
        out_shape=outs,
        in_specs=[SMEM if x.size <= 256 else VMEM for x in ins],
        out_specs=[VMEM] * len(outs),
        compiler_params=pltpu.CompilerParams(vmem_limit_bytes=grant * 2**20),
        cost_estimate=pl.CostEstimate(flops=flops, bytes_accessed=moved, transcendentals=0),
        name=name,
    )(*ins)


def shape(*dims, dtype=bf16):
    return jax.ShapeDtypeStruct(dims, dtype)


def dot(left, right):
    return jnp.dot(left, right, preferred_element_type=f32)


def contract(left, right, axis_left, axis_right):
    dims = (((axis_left,), (axis_right,)), ((), ()))
    return lax.dot_general(left, right, dims, preferred_element_type=f32)


def split(value):
    high = value.astype(bf16)
    return high, (value - high.astype(f32)).astype(bf16)


def product(left, right):
    return dot(left[0], right[0]) + (dot(left[0], right[1]) + dot(left[1], right[0]))


def block(wide):
    size = wide.shape[1] // 2
    real, imag = wide[:, :size], wide[:, size:]
    return jnp.concatenate([wide, jnp.concatenate([-imag, real], axis=1)], axis=0)


def both_of(pair, form):
    return form(pair[0]), form(pair[1])


def couple(rows_h, rows_s, shift_real, shift_imag):
    margin = rows_s.astype(f32)
    real = (rows_h.astype(f32) - shift_real * margin).astype(bf16)
    imag = (-shift_imag * margin).astype(bf16)
    return real, imag


def invert_body(shift, pivot_h, pivot_s, inverse):
    size = pivot_h.shape[0]
    shift_real, shift_imag = shift[0, 0], shift[0, 1]
    margin = pivot_s[...].astype(f32)
    real = pivot_h[...].astype(f32) - shift_real * margin
    imag = -shift_imag * margin
    on_diag = lax.broadcasted_iota(jnp.int32, (size, size), 0) == lax.broadcasted_iota(
        jnp.int32, (size, size), 1
    )

    def scales(axis):
        diag_real = jnp.sum(jnp.where(on_diag, real, 0.0), axis=axis, keepdims=True)
        diag_imag = jnp.sum(jnp.where(on_diag, imag, 0.0), axis=axis, keepdims=True)
        denom = diag_real * diag_real + diag_imag * diag_imag
        return diag_real / denom, -diag_imag / denom

    col_real, col_imag = scales(0)
    err_real = jnp.where(on_diag, 0.0, imag * col_imag - real * col_real)
    err_imag = jnp.where(on_diag, 0.0, -(real * col_imag + imag * col_real))
    one = jnp.concatenate([jnp.where(on_diag, 1.0, 0.0), jnp.zeros((size, size), f32)], axis=1)
    err = jnp.concatenate([err_real, err_imag], axis=1)
    err_pair = split(err)
    err2 = product(err_pair, both_of(err_pair, block))
    err2_pair = split(err2)
    square = both_of(err2_pair, block)
    err3 = product(err_pair, square)
    err4_pair = split(product(err2_pair, square))
    first = one + err + err2 + err3
    fourth = both_of(err4_pair, block)
    second = first + product(split(first), fourth)
    err8_pair = split(product(err4_pair, fourth))
    total = second + product(split(second), both_of(err8_pair, block))
    sum_real, sum_imag = total[:, :size], total[:, size:]
    row_real, row_imag = scales(1)
    inv_real = row_real * sum_real - row_imag * sum_imag
    inv_imag = row_real * sum_imag + row_imag * sum_real
    inverse[0], inverse[1] = split(jnp.concatenate([inv_real, inv_imag], axis=1))


def solve(rows_h, rows_s, shift, inverse):
    coupling = jnp.concatenate(couple(rows_h, rows_s, shift[0, 0], shift[0, 1]), axis=1)
    return (dot(coupling, block(inverse[0])) + dot(coupling, block(inverse[1]))).astype(bf16)


def local_body(shift, weight, panel_h, panel_s, inverse, right, base):
    size = panel_h.shape[1]
    solved = solve(panel_h[...], panel_s[...], shift, inverse)
    right[:size] = solved[:, :size]
    right[size:] = solved[:, size:]
    whole = inverse[0].astype(f32) + inverse[1].astype(f32)
    density = weight[0, 0] * whole[:, size:] + weight[0, 1] * whole[:, :size]
    first_device = (lax.axis_index("row") == 0) & (lax.axis_index("col") == 0)
    base[...] = jnp.where(first_device, density.T, 0.0)


def pack_body(panel_h, panel_s, front_h, front_s, out, panels, fronts, sems):
    half = panels.shape[1] // 2
    share, size = fronts.shape[1], out.shape[2]
    shares = panels.shape[1] // share
    at = pl.ds(pl.multiple_of(lax.axis_index("col") * 2 * half, 2 * half), 2 * half)
    of = pl.ds(pl.multiple_of(lax.rem(lax.axis_index("pole"), shares) * share, share), share)
    copies = [
        pltpu.make_async_copy(panel_h.at[at], panels.at[0], sems.at[0]),
        pltpu.make_async_copy(panel_s.at[at], panels.at[1], sems.at[1]),
        pltpu.make_async_copy(front_h.at[of], fronts.at[0], sems.at[2]),
        pltpu.make_async_copy(front_s.at[of], fronts.at[1], sems.at[3]),
    ]
    for copy in copies:
        copy.start()
    for copy in copies:
        copy.wait()
    for row in range(out.shape[0]):
        core = row % 2
        for part in range(2):
            low = part * half
            out[row, low : low + half] = panels[part, core * half : (core + 1) * half]
            low = 2 * half + part * share
            out[row, low : low + share] = fronts[part, :, row * size : (row + 1) * size]


def solve_body(shift, received, inverse, solved, share):
    strips, rows, size = received.shape
    half = solved.shape[0] // strips
    rows_h = received[:, :half].reshape(strips * half, size)
    rows_s = received[:, half : 2 * half].reshape(strips * half, size)
    solved[...] = solve(rows_h, rows_s, shift, inverse)
    share[...] = received[:, 2 * half :]


def ordered(mine, other):
    low = lax.rem(lax.axis_index("row"), 2) == 0
    return jnp.where(low, mine, other), jnp.where(low, other, mine)


def fold(member, out, at):
    pieces = out.shape[0]
    half = out.shape[1] // 2
    cols = 2 * member.shape[1] // 128
    low_lane = lax.broadcasted_iota(jnp.int32, (half, 128), 1) < 64
    for pole in range(pieces // cols):
        for pair in range(cols // 2):
            rows = pole * 2 * half
            top = member[rows : rows + half, pair * 128 : pair * 128 + 128]
            bottom = member[rows + half : rows + 2 * half, pair * 128 : pair * 128 + 128]
            even = jnp.where(low_lane, top, pltpu.roll(bottom, 64, 1))
            odd = jnp.where(low_lane, pltpu.roll(top, 64, 1), bottom)
            out[pole * cols + 2 * pair, at : at + half] = even
            out[pole * cols + 2 * pair + 1, at : at + half] = odd


def column_body(weight, mine, other, ancestor, right, base, out, far):
    strips, half = ancestor.shape[1], ancestor.shape[2] // 2
    size = ancestor.shape[3]
    wide = mine.shape[1]
    top, bottom = ordered(mine[...], other[...])
    far[:, :half] = top.reshape(strips, half, wide)
    far[:, half:] = bottom.reshape(strips, half, wide)
    rows = far[...].reshape(strips * 2 * half, wide)
    by_real = contract(rows, ancestor[0].reshape(strips * 2 * half, size), 0, 0)
    by_imag = contract(rows, ancestor[1].reshape(strips * 2 * half, size), 0, 0)
    part_real = by_real[:size] - by_imag[size:]
    part_imag = by_real[size:] + by_imag[:size]
    weight_real, weight_imag = weight[0, 0], weight[0, 1]
    density = -(weight_real * part_imag + weight_imag * part_real)
    twin = -(weight_real * part_real - weight_imag * part_imag)
    high, low = split(jnp.concatenate([density, twin], axis=1))
    pivot = base[...] - (dot(high, right[...]) + dot(low, right[...]))
    fold(density, out, 0)
    fold(pivot, out, out.shape[1] // 2)


def sums_body(parts, spread, rows):
    half, width = parts.shape[1] // 2, rows.shape[1]
    total = jnp.sum(parts[...], axis=0)
    rows[:half] = total[:half, :width]
    rows[half:] = total[:half, width:]
    spread[...] = jnp.broadcast_to(total[None, half:], spread.shape)


def pivot_body(parts, out):
    half = parts.shape[1]
    width = 64
    cols = out.shape[1] // width
    total = jnp.sum(parts[...].reshape(-1, cols, half, 128), axis=0)
    for index in range(128 // width):
        lanes = slice(index * width, (index + 1) * width)
        strips = [total[col][:, lanes] for col in range(cols)]
        out[index * half : (index + 1) * half] = jnp.concatenate(strips, axis=1)


def update_body(shift, panel_h, panel_s, mine, other, out):
    strips, rows = out.shape[0], out.shape[1] * out.shape[2]
    half = mine.shape[0] // strips
    group = 4
    top, bottom = ordered(mine[...], other[...])
    real, imag = couple(panel_h[...], panel_s[...], shift[0, 0], shift[0, 1])
    wide = jnp.concatenate(
        [jnp.concatenate([real, -imag], axis=1), jnp.concatenate([imag, real], axis=1)], axis=0
    )
    for first in range(0, strips, group):
        solved = jnp.concatenate(
            [
                member[strip * half : (strip + 1) * half]
                for strip in range(first, first + group)
                for member in (top, bottom)
            ],
            axis=0,
        )
        update = contract(solved, wide, 1, 1)
        out[first : first + group] = update.reshape((group,) + out.shape[1:])


def schur_body(shift, pattern, update, *refs):
    shares, out = refs[:-1], refs[-1]
    strips, count, share, size = out.shape[1:]
    pole = lax.axis_index("pole")
    row = lax.axis_index("row")
    shift_real, shift_imag = shift[0, 0], shift[0, 1]
    for step, member in enumerate(shares):
        at = lax.rem(pole + count - step, count)
        for strip in range(strips):
            mask = pattern[strip, row].astype(f32)
            margin = mask * member[strip, share:].astype(f32)
            real = mask * member[strip, :share].astype(f32) - shift_real * margin
            out[0, strip, at] = (real - update[strip, at, :, :size]).astype(bf16)
            out[1, strip, at] = (-shift_imag * margin - update[strip, at, :, size:]).astype(bf16)


def shards(
    front_h,
    front_s,
    panel_h,
    panel_s,
    pivot_h,
    pivot_s,
    pole_shift,
    pole_weight,
    pattern,
    ancestor_inverse,
):
    row_count = lax.axis_size("row")
    col_count = lax.axis_size("col")
    pole_count = lax.axis_size("pole")
    col_index = lax.axis_index("col")
    size = pivot_h.shape[0]
    width = size // col_count
    piece = size // pole_count
    half = width // 2
    neighbour = [(i, i ^ 1) for i in range(row_count)]

    quarters = 4
    share = width // quarters

    (sent,) = pl.pallas_call(
        pack_body,
        out_shape=[shape(row_count, width + 2 * share, size)],
        in_specs=[pl.BlockSpec(memory_space=pl.ANY)] * 4,
        out_specs=[VMEM],
        scratch_shapes=[
            pltpu.VMEM((2, width, size), bf16),
            pltpu.VMEM((2, share, row_count * size), bf16),
            pltpu.SemaphoreType.DMA((4,)),
        ],
        cost_estimate=pl.CostEstimate(flops=0, bytes_accessed=2**20, transcendentals=0),
        name="pack",
    )(panel_h, panel_s, front_h, front_s)
    received = lax.all_to_all(sent, "row", split_axis=0, concat_axis=0, tiled=True)

    (inverse,) = call(
        invert_body,
        [shape(2, size, 2 * size)],
        [pole_shift, pivot_h, pivot_s],
        6 * 4 * 3 * 2 * size**3,
        "pivot_inverse",
    )
    mine, shared = call(
        solve_body,
        [shape(row_count * half, 2 * size), shape(row_count, 2 * share, size)],
        [pole_shift, received, inverse],
        2 * 8 * row_count * half * size * size,
        "solved_rows",
    )
    other = lax.ppermute(mine, "row", neighbour)
    right, base = call(
        local_body,
        [shape(2 * size, size), shape(size, size, dtype=f32)],
        [pole_shift, pole_weight, panel_h, panel_s, inverse],
        2 * 8 * size**3,
        "local_rows",
    )

    ancestor = ancestor_inverse.reshape(2, row_count, width, size)
    (both,) = pl.pallas_call(
        column_body,
        out_shape=[shape(pole_count * col_count, piece, 128, dtype=f32)],
        in_specs=[SMEM] + [VMEM] * 5,
        out_specs=[VMEM],
        scratch_shapes=[pltpu.VMEM((row_count, width, 2 * size), bf16)],
        compiler_params=pltpu.CompilerParams(vmem_limit_bytes=16 * 2**20),
        cost_estimate=pl.CostEstimate(
            flops=8 * row_count * width * size * size, bytes_accessed=4 * 2**20, transcendentals=0
        ),
        name="column",
    )(pole_weight, mine, other, ancestor, right, base)

    onward = [(i, (i + 1) % pole_count) for i in range(pole_count)]
    back = [(i, (i - 1) % pole_count) for i in range(pole_count)]
    shared, both = lax.optimization_barrier((shared, both))
    before = lax.ppermute(shared, "pole", onward)
    after = lax.ppermute(shared, "pole", back)

    both = lax.all_to_all(both, ("pole", "col"), split_axis=0, concat_axis=0, tiled=True)
    spread, rows_out = call(
        sums_body,
        [
            shape(row_count * col_count, piece // 2, 128, dtype=f32),
            shape(piece, width, dtype=f32),
        ],
        [both],
        0,
        "sums",
    )
    before, after, spread = lax.optimization_barrier((before, after, spread))
    second = lax.ppermute(before, "pole", onward)
    spread = lax.all_to_all(spread, ("row", "col"), split_axis=0, concat_axis=0, tiled=True)
    (pivot_out,) = call(pivot_body, [shape(piece, size, dtype=f32)], [spread], 0, "pivot")

    (update,) = call(
        update_body,
        [shape(row_count, quarters, share, 2 * size, dtype=f32)],
        [pole_shift, panel_h, panel_s, mine, other],
        8 * row_count * width * size * size,
        "update",
    )
    (schur,) = call(
        schur_body,
        [shape(2, row_count, quarters, share, size)],
        [pole_shift, pattern, update, shared, before, second, after],
        0,
        "schur",
    )
    return (schur.reshape(1, 2, row_count, 1, width, size), rows_out.T, pivot_out.T)


def solution(mesh):
    in_specs = (
        P(("row", "col"), None),
        P(("row", "col"), None),
        P("row", None),
        P("row", None),
        P(),
        P(),
        P("pole", None),
        P("pole", None),
        P(),
        P("pole", None, None, "col", None, "row"),
    )
    out_specs = (
        P("pole", None, None, "col", None, "row"),
        P(("row", "col"), "pole"),
        P(None, "pole"),
    )
    return jax.shard_map(shards, mesh=mesh, in_specs=in_specs, out_specs=out_specs, check_vma=False)
```

```python
import functools

import jax
import jax.numpy as jnp
from jax import lax
from jax.experimental import pallas as pl
from jax.experimental.pallas import tpu as pltpu
from jax.sharding import PartitionSpec as P

bf16 = jnp.bfloat16
f32 = jnp.float32
VMEM = pl.BlockSpec(memory_space=pltpu.VMEM)
SMEM = pl.BlockSpec(memory_space=pltpu.SMEM)


def call(body, outs, ins, flops, name, grant=16):
    moved = sum(x.size * x.dtype.itemsize for x in list(ins) + list(outs))
    return pl.pallas_call(
        body,
        out_shape=outs,
        in_specs=[SMEM if x.size <= 256 else VMEM for x in ins],
        out_specs=[VMEM] * len(outs),
        compiler_params=pltpu.CompilerParams(vmem_limit_bytes=grant * 2**20),
        cost_estimate=pl.CostEstimate(flops=flops, bytes_accessed=moved, transcendentals=0),
        name=name,
    )(*ins)


def shape(*dims, dtype=bf16):
    return jax.ShapeDtypeStruct(dims, dtype)


def dot(left, right):
    return jnp.dot(left, right, preferred_element_type=f32)


def contract(left, right, axis_left, axis_right):
    dims = (((axis_left,), (axis_right,)), ((), ()))
    return lax.dot_general(left, right, dims, preferred_element_type=f32)


def split(value):
    high = value.astype(bf16)
    return high, (value - high.astype(f32)).astype(bf16)


def product(left, right):
    return dot(left[0], right[0]) + (dot(left[0], right[1]) + dot(left[1], right[0]))


def block(wide):
    size = wide.shape[1] // 2
    real, imag = wide[:, :size], wide[:, size:]
    return jnp.concatenate([wide, jnp.concatenate([-imag, real], axis=1)], axis=0)


def both_of(pair, form):
    return form(pair[0]), form(pair[1])


def couple(rows_h, rows_s, shift_real, shift_imag):
    margin = rows_s.astype(f32)
    real = (rows_h.astype(f32) - shift_real * margin).astype(bf16)
    imag = (-shift_imag * margin).astype(bf16)
    return real, imag


def invert_body(shift, pivot_h, pivot_s, inverse):
    size = pivot_h.shape[0]
    shift_real, shift_imag = shift[0, 0], shift[0, 1]
    margin = pivot_s[...].astype(f32)
    real = pivot_h[...].astype(f32) - shift_real * margin
    imag = -shift_imag * margin
    on_diag = lax.broadcasted_iota(jnp.int32, (size, size), 0) == lax.broadcasted_iota(
        jnp.int32, (size, size), 1
    )

    def scales(axis):
        diag_real = jnp.sum(jnp.where(on_diag, real, 0.0), axis=axis, keepdims=True)
        diag_imag = jnp.sum(jnp.where(on_diag, imag, 0.0), axis=axis, keepdims=True)
        denom = diag_real * diag_real + diag_imag * diag_imag
        return diag_real / denom, -diag_imag / denom

    col_real, col_imag = scales(0)
    err_real = jnp.where(on_diag, 0.0, imag * col_imag - real * col_real)
    err_imag = jnp.where(on_diag, 0.0, -(real * col_imag + imag * col_real))
    one = jnp.concatenate([jnp.where(on_diag, 1.0, 0.0), jnp.zeros((size, size), f32)], axis=1)
    err = jnp.concatenate([err_real, err_imag], axis=1)
    err_pair = split(err)
    err2 = product(err_pair, both_of(err_pair, block))
    err2_pair = split(err2)
    square = both_of(err2_pair, block)
    err3 = product(err_pair, square)
    err4_pair = split(product(err2_pair, square))
    first = one + err + err2 + err3
    fourth = both_of(err4_pair, block)
    second = first + product(split(first), fourth)
    err8_pair = split(product(err4_pair, fourth))
    total = second + product(split(second), both_of(err8_pair, block))
    sum_real, sum_imag = total[:, :size], total[:, size:]
    row_real, row_imag = scales(1)
    inv_real = row_real * sum_real - row_imag * sum_imag
    inv_imag = row_real * sum_imag + row_imag * sum_real
    inverse[0], inverse[1] = split(jnp.concatenate([inv_real, inv_imag], axis=1))


def solve(rows_h, rows_s, shift, inverse):
    coupling = jnp.concatenate(couple(rows_h, rows_s, shift[0, 0], shift[0, 1]), axis=1)
    return (dot(coupling, block(inverse[0])) + dot(coupling, block(inverse[1]))).astype(bf16)


def local_body(shift, weight, panel_h, panel_s, inverse, right, base):
    size = panel_h.shape[1]
    solved = solve(panel_h[...], panel_s[...], shift, inverse)
    right[:size] = solved[:, :size]
    right[size:] = solved[:, size:]
    whole = inverse[0].astype(f32) + inverse[1].astype(f32)
    density = weight[0, 0] * whole[:, size:] + weight[0, 1] * whole[:, :size]
    first_device = (lax.axis_index("row") == 0) & (lax.axis_index("col") == 0)
    base[...] = jnp.where(first_device, density.T, 0.0)


def pack_body(panel_h, panel_s, front_h, front_s, out, sem):
    rows, height, size = out.shape
    shares = 4
    width = front_h.shape[0]
    half, share = width // 2, width // shares
    strip = lax.axis_index("col") * width
    of = pl.ds(pl.multiple_of(lax.rem(lax.axis_index("pole"), shares) * share, share), share)
    for row in range(rows):
        at = pl.ds(pl.multiple_of(strip + (row % 2) * half, half), half)
        columns = pl.ds(row * size, size)
        for part, (panel, front) in enumerate(((panel_h, front_h), (panel_s, front_s))):
            low = part * half
            pltpu.make_async_copy(panel.at[at], out.at[row, pl.ds(low, half)], sem).start()
            low = 2 * half + part * share
            pltpu.make_async_copy(
                front.at[of, columns], out.at[row, pl.ds(low, share)], sem
            ).start()
    pltpu.make_async_copy(out, out, sem).wait()


def solve_body(shift, received, inverse, solved, share):
    strips, rows, size = received.shape
    half = solved.shape[0] // strips
    rows_h = received[:, :half].reshape(strips * half, size)
    rows_s = received[:, half : 2 * half].reshape(strips * half, size)
    solved[...] = solve(rows_h, rows_s, shift, inverse)
    share[...] = received[:, 2 * half :]


def ordered(mine, other):
    low = lax.rem(lax.axis_index("row"), 2) == 0
    return jnp.where(low, mine, other), jnp.where(low, other, mine)


def fold(member, out, at):
    pieces = out.shape[0]
    half = out.shape[1] // 2
    cols = 2 * member.shape[1] // 128
    low_lane = lax.broadcasted_iota(jnp.int32, (half, 128), 1) < 64
    for pole in range(pieces // cols):
        for pair in range(cols // 2):
            rows = pole * 2 * half
            top = member[rows : rows + half, pair * 128 : pair * 128 + 128]
            bottom = member[rows + half : rows + 2 * half, pair * 128 : pair * 128 + 128]
            even = jnp.where(low_lane, top, pltpu.roll(bottom, 64, 1))
            odd = jnp.where(low_lane, pltpu.roll(top, 64, 1), bottom)
            out[pole * cols + 2 * pair, at : at + half] = even.astype(out.dtype)
            out[pole * cols + 2 * pair + 1, at : at + half] = odd.astype(out.dtype)


def column_body(weight, mine, other, ancestor, right, base, out, far):
    strips, half = ancestor.shape[1], ancestor.shape[2] // 2
    size = ancestor.shape[3]
    wide = mine.shape[1]
    top, bottom = ordered(mine[...], other[...])
    far[:, :half] = top.reshape(strips, half, wide)
    far[:, half:] = bottom.reshape(strips, half, wide)
    rows = far[...].reshape(strips * 2 * half, wide)
    by_real = contract(rows, ancestor[0].reshape(strips * 2 * half, size), 0, 0)
    by_imag = contract(rows, ancestor[1].reshape(strips * 2 * half, size), 0, 0)
    part_real = by_real[:size] - by_imag[size:]
    part_imag = by_real[size:] + by_imag[:size]
    weight_real, weight_imag = weight[0, 0], weight[0, 1]
    density = -(weight_real * part_imag + weight_imag * part_real)
    twin = -(weight_real * part_real - weight_imag * part_imag)
    high, low = split(jnp.concatenate([density, twin], axis=1))
    pivot = base[...] - (dot(high, right[...]) + dot(low, right[...]))
    fold(density, out, 0)
    fold(pivot, out, out.shape[1] // 2)


def sums_body(parts, spread, rows):
    half, width = parts.shape[1] // 2, rows.shape[1]
    total = jnp.sum(parts[...].astype(f32), axis=0)
    rows[:half] = total[:half, :width]
    rows[half:] = total[:half, width:]
    spread[...] = jnp.broadcast_to(total[None, half:].astype(spread.dtype), spread.shape)


def pivot_body(parts, out):
    half = parts.shape[1]
    width = 64
    cols = out.shape[1] // width
    total = jnp.sum(parts[...].astype(f32).reshape(-1, cols, half, 128), axis=0)
    for index in range(128 // width):
        lanes = slice(index * width, (index + 1) * width)
        strips = [total[col][:, lanes] for col in range(cols)]
        out[index * half : (index + 1) * half] = jnp.concatenate(strips, axis=1)


def update_body(shift, panel_h, panel_s, mine, other, out):
    strips, rows = out.shape[0], out.shape[1] * out.shape[2]
    half = mine.shape[0] // strips
    group = 4
    top, bottom = ordered(mine[...], other[...])
    real, imag = couple(panel_h[...], panel_s[...], shift[0, 0], shift[0, 1])
    wide = jnp.concatenate(
        [jnp.concatenate([real, -imag], axis=1), jnp.concatenate([imag, real], axis=1)], axis=0
    )
    for first in range(0, strips, group):
        solved = jnp.concatenate(
            [
                member[strip * half : (strip + 1) * half]
                for strip in range(first, first + group)
                for member in (top, bottom)
            ],
            axis=0,
        )
        update = contract(solved, wide, 1, 1)
        out[first : first + group] = update.reshape((group,) + out.shape[1:])


def schur_body(shift, pattern, update, *refs):
    shares, out = refs[:-1], refs[-1]
    strips, count, share, size = out.shape[1:]
    pole = lax.axis_index("pole")
    row = lax.axis_index("row")
    shift_real, shift_imag = shift[0, 0], shift[0, 1]
    for step, member in enumerate(shares):
        at = lax.rem(pole + count - step, count)
        for strip in range(strips):
            mask = pattern[strip, row].astype(f32)
            margin = mask * member[strip, share:].astype(f32)
            real = mask * member[strip, :share].astype(f32) - shift_real * margin
            out[0, strip, at] = (real - update[strip, at, :, :size]).astype(bf16)
            out[1, strip, at] = (-shift_imag * margin - update[strip, at, :, size:]).astype(bf16)


def shards(
    front_h,
    front_s,
    panel_h,
    panel_s,
    pivot_h,
    pivot_s,
    pole_shift,
    pole_weight,
    pattern,
    ancestor_inverse,
):
    row_count = lax.axis_size("row")
    col_count = lax.axis_size("col")
    pole_count = lax.axis_size("pole")
    col_index = lax.axis_index("col")
    size = pivot_h.shape[0]
    width = size // col_count
    piece = size // pole_count
    half = width // 2
    neighbour = [(i, i ^ 1) for i in range(row_count)]

    quarters = 4
    share = width // quarters

    (sent,) = pl.pallas_call(
        pack_body,
        out_shape=[shape(row_count, width + 2 * share, size)],
        in_specs=[pl.BlockSpec(memory_space=pl.ANY)] * 4,
        out_specs=[pl.BlockSpec(memory_space=pl.ANY)],
        scratch_shapes=[pltpu.SemaphoreType.DMA],
        cost_estimate=pl.CostEstimate(flops=0, bytes_accessed=2**20, transcendentals=0),
        name="pack",
    )(panel_h, panel_s, front_h, front_s)
    received = lax.all_to_all(sent, "row", split_axis=0, concat_axis=0, tiled=True)

    (inverse,) = call(
        invert_body,
        [shape(2, size, 2 * size)],
        [pole_shift, pivot_h, pivot_s],
        6 * 4 * 3 * 2 * size**3,
        "pivot_inverse",
    )
    mine, shared = call(
        solve_body,
        [shape(row_count * half, 2 * size), shape(row_count, 2 * share, size)],
        [pole_shift, received, inverse],
        2 * 8 * row_count * half * size * size,
        "solved_rows",
    )
    other = lax.ppermute(mine, "row", neighbour)
    right, base = call(
        local_body,
        [shape(2 * size, size), shape(size, size, dtype=f32)],
        [pole_shift, pole_weight, panel_h, panel_s, inverse],
        2 * 8 * size**3,
        "local_rows",
    )

    ancestor = ancestor_inverse.reshape(2, row_count, width, size)
    (both,) = pl.pallas_call(
        column_body,
        out_shape=[shape(pole_count * col_count, piece, 128)],
        in_specs=[SMEM] + [VMEM] * 5,
        out_specs=[VMEM],
        scratch_shapes=[pltpu.VMEM((row_count, width, 2 * size), bf16)],
        compiler_params=pltpu.CompilerParams(vmem_limit_bytes=16 * 2**20),
        cost_estimate=pl.CostEstimate(
            flops=8 * row_count * width * size * size, bytes_accessed=4 * 2**20, transcendentals=0
        ),
        name="column",
    )(pole_weight, mine, other, ancestor, right, base)

    onward = [(i, (i + 1) % pole_count) for i in range(pole_count)]
    back = [(i, (i - 1) % pole_count) for i in range(pole_count)]
    shared, both = lax.optimization_barrier((shared, both))
    before = lax.ppermute(shared, "pole", onward)
    after = lax.ppermute(shared, "pole", back)

    both = lax.all_to_all(both, ("pole", "col"), split_axis=0, concat_axis=0, tiled=True)
    spread, rows_out = call(
        sums_body,
        [
            shape(row_count * col_count, piece // 2, 128),
            shape(piece, width, dtype=f32),
        ],
        [both],
        0,
        "sums",
    )
    before, spread = lax.optimization_barrier((before, spread))
    second = lax.ppermute(before, "pole", onward)
    spread = lax.all_to_all(spread, ("row", "col"), split_axis=0, concat_axis=0, tiled=True)
    (pivot_out,) = call(pivot_body, [shape(piece, size, dtype=f32)], [spread], 0, "pivot")

    (update,) = call(
        update_body,
        [shape(row_count, quarters, share, 2 * size, dtype=f32)],
        [pole_shift, panel_h, panel_s, mine, other],
        8 * row_count * width * size * size,
        "update",
    )
    (schur,) = call(
        schur_body,
        [shape(2, row_count, quarters, share, size)],
        [pole_shift, pattern, update, shared, before, second, after],
        0,
        "schur",
    )
    return (schur.reshape(1, 2, row_count, 1, width, size), rows_out.T, pivot_out.T)


def solution(mesh):
    in_specs = (
        P(("row", "col"), None),
        P(("row", "col"), None),
        P("row", None),
        P("row", None),
        P(),
        P(),
        P("pole", None),
        P("pole", None),
        P(),
        P("pole", None, None, "col", None, "row"),
    )
    out_specs = (
        P("pole", None, None, "col", None, "row"),
        P(("row", "col"), "pole"),
        P(None, "pole"),
    )
    return jax.shard_map(shards, mesh=mesh, in_specs=in_specs, out_specs=out_specs, check_vma=False)
```

```python
import functools

import jax
import jax.numpy as jnp
from jax import lax
from jax.experimental import pallas as pl
from jax.experimental.pallas import tpu as pltpu
from jax.sharding import PartitionSpec as P

bf16 = jnp.bfloat16
f32 = jnp.float32
VMEM = pl.BlockSpec(memory_space=pltpu.VMEM)
SMEM = pl.BlockSpec(memory_space=pltpu.SMEM)


def call(body, outs, ins, flops, name, grant=16):
    moved = sum(x.size * x.dtype.itemsize for x in list(ins) + list(outs))
    return pl.pallas_call(
        body,
        out_shape=outs,
        in_specs=[SMEM if x.size <= 256 else VMEM for x in ins],
        out_specs=[VMEM] * len(outs),
        compiler_params=pltpu.CompilerParams(vmem_limit_bytes=grant * 2**20),
        cost_estimate=pl.CostEstimate(flops=flops, bytes_accessed=moved, transcendentals=0),
        name=name,
    )(*ins)


def shape(*dims, dtype=bf16):
    return jax.ShapeDtypeStruct(dims, dtype)


def dot(left, right):
    return jnp.dot(left, right, preferred_element_type=f32)


def contract(left, right, axis_left, axis_right):
    dims = (((axis_left,), (axis_right,)), ((), ()))
    return lax.dot_general(left, right, dims, preferred_element_type=f32)


def split(value):
    high = value.astype(bf16)
    return high, (value - high.astype(f32)).astype(bf16)


def product(left, right):
    return dot(left[0], right[0]) + (dot(left[0], right[1]) + dot(left[1], right[0]))


def block(wide):
    size = wide.shape[1] // 2
    real, imag = wide[:, :size], wide[:, size:]
    return jnp.concatenate([wide, jnp.concatenate([-imag, real], axis=1)], axis=0)


def both_of(pair, form):
    return form(pair[0]), form(pair[1])


def couple(rows_h, rows_s, shift_real, shift_imag):
    margin = rows_s.astype(f32)
    real = (rows_h.astype(f32) - shift_real * margin).astype(bf16)
    imag = (-shift_imag * margin).astype(bf16)
    return real, imag


def invert_body(shift, pivot_h, pivot_s, inverse):
    size = pivot_h.shape[0]
    shift_real, shift_imag = shift[0, 0], shift[0, 1]
    margin = pivot_s[...].astype(f32)
    real = pivot_h[...].astype(f32) - shift_real * margin
    imag = -shift_imag * margin
    on_diag = lax.broadcasted_iota(jnp.int32, (size, size), 0) == lax.broadcasted_iota(
        jnp.int32, (size, size), 1
    )

    def scales(axis):
        diag_real = jnp.sum(jnp.where(on_diag, real, 0.0), axis=axis, keepdims=True)
        diag_imag = jnp.sum(jnp.where(on_diag, imag, 0.0), axis=axis, keepdims=True)
        denom = diag_real * diag_real + diag_imag * diag_imag
        return diag_real / denom, -diag_imag / denom

    col_real, col_imag = scales(0)
    err_real = jnp.where(on_diag, 0.0, imag * col_imag - real * col_real)
    err_imag = jnp.where(on_diag, 0.0, -(real * col_imag + imag * col_real))
    one = jnp.concatenate([jnp.where(on_diag, 1.0, 0.0), jnp.zeros((size, size), f32)], axis=1)
    err = jnp.concatenate([err_real, err_imag], axis=1)
    err_pair = split(err)
    err2 = product(err_pair, both_of(err_pair, block))
    err2_pair = split(err2)
    square = both_of(err2_pair, block)
    err3 = product(err_pair, square)
    err4_pair = split(product(err2_pair, square))
    first = one + err + err2 + err3
    fourth = both_of(err4_pair, block)
    second = first + product(split(first), fourth)
    err8_pair = split(product(err4_pair, fourth))
    total = second + product(split(second), both_of(err8_pair, block))
    sum_real, sum_imag = total[:, :size], total[:, size:]
    row_real, row_imag = scales(1)
    inv_real = row_real * sum_real - row_imag * sum_imag
    inv_imag = row_real * sum_imag + row_imag * sum_real
    inverse[0], inverse[1] = split(jnp.concatenate([inv_real, inv_imag], axis=1))


def solve(rows_h, rows_s, shift, inverse):
    coupling = jnp.concatenate(couple(rows_h, rows_s, shift[0, 0], shift[0, 1]), axis=1)
    return (dot(coupling, block(inverse[0])) + dot(coupling, block(inverse[1]))).astype(bf16)


def local_body(shift, weight, panel_h, panel_s, inverse, right, base):
    size = panel_h.shape[1]
    solved = solve(panel_h[...], panel_s[...], shift, inverse)
    right[:size] = solved[:, :size]
    right[size:] = solved[:, size:]
    whole = inverse[0].astype(f32) + inverse[1].astype(f32)
    density = weight[0, 0] * whole[:, size:] + weight[0, 1] * whole[:, :size]
    first_device = (lax.axis_index("row") == 0) & (lax.axis_index("col") == 0)
    base[...] = jnp.where(first_device, density.T, 0.0)


def pack_body(panel_h, panel_s, front_h, front_s, out, panels, fronts, sems):
    half = panels.shape[1] // 2
    share, size = fronts.shape[1], out.shape[2]
    shares = panels.shape[1] // share
    at = pl.ds(pl.multiple_of(lax.axis_index("col") * 2 * half, 2 * half), 2 * half)
    of = pl.ds(pl.multiple_of(lax.rem(lax.axis_index("pole"), shares) * share, share), share)
    copies = [
        pltpu.make_async_copy(panel_h.at[at], panels.at[0], sems.at[0]),
        pltpu.make_async_copy(panel_s.at[at], panels.at[1], sems.at[1]),
        pltpu.make_async_copy(front_h.at[of], fronts.at[0], sems.at[2]),
        pltpu.make_async_copy(front_s.at[of], fronts.at[1], sems.at[3]),
    ]
    for copy in copies:
        copy.start()
    for copy in copies:
        copy.wait()
    for row in range(out.shape[0]):
        core = row % 2
        for part in range(2):
            low = part * half
            out[row, low : low + half] = panels[part, core * half : (core + 1) * half]
            low = 2 * half + part * share
            out[row, low : low + share] = fronts[part, :, row * size : (row + 1) * size]


def solve_body(shift, received, inverse, solved, share):
    strips, rows, size = received.shape
    half = solved.shape[0] // strips
    rows_h = received[:, :half].reshape(strips * half, size)
    rows_s = received[:, half : 2 * half].reshape(strips * half, size)
    solved[...] = solve(rows_h, rows_s, shift, inverse)
    share[...] = received[:, 2 * half :]


def ordered(mine, other):
    low = lax.rem(lax.axis_index("row"), 2) == 0
    return jnp.where(low, mine, other), jnp.where(low, other, mine)


def fold(member, out, at):
    pieces = out.shape[0]
    half = out.shape[1] // 2
    cols = 2 * member.shape[1] // 128
    low_lane = lax.broadcasted_iota(jnp.int32, (half, 128), 1) < 64
    for pole in range(pieces // cols):
        for pair in range(cols // 2):
            rows = pole * 2 * half
            top = member[rows : rows + half, pair * 128 : pair * 128 + 128]
            bottom = member[rows + half : rows + 2 * half, pair * 128 : pair * 128 + 128]
            even = jnp.where(low_lane, top, pltpu.roll(bottom, 64, 1))
            odd = jnp.where(low_lane, pltpu.roll(top, 64, 1), bottom)
            out[pole * cols + 2 * pair, at : at + half] = even.astype(out.dtype)
            out[pole * cols + 2 * pair + 1, at : at + half] = odd.astype(out.dtype)


def column_body(weight, mine, other, ancestor, right, base, out, far):
    strips, half = ancestor.shape[1], ancestor.shape[2] // 2
    size = ancestor.shape[3]
    wide = mine.shape[1]
    top, bottom = ordered(mine[...], other[...])
    far[:, :half] = top.reshape(strips, half, wide)
    far[:, half:] = bottom.reshape(strips, half, wide)
    rows = far[...].reshape(strips * 2 * half, wide)
    by_real = contract(rows, ancestor[0].reshape(strips * 2 * half, size), 0, 0)
    by_imag = contract(rows, ancestor[1].reshape(strips * 2 * half, size), 0, 0)
    part_real = by_real[:size] - by_imag[size:]
    part_imag = by_real[size:] + by_imag[:size]
    weight_real, weight_imag = weight[0, 0], weight[0, 1]
    density = -(weight_real * part_imag + weight_imag * part_real)
    twin = -(weight_real * part_real - weight_imag * part_imag)
    high, low = split(jnp.concatenate([density, twin], axis=1))
    pivot = base[...] - (dot(high, right[...]) + dot(low, right[...]))
    fold(density, out, 0)
    fold(pivot, out, out.shape[1] // 2)


def sums_body(parts, spread, rows):
    half, width = parts.shape[1] // 2, rows.shape[1]
    total = jnp.sum(parts[...].astype(f32), axis=0)
    rows[:half] = total[:half, :width]
    rows[half:] = total[:half, width:]
    spread[...] = jnp.broadcast_to(total[None, half:].astype(spread.dtype), spread.shape)


def pivot_body(parts, out):
    half = parts.shape[1]
    width = 64
    cols = out.shape[1] // width
    total = jnp.sum(parts[...].astype(f32).reshape(-1, cols, half, 128), axis=0)
    for index in range(128 // width):
        lanes = slice(index * width, (index + 1) * width)
        strips = [total[col][:, lanes] for col in range(cols)]
        out[index * half : (index + 1) * half] = jnp.concatenate(strips, axis=1)


def update_body(shift, panel_h, panel_s, mine, other, out):
    strips, rows = out.shape[0], out.shape[1] * out.shape[2]
    half = mine.shape[0] // strips
    group = 4
    top, bottom = ordered(mine[...], other[...])
    real, imag = couple(panel_h[...], panel_s[...], shift[0, 0], shift[0, 1])
    wide = jnp.concatenate(
        [jnp.concatenate([real, -imag], axis=1), jnp.concatenate([imag, real], axis=1)], axis=0
    )
    for first in range(0, strips, group):
        solved = jnp.concatenate(
            [
                member[strip * half : (strip + 1) * half]
                for strip in range(first, first + group)
                for member in (top, bottom)
            ],
            axis=0,
        )
        update = contract(solved, wide, 1, 1)
        out[first : first + group] = update.reshape((group,) + out.shape[1:])


def schur_body(shift, pattern, update, *refs):
    shares, out = refs[:-1], refs[-1]
    strips, count, share, size = out.shape[1:]
    pole = lax.axis_index("pole")
    row = lax.axis_index("row")
    shift_real, shift_imag = shift[0, 0], shift[0, 1]
    for step, member in enumerate(shares):
        at = lax.rem(pole + count - step, count)
        for strip in range(strips):
            mask = pattern[strip, row].astype(f32)
            margin = mask * member[strip, share:].astype(f32)
            real = mask * member[strip, :share].astype(f32) - shift_real * margin
            out[0, strip, at] = (real - update[strip, at, :, :size]).astype(bf16)
            out[1, strip, at] = (-shift_imag * margin - update[strip, at, :, size:]).astype(bf16)


def shards(
    front_h,
    front_s,
    panel_h,
    panel_s,
    pivot_h,
    pivot_s,
    pole_shift,
    pole_weight,
    pattern,
    ancestor_inverse,
):
    row_count = lax.axis_size("row")
    col_count = lax.axis_size("col")
    pole_count = lax.axis_size("pole")
    col_index = lax.axis_index("col")
    size = pivot_h.shape[0]
    width = size // col_count
    piece = size // pole_count
    half = width // 2
    neighbour = [(i, i ^ 1) for i in range(row_count)]

    quarters = 4
    share = width // quarters

    (sent,) = pl.pallas_call(
        pack_body,
        out_shape=[shape(row_count, width + 2 * share, size)],
        in_specs=[pl.BlockSpec(memory_space=pl.ANY)] * 4,
        out_specs=[VMEM],
        scratch_shapes=[
            pltpu.VMEM((2, width, size), bf16),
            pltpu.VMEM((2, share, row_count * size), bf16),
            pltpu.SemaphoreType.DMA((4,)),
        ],
        cost_estimate=pl.CostEstimate(flops=0, bytes_accessed=2**20, transcendentals=0),
        name="pack",
    )(panel_h, panel_s, front_h, front_s)
    received = lax.all_to_all(sent, "row", split_axis=0, concat_axis=0, tiled=True)

    (inverse,) = call(
        invert_body,
        [shape(2, size, 2 * size)],
        [pole_shift, pivot_h, pivot_s],
        6 * 4 * 3 * 2 * size**3,
        "pivot_inverse",
    )
    mine, shared = call(
        solve_body,
        [shape(row_count * half, 2 * size), shape(row_count, 2 * share, size)],
        [pole_shift, received, inverse],
        2 * 8 * row_count * half * size * size,
        "solved_rows",
    )
    other = lax.ppermute(mine, "row", neighbour)
    right, base = call(
        local_body,
        [shape(2 * size, size), shape(size, size, dtype=f32)],
        [pole_shift, pole_weight, panel_h, panel_s, inverse],
        2 * 8 * size**3,
        "local_rows",
    )

    ancestor = ancestor_inverse.reshape(2, row_count, width, size)
    (both,) = pl.pallas_call(
        column_body,
        out_shape=[shape(pole_count * col_count, piece, 128)],
        in_specs=[SMEM] + [VMEM] * 5,
        out_specs=[VMEM],
        scratch_shapes=[pltpu.VMEM((row_count, width, 2 * size), bf16)],
        compiler_params=pltpu.CompilerParams(vmem_limit_bytes=16 * 2**20),
        cost_estimate=pl.CostEstimate(
            flops=8 * row_count * width * size * size, bytes_accessed=4 * 2**20, transcendentals=0
        ),
        name="column",
    )(pole_weight, mine, other, ancestor, right, base)

    onward = [(i, (i + 1) % pole_count) for i in range(pole_count)]
    back = [(i, (i - 1) % pole_count) for i in range(pole_count)]
    shared, both = lax.optimization_barrier((shared, both))
    before = lax.ppermute(shared, "pole", onward)
    after = lax.ppermute(shared, "pole", back)

    both = lax.all_to_all(both, ("pole", "col"), split_axis=0, concat_axis=0, tiled=True)
    spread, rows_out = call(
        sums_body,
        [
            shape(row_count * col_count, piece // 2, 128),
            shape(piece, width, dtype=f32),
        ],
        [both],
        0,
        "sums",
    )
    before, spread = lax.optimization_barrier((before, spread))
    second = lax.ppermute(before, "pole", onward)
    spread = lax.all_to_all(spread, ("row", "col"), split_axis=0, concat_axis=0, tiled=True)
    (pivot_out,) = call(pivot_body, [shape(piece, size, dtype=f32)], [spread], 0, "pivot")

    (update,) = call(
        update_body,
        [shape(row_count, quarters, share, 2 * size, dtype=f32)],
        [pole_shift, panel_h, panel_s, mine, other],
        8 * row_count * width * size * size,
        "update",
    )
    (schur,) = call(
        schur_body,
        [shape(2, row_count, quarters, share, size)],
        [pole_shift, pattern, update, shared, before, second, after],
        0,
        "schur",
    )
    return (schur.reshape(1, 2, row_count, 1, width, size), rows_out.T, pivot_out.T)


def solution(mesh):
    in_specs = (
        P(("row", "col"), None),
        P(("row", "col"), None),
        P("row", None),
        P("row", None),
        P(),
        P(),
        P("pole", None),
        P("pole", None),
        P(),
        P("pole", None, None, "col", None, "row"),
    )
    out_specs = (
        P("pole", None, None, "col", None, "row"),
        P(("row", "col"), "pole"),
        P(None, "pole"),
    )
    return jax.shard_map(shards, mesh=mesh, in_specs=in_specs, out_specs=out_specs, check_vma=False)
```

```python
import functools

import jax
import jax.numpy as jnp
from jax import lax
from jax.experimental import pallas as pl
from jax.experimental.pallas import tpu as pltpu
from jax.sharding import PartitionSpec as P

bf16 = jnp.bfloat16
f32 = jnp.float32
VMEM = pl.BlockSpec(memory_space=pltpu.VMEM)
SMEM = pl.BlockSpec(memory_space=pltpu.SMEM)


def call(body, outs, ins, flops, name, grant=16):
    moved = sum(x.size * x.dtype.itemsize for x in list(ins) + list(outs))
    return pl.pallas_call(
        body,
        out_shape=outs,
        in_specs=[SMEM if x.size <= 256 else VMEM for x in ins],
        out_specs=[VMEM] * len(outs),
        compiler_params=pltpu.CompilerParams(vmem_limit_bytes=grant * 2**20),
        cost_estimate=pl.CostEstimate(flops=flops, bytes_accessed=moved, transcendentals=0),
        name=name,
    )(*ins)


def shape(*dims, dtype=bf16):
    return jax.ShapeDtypeStruct(dims, dtype)


def dot(left, right):
    return jnp.dot(left, right, preferred_element_type=f32)


def contract(left, right, axis_left, axis_right):
    dims = (((axis_left,), (axis_right,)), ((), ()))
    return lax.dot_general(left, right, dims, preferred_element_type=f32)


def split(value):
    high = value.astype(bf16)
    return high, (value - high.astype(f32)).astype(bf16)


def product(left, right):
    return dot(left[0], right[0]) + (dot(left[0], right[1]) + dot(left[1], right[0]))


def block(wide):
    size = wide.shape[1] // 2
    real, imag = wide[:, :size], wide[:, size:]
    return jnp.concatenate([wide, jnp.concatenate([-imag, real], axis=1)], axis=0)


def both_of(pair, form):
    return form(pair[0]), form(pair[1])


def couple(rows_h, rows_s, shift_real, shift_imag):
    margin = rows_s.astype(f32)
    real = (rows_h.astype(f32) - shift_real * margin).astype(bf16)
    imag = (-shift_imag * margin).astype(bf16)
    return real, imag


def invert_body(shift, pivot_h, pivot_s, inverse):
    size = pivot_h.shape[0]
    shift_real, shift_imag = shift[0, 0], shift[0, 1]
    margin = pivot_s[...].astype(f32)
    real = pivot_h[...].astype(f32) - shift_real * margin
    imag = -shift_imag * margin
    on_diag = lax.broadcasted_iota(jnp.int32, (size, size), 0) == lax.broadcasted_iota(
        jnp.int32, (size, size), 1
    )

    def scales(axis):
        diag_real = jnp.sum(jnp.where(on_diag, real, 0.0), axis=axis, keepdims=True)
        diag_imag = jnp.sum(jnp.where(on_diag, imag, 0.0), axis=axis, keepdims=True)
        denom = diag_real * diag_real + diag_imag * diag_imag
        return diag_real / denom, -diag_imag / denom

    col_real, col_imag = scales(0)
    err_real = jnp.where(on_diag, 0.0, imag * col_imag - real * col_real)
    err_imag = jnp.where(on_diag, 0.0, -(real * col_imag + imag * col_real))
    one = jnp.concatenate([jnp.where(on_diag, 1.0, 0.0), jnp.zeros((size, size), f32)], axis=1)
    err = jnp.concatenate([err_real, err_imag], axis=1)
    err_pair = split(err)
    err2 = product(err_pair, both_of(err_pair, block))
    err2_pair = split(err2)
    square = both_of(err2_pair, block)
    err3 = product(err_pair, square)
    err4_pair = split(product(err2_pair, square))
    first = one + err + err2 + err3
    fourth = both_of(err4_pair, block)
    second = first + product(split(first), fourth)
    err8_pair = split(product(err4_pair, fourth))
    total = second + product(split(second), both_of(err8_pair, block))
    sum_real, sum_imag = total[:, :size], total[:, size:]
    row_real, row_imag = scales(1)
    inv_real = row_real * sum_real - row_imag * sum_imag
    inv_imag = row_real * sum_imag + row_imag * sum_real
    inverse[0], inverse[1] = split(jnp.concatenate([inv_real, inv_imag], axis=1))


def solve(rows_h, rows_s, shift, inverse):
    coupling = jnp.concatenate(couple(rows_h, rows_s, shift[0, 0], shift[0, 1]), axis=1)
    return (dot(coupling, block(inverse[0])) + dot(coupling, block(inverse[1]))).astype(bf16)


def local_body(shift, weight, panel_h, panel_s, inverse, right, base):
    size = panel_h.shape[1]
    solved = solve(panel_h[...], panel_s[...], shift, inverse)
    right[:size] = solved[:, :size]
    right[size:] = solved[:, size:]
    whole = inverse[0].astype(f32) + inverse[1].astype(f32)
    density = weight[0, 0] * whole[:, size:] + weight[0, 1] * whole[:, :size]
    first_device = (lax.axis_index("row") == 0) & (lax.axis_index("col") == 0)
    base[...] = jnp.where(first_device, density.T, 0.0)


def pack_body(panel_h, panel_s, front_h, front_s, out, panels, fronts, sems):
    half = panels.shape[1] // 2
    share, size = fronts.shape[1], out.shape[2]
    shares = panels.shape[1] // share
    at = pl.ds(pl.multiple_of(lax.axis_index("col") * 2 * half, 2 * half), 2 * half)
    of = pl.ds(pl.multiple_of(lax.rem(lax.axis_index("pole"), shares) * share, share), share)
    copies = [
        pltpu.make_async_copy(panel_h.at[at], panels.at[0], sems.at[0]),
        pltpu.make_async_copy(panel_s.at[at], panels.at[1], sems.at[1]),
        pltpu.make_async_copy(front_h.at[of], fronts.at[0], sems.at[2]),
        pltpu.make_async_copy(front_s.at[of], fronts.at[1], sems.at[3]),
    ]
    for copy in copies:
        copy.start()
    for copy in copies:
        copy.wait()
    for row in range(out.shape[0]):
        core = row % 2
        for part in range(2):
            low = part * half
            out[row, low : low + half] = panels[part, core * half : (core + 1) * half]
            low = 2 * half + part * share
            out[row, low : low + share] = fronts[part, :, row * size : (row + 1) * size]


def solve_body(shift, received, inverse, solved, low, high):
    strips, rows, size = received.shape
    half = solved.shape[0] // strips
    rows_h = received[:, :half].reshape(strips * half, size)
    rows_s = received[:, half : 2 * half].reshape(strips * half, size)
    solved[...] = solve(rows_h, rows_s, shift, inverse)
    low[...] = received[: strips // 2, 2 * half :]
    high[...] = received[strips // 2 :, 2 * half :]


def ordered(mine, other):
    low = lax.rem(lax.axis_index("row"), 2) == 0
    return jnp.where(low, mine, other), jnp.where(low, other, mine)


def fold(member, out, at):
    pieces = out.shape[0]
    half = out.shape[1] // 2
    cols = 2 * member.shape[1] // 128
    low_lane = lax.broadcasted_iota(jnp.int32, (half, 128), 1) < 64
    for pole in range(pieces // cols):
        for pair in range(cols // 2):
            rows = pole * 2 * half
            top = member[rows : rows + half, pair * 128 : pair * 128 + 128]
            bottom = member[rows + half : rows + 2 * half, pair * 128 : pair * 128 + 128]
            even = jnp.where(low_lane, top, pltpu.roll(bottom, 64, 1))
            odd = jnp.where(low_lane, pltpu.roll(top, 64, 1), bottom)
            out[pole * cols + 2 * pair, at : at + half] = even.astype(out.dtype)
            out[pole * cols + 2 * pair + 1, at : at + half] = odd.astype(out.dtype)


def column_body(weight, mine, other, ancestor, right, base, out, far):
    strips, half = ancestor.shape[1], ancestor.shape[2] // 2
    size = ancestor.shape[3]
    wide = mine.shape[1]
    top, bottom = ordered(mine[...], other[...])
    far[:, :half] = top.reshape(strips, half, wide)
    far[:, half:] = bottom.reshape(strips, half, wide)
    rows = far[...].reshape(strips * 2 * half, wide)
    by_real = contract(rows, ancestor[0].reshape(strips * 2 * half, size), 0, 0)
    by_imag = contract(rows, ancestor[1].reshape(strips * 2 * half, size), 0, 0)
    part_real = by_real[:size] - by_imag[size:]
    part_imag = by_real[size:] + by_imag[:size]
    weight_real, weight_imag = weight[0, 0], weight[0, 1]
    density = -(weight_real * part_imag + weight_imag * part_real)
    twin = -(weight_real * part_real - weight_imag * part_imag)
    high, low = split(jnp.concatenate([density, twin], axis=1))
    pivot = base[...] - (dot(high, right[...]) + dot(low, right[...]))
    fold(density, out, 0)
    fold(pivot, out, out.shape[1] // 2)


def sums_body(parts, spread, rows):
    half, width = parts.shape[1] // 2, rows.shape[1]
    total = jnp.sum(parts[...].astype(f32), axis=0)
    rows[:half] = total[:half, :width]
    rows[half:] = total[:half, width:]
    spread[...] = jnp.broadcast_to(total[None, half:].astype(spread.dtype), spread.shape)


def pivot_body(parts, out):
    half = parts.shape[1]
    width = 64
    cols = out.shape[1] // width
    total = jnp.sum(parts[...].astype(f32).reshape(-1, cols, half, 128), axis=0)
    for index in range(128 // width):
        lanes = slice(index * width, (index + 1) * width)
        strips = [total[col][:, lanes] for col in range(cols)]
        out[index * half : (index + 1) * half] = jnp.concatenate(strips, axis=1)


def update_body(shift, panel_h, panel_s, mine, other, out):
    strips, rows = out.shape[0], out.shape[1] * out.shape[2]
    half = mine.shape[0] // strips
    group = 4
    top, bottom = ordered(mine[...], other[...])
    real, imag = couple(panel_h[...], panel_s[...], shift[0, 0], shift[0, 1])
    wide = jnp.concatenate(
        [jnp.concatenate([real, -imag], axis=1), jnp.concatenate([imag, real], axis=1)], axis=0
    )
    for first in range(0, strips, group):
        solved = jnp.concatenate(
            [
                member[strip * half : (strip + 1) * half]
                for strip in range(first, first + group)
                for member in (top, bottom)
            ],
            axis=0,
        )
        update = contract(solved, wide, 1, 1)
        out[first : first + group] = update.reshape((group,) + out.shape[1:])


def schur_body(shift, pattern, update, *refs):
    low, high, from_below, from_above, below, above, out = refs
    strips, count, share, size = out.shape[1:]
    half = strips // 2
    pole = lax.axis_index("pole")
    row = lax.axis_index("row")
    shift_real, shift_imag = shift[0, 0], shift[0, 1]
    members = (
        (low, 0, 0, 0),
        (high, 0, 0, half),
        (from_below, 0, -1, 0),
        (below, 0, -1, half),
        (below, half, -2, 0),
        (above, 0, 1, 0),
        (from_above, 0, 1, half),
        (above, half, 2, half),
    )
    for member, start, step, first in members:
        at = lax.rem(pole + count + step, count)
        for index in range(half):
            strip = first + index
            mask = pattern[strip, row].astype(f32)
            margin = mask * member[start + index, share:].astype(f32)
            real = mask * member[start + index, :share].astype(f32) - shift_real * margin
            out[0, strip, at] = (real - update[strip, at, :, :size]).astype(bf16)
            out[1, strip, at] = (-shift_imag * margin - update[strip, at, :, size:]).astype(bf16)


def shards(
    front_h,
    front_s,
    panel_h,
    panel_s,
    pivot_h,
    pivot_s,
    pole_shift,
    pole_weight,
    pattern,
    ancestor_inverse,
):
    row_count = lax.axis_size("row")
    col_count = lax.axis_size("col")
    pole_count = lax.axis_size("pole")
    col_index = lax.axis_index("col")
    size = pivot_h.shape[0]
    width = size // col_count
    piece = size // pole_count
    half = width // 2
    neighbour = [(i, i ^ 1) for i in range(row_count)]

    quarters = 4
    share = width // quarters

    (sent,) = pl.pallas_call(
        pack_body,
        out_shape=[shape(row_count, width + 2 * share, size)],
        in_specs=[pl.BlockSpec(memory_space=pl.ANY)] * 4,
        out_specs=[VMEM],
        scratch_shapes=[
            pltpu.VMEM((2, width, size), bf16),
            pltpu.VMEM((2, share, row_count * size), bf16),
            pltpu.SemaphoreType.DMA((4,)),
        ],
        cost_estimate=pl.CostEstimate(flops=0, bytes_accessed=2**20, transcendentals=0),
        name="pack",
    )(panel_h, panel_s, front_h, front_s)
    received = lax.all_to_all(sent, "row", split_axis=0, concat_axis=0, tiled=True)

    (inverse,) = call(
        invert_body,
        [shape(2, size, 2 * size)],
        [pole_shift, pivot_h, pivot_s],
        6 * 4 * 3 * 2 * size**3,
        "pivot_inverse",
    )
    mine, low, high = call(
        solve_body,
        [shape(row_count * half, 2 * size)] + [shape(row_count // 2, 2 * share, size)] * 2,
        [pole_shift, received, inverse],
        2 * 8 * row_count * half * size * size,
        "solved_rows",
    )
    other = lax.ppermute(mine, "row", neighbour)
    right, base = call(
        local_body,
        [shape(2 * size, size), shape(size, size, dtype=f32)],
        [pole_shift, pole_weight, panel_h, panel_s, inverse],
        2 * 8 * size**3,
        "local_rows",
    )

    ancestor = ancestor_inverse.reshape(2, row_count, width, size)
    (both,) = pl.pallas_call(
        column_body,
        out_shape=[shape(pole_count * col_count, piece, 128)],
        in_specs=[SMEM] + [VMEM] * 5,
        out_specs=[VMEM],
        scratch_shapes=[pltpu.VMEM((row_count, width, 2 * size), bf16)],
        compiler_params=pltpu.CompilerParams(vmem_limit_bytes=16 * 2**20),
        cost_estimate=pl.CostEstimate(
            flops=8 * row_count * width * size * size, bytes_accessed=4 * 2**20, transcendentals=0
        ),
        name="column",
    )(pole_weight, mine, other, ancestor, right, base)

    onward = [(i, (i + 1) % pole_count) for i in range(pole_count)]
    back = [(i, (i - 1) % pole_count) for i in range(pole_count)]
    low, high, both = lax.optimization_barrier((low, high, both))
    from_below = lax.ppermute(low, "pole", onward)
    from_above = lax.ppermute(high, "pole", back)

    both = lax.all_to_all(both, ("pole", "col"), split_axis=0, concat_axis=0, tiled=True)
    spread, rows_out = call(
        sums_body,
        [
            shape(row_count * col_count, piece // 2, 128),
            shape(piece, width, dtype=f32),
        ],
        [both],
        0,
        "sums",
    )
    from_below, from_above, spread = lax.optimization_barrier((from_below, from_above, spread))
    below = lax.ppermute(jnp.concatenate([high, from_below]), "pole", onward)
    above = lax.ppermute(jnp.concatenate([low, from_above]), "pole", back)
    spread = lax.all_to_all(spread, ("row", "col"), split_axis=0, concat_axis=0, tiled=True)
    (pivot_out,) = call(pivot_body, [shape(piece, size, dtype=f32)], [spread], 0, "pivot")

    (update,) = call(
        update_body,
        [shape(row_count, quarters, share, 2 * size, dtype=f32)],
        [pole_shift, panel_h, panel_s, mine, other],
        8 * row_count * width * size * size,
        "update",
    )
    (schur,) = call(
        schur_body,
        [shape(2, row_count, quarters, share, size)],
        [pole_shift, pattern, update, low, high, from_below, from_above, below, above],
        0,
        "schur",
    )
    return (schur.reshape(1, 2, row_count, 1, width, size), rows_out.T, pivot_out.T)


def solution(mesh):
    in_specs = (
        P(("row", "col"), None),
        P(("row", "col"), None),
        P("row", None),
        P("row", None),
        P(),
        P(),
        P("pole", None),
        P("pole", None),
        P(),
        P("pole", None, None, "col", None, "row"),
    )
    out_specs = (
        P("pole", None, None, "col", None, "row"),
        P(("row", "col"), "pole"),
        P(None, "pole"),
    )
    return jax.shard_map(shards, mesh=mesh, in_specs=in_specs, out_specs=out_specs, check_vma=False)
```

```python
import functools

import jax
import jax.numpy as jnp
from jax import lax
from jax.experimental import pallas as pl
from jax.experimental.pallas import tpu as pltpu
from jax.sharding import PartitionSpec as P

bf16 = jnp.bfloat16
f32 = jnp.float32
VMEM = pl.BlockSpec(memory_space=pltpu.VMEM)
SMEM = pl.BlockSpec(memory_space=pltpu.SMEM)


def call(body, outs, ins, flops, name, grant=16):
    moved = sum(x.size * x.dtype.itemsize for x in list(ins) + list(outs))
    return pl.pallas_call(
        body,
        out_shape=outs,
        in_specs=[SMEM if x.size <= 256 else VMEM for x in ins],
        out_specs=[VMEM] * len(outs),
        compiler_params=pltpu.CompilerParams(vmem_limit_bytes=grant * 2**20),
        cost_estimate=pl.CostEstimate(flops=flops, bytes_accessed=moved, transcendentals=0),
        name=name,
    )(*ins)


def shape(*dims, dtype=bf16):
    return jax.ShapeDtypeStruct(dims, dtype)


def dot(left, right):
    return jnp.dot(left, right, preferred_element_type=f32)


def contract(left, right, axis_left, axis_right):
    dims = (((axis_left,), (axis_right,)), ((), ()))
    return lax.dot_general(left, right, dims, preferred_element_type=f32)


def split(value):
    high = value.astype(bf16)
    return high, (value - high.astype(f32)).astype(bf16)


def product(left, right):
    return dot(left[0], right[0]) + (dot(left[0], right[1]) + dot(left[1], right[0]))


def block(wide):
    size = wide.shape[1] // 2
    real, imag = wide[:, :size], wide[:, size:]
    return jnp.concatenate([wide, jnp.concatenate([-imag, real], axis=1)], axis=0)


def both_of(pair, form):
    return form(pair[0]), form(pair[1])


def couple(rows_h, rows_s, shift_real, shift_imag):
    margin = rows_s.astype(f32)
    real = (rows_h.astype(f32) - shift_real * margin).astype(bf16)
    imag = (-shift_imag * margin).astype(bf16)
    return real, imag


def invert_body(shift, pivot_h, pivot_s, inverse):
    size = pivot_h.shape[0]
    shift_real, shift_imag = shift[0, 0], shift[0, 1]
    margin = pivot_s[...].astype(f32)
    real = pivot_h[...].astype(f32) - shift_real * margin
    imag = -shift_imag * margin
    on_diag = lax.broadcasted_iota(jnp.int32, (size, size), 0) == lax.broadcasted_iota(
        jnp.int32, (size, size), 1
    )

    def scales(axis):
        diag_real = jnp.sum(jnp.where(on_diag, real, 0.0), axis=axis, keepdims=True)
        diag_imag = jnp.sum(jnp.where(on_diag, imag, 0.0), axis=axis, keepdims=True)
        denom = diag_real * diag_real + diag_imag * diag_imag
        return diag_real / denom, -diag_imag / denom

    col_real, col_imag = scales(0)
    err_real = jnp.where(on_diag, 0.0, imag * col_imag - real * col_real)
    err_imag = jnp.where(on_diag, 0.0, -(real * col_imag + imag * col_real))
    one = jnp.concatenate([jnp.where(on_diag, 1.0, 0.0), jnp.zeros((size, size), f32)], axis=1)
    err = jnp.concatenate([err_real, err_imag], axis=1)
    err_pair = split(err)
    err2 = product(err_pair, both_of(err_pair, block))
    err2_pair = split(err2)
    square = both_of(err2_pair, block)
    err3 = product(err_pair, square)
    err4_pair = split(product(err2_pair, square))
    first = one + err + err2 + err3
    fourth = both_of(err4_pair, block)
    second = first + product(split(first), fourth)
    err8_pair = split(product(err4_pair, fourth))
    total = second + product(split(second), both_of(err8_pair, block))
    sum_real, sum_imag = total[:, :size], total[:, size:]
    row_real, row_imag = scales(1)
    inv_real = row_real * sum_real - row_imag * sum_imag
    inv_imag = row_real * sum_imag + row_imag * sum_real
    inverse[0], inverse[1] = split(jnp.concatenate([inv_real, inv_imag], axis=1))


def solve(rows_h, rows_s, shift, inverse):
    coupling = jnp.concatenate(couple(rows_h, rows_s, shift[0, 0], shift[0, 1]), axis=1)
    return (dot(coupling, block(inverse[0])) + dot(coupling, block(inverse[1]))).astype(bf16)


def local_body(shift, weight, panel_h, panel_s, inverse, right, base):
    size = panel_h.shape[1]
    solved = solve(panel_h[...], panel_s[...], shift, inverse)
    right[:size] = solved[:, :size]
    right[size:] = solved[:, size:]
    whole = inverse[0].astype(f32) + inverse[1].astype(f32)
    density = weight[0, 0] * whole[:, size:] + weight[0, 1] * whole[:, :size]
    first_device = (lax.axis_index("row") == 0) & (lax.axis_index("col") == 0)
    base[...] = jnp.where(first_device, density.T, 0.0)


def pack_body(panel_h, panel_s, front_h, front_s, out, panels, fronts, sems):
    half = panels.shape[1] // 2
    share, size = fronts.shape[1], out.shape[2]
    shares = panels.shape[1] // share
    at = pl.ds(pl.multiple_of(lax.axis_index("col") * 2 * half, 2 * half), 2 * half)
    of = pl.ds(pl.multiple_of(lax.rem(lax.axis_index("pole"), shares) * share, share), share)
    copies = [
        pltpu.make_async_copy(panel_h.at[at], panels.at[0], sems.at[0]),
        pltpu.make_async_copy(panel_s.at[at], panels.at[1], sems.at[1]),
        pltpu.make_async_copy(front_h.at[of], fronts.at[0], sems.at[2]),
        pltpu.make_async_copy(front_s.at[of], fronts.at[1], sems.at[3]),
    ]
    for copy in copies:
        copy.start()
    for copy in copies:
        copy.wait()
    for row in range(out.shape[0]):
        core = row % 2
        for part in range(2):
            low = part * half
            out[row, low : low + half] = panels[part, core * half : (core + 1) * half]
            low = 2 * half + part * share
            out[row, low : low + share] = fronts[part, :, row * size : (row + 1) * size]


def solve_body(shift, received, inverse, solved, up, down):
    strips, rows, size = received.shape
    half = solved.shape[0] // strips
    rows_h = received[:, :half].reshape(strips * half, size)
    rows_s = received[:, half : 2 * half].reshape(strips * half, size)
    solved[...] = solve(rows_h, rows_s, shift, inverse)
    up[...] = received[: up.shape[0], 2 * half :]
    down[...] = received[strips - down.shape[0] :, 2 * half :]


def ordered(mine, other):
    low = lax.rem(lax.axis_index("row"), 2) == 0
    return jnp.where(low, mine, other), jnp.where(low, other, mine)


def fold(member, out, at):
    pieces = out.shape[0]
    half = out.shape[1] // 2
    cols = 2 * member.shape[1] // 128
    low_lane = lax.broadcasted_iota(jnp.int32, (half, 128), 1) < 64
    for pole in range(pieces // cols):
        for pair in range(cols // 2):
            rows = pole * 2 * half
            top = member[rows : rows + half, pair * 128 : pair * 128 + 128]
            bottom = member[rows + half : rows + 2 * half, pair * 128 : pair * 128 + 128]
            even = jnp.where(low_lane, top, pltpu.roll(bottom, 64, 1))
            odd = jnp.where(low_lane, pltpu.roll(top, 64, 1), bottom)
            poles = pieces // cols
            out[2 * pair * poles + pole, at : at + half] = even.astype(out.dtype)
            out[(2 * pair + 1) * poles + pole, at : at + half] = odd.astype(out.dtype)


def column_body(weight, mine, other, ancestor, right, base, out, far):
    strips, half = ancestor.shape[1], ancestor.shape[2] // 2
    size = ancestor.shape[3]
    wide = mine.shape[1]
    top, bottom = ordered(mine[...], other[...])
    far[:, :half] = top.reshape(strips, half, wide)
    far[:, half:] = bottom.reshape(strips, half, wide)
    rows = far[...].reshape(strips * 2 * half, wide)
    by_real = contract(rows, ancestor[0].reshape(strips * 2 * half, size), 0, 0)
    by_imag = contract(rows, ancestor[1].reshape(strips * 2 * half, size), 0, 0)
    part_real = by_real[:size] - by_imag[size:]
    part_imag = by_real[size:] + by_imag[:size]
    weight_real, weight_imag = weight[0, 0], weight[0, 1]
    density = -(weight_real * part_imag + weight_imag * part_real)
    twin = -(weight_real * part_real - weight_imag * part_imag)
    high, low = split(jnp.concatenate([density, twin], axis=1))
    pivot = base[...] - (dot(high, right[...]) + dot(low, right[...]))
    fold(density, out, 0)
    fold(pivot, out, out.shape[1] // 2)


def sums_body(parts, spread, rows):
    half, width = parts.shape[1] // 2, rows.shape[1]
    total = jnp.sum(parts[...].astype(f32), axis=0)
    rows[:half] = total[:half, :width]
    rows[half:] = total[:half, width:]
    spread[...] = jnp.broadcast_to(total[None, half:].astype(spread.dtype), spread.shape)


def pivot_body(parts, out):
    half = parts.shape[1]
    width = 64
    cols = out.shape[1] // width
    total = jnp.sum(parts[...].astype(f32).reshape(-1, cols, half, 128), axis=0)
    for index in range(128 // width):
        lanes = slice(index * width, (index + 1) * width)
        strips = [total[col][:, lanes] for col in range(cols)]
        out[index * half : (index + 1) * half] = jnp.concatenate(strips, axis=1)


def update_body(shift, panel_h, panel_s, mine, other, out):
    strips, rows = out.shape[0], out.shape[1] * out.shape[2]
    half = mine.shape[0] // strips
    group = 4
    top, bottom = ordered(mine[...], other[...])
    real, imag = couple(panel_h[...], panel_s[...], shift[0, 0], shift[0, 1])
    wide = jnp.concatenate(
        [jnp.concatenate([real, -imag], axis=1), jnp.concatenate([imag, real], axis=1)], axis=0
    )
    for first in range(0, strips, group):
        solved = jnp.concatenate(
            [
                member[strip * half : (strip + 1) * half]
                for strip in range(first, first + group)
                for member in (top, bottom)
            ],
            axis=0,
        )
        update = contract(solved, wide, 1, 1)
        out[first : first + group] = update.reshape((group,) + out.shape[1:])


def relay_body(up, down, from_below, from_above, below, above):
    more = up.shape[0]
    less = more // 3
    half = more - less
    below[:less] = down[half:]
    below[less:] = from_below[:half]
    above[:less] = up[:less]
    above[less:] = from_above[less:]


def schur_tiles(shift, pattern, update, members, buffer, out, sems):
    strips, count, share, size = out.shape[1:]
    pole = lax.axis_index("pole")
    row = lax.axis_index("row")
    shift_real, shift_imag = shift[0, 0], shift[0, 1]
    copies = []
    for member, start, length, step, first in members:
        at = lax.rem(pole + count + step, count)
        for index in range(length):
            strip = first + index
            mask = pattern[strip, row].astype(f32)
            margin = mask * member[start + index, share:].astype(f32)
            real = mask * member[start + index, :share].astype(f32) - shift_real * margin
            buffer[0, strip, at] = (real - update[strip, at, :, :size]).astype(bf16)
            buffer[1, strip, at] = (-shift_imag * margin - update[strip, at, :, size:]).astype(bf16)
        where = (slice(None), pl.ds(first, length), at)
        copies.append(pltpu.make_async_copy(buffer.at[where], out.at[where], sems.at[len(copies)]))
        copies[-1].start()
    for copy in copies:
        copy.wait()


def schur_first_body(shift, pattern, update, up, down, from_below, from_above, out, buffer, sems):
    more, less = up.shape[0], out.shape[1] - up.shape[0]
    members = (
        (up, 0, more, 0, 0),
        (down, more - less, less, 0, more),
        (from_below, 0, more, -1, 0),
        (from_above, 0, more, 1, less),
    )
    schur_tiles(shift, pattern, update, members, buffer, out, sems)


def schur_last_body(shift, pattern, update, below, above, begun, out, buffer, sems):
    del begun
    half = out.shape[1] // 2
    less = below.shape[0] - half
    members = (
        (below, 0, less, -1, 2 * half - less),
        (below, less, half, -2, 0),
        (above, 0, less, 1, 0),
        (above, less, half, 2, half),
    )
    schur_tiles(shift, pattern, update, members, buffer, out, sems)


def shards(
    front_h,
    front_s,
    panel_h,
    panel_s,
    pivot_h,
    pivot_s,
    pole_shift,
    pole_weight,
    pattern,
    ancestor_inverse,
):
    row_count = lax.axis_size("row")
    col_count = lax.axis_size("col")
    pole_count = lax.axis_size("pole")
    col_index = lax.axis_index("col")
    size = pivot_h.shape[0]
    width = size // col_count
    piece = size // pole_count
    half = width // 2
    neighbour = [(i, i ^ 1) for i in range(row_count)]

    quarters = 4
    share = width // quarters

    (sent,) = pl.pallas_call(
        pack_body,
        out_shape=[shape(row_count, width + 2 * share, size)],
        in_specs=[pl.BlockSpec(memory_space=pl.ANY)] * 4,
        out_specs=[VMEM],
        scratch_shapes=[
            pltpu.VMEM((2, width, size), bf16),
            pltpu.VMEM((2, share, row_count * size), bf16),
            pltpu.SemaphoreType.DMA((4,)),
        ],
        cost_estimate=pl.CostEstimate(flops=0, bytes_accessed=2**20, transcendentals=0),
        name="pack",
    )(panel_h, panel_s, front_h, front_s)
    received = lax.all_to_all(sent, "row", split_axis=0, concat_axis=0, tiled=True)

    (inverse,) = call(
        invert_body,
        [shape(2, size, 2 * size)],
        [pole_shift, pivot_h, pivot_s],
        6 * 4 * 3 * 2 * size**3,
        "pivot_inverse",
    )
    less = row_count // 4
    more = row_count - less
    mine, up, down = call(
        solve_body,
        [shape(row_count * half, 2 * size)] + [shape(more, 2 * share, size)] * 2,
        [pole_shift, received, inverse],
        2 * 8 * row_count * half * size * size,
        "solved_rows",
    )
    other = lax.ppermute(mine, "row", neighbour)
    right, base = call(
        local_body,
        [shape(2 * size, size), shape(size, size, dtype=f32)],
        [pole_shift, pole_weight, panel_h, panel_s, inverse],
        2 * 8 * size**3,
        "local_rows",
    )

    ancestor = ancestor_inverse.reshape(2, row_count, width, size)
    (both,) = pl.pallas_call(
        column_body,
        out_shape=[shape(pole_count * col_count, piece, 128)],
        in_specs=[SMEM] + [VMEM] * 5,
        out_specs=[VMEM],
        scratch_shapes=[pltpu.VMEM((row_count, width, 2 * size), bf16)],
        compiler_params=pltpu.CompilerParams(vmem_limit_bytes=16 * 2**20),
        cost_estimate=pl.CostEstimate(
            flops=8 * row_count * width * size * size, bytes_accessed=4 * 2**20, transcendentals=0
        ),
        name="column",
    )(pole_weight, mine, other, ancestor, right, base)

    onward = [(i, (i + 1) % pole_count) for i in range(pole_count)]
    back = [(i, (i - 1) % pole_count) for i in range(pole_count)]
    up, down, both = lax.optimization_barrier((up, down, both))
    from_below = lax.ppermute(up, "pole", onward)
    from_above = lax.ppermute(down, "pole", back)

    both = lax.all_to_all(both, ("col", "pole"), split_axis=0, concat_axis=0, tiled=True)
    spread, rows_out = call(
        sums_body,
        [
            shape(row_count * col_count, piece // 2, 128),
            shape(piece, width, dtype=f32),
        ],
        [both],
        0,
        "sums",
    )
    from_below, from_above, spread = lax.optimization_barrier((from_below, from_above, spread))
    below, above = call(
        relay_body,
        [shape(more, 2 * share, size)] * 2,
        [up, down, from_below, from_above],
        0,
        "relay",
    )
    below = lax.ppermute(below, "pole", onward)
    above = lax.ppermute(above, "pole", back)
    spread = lax.all_to_all(spread, ("row", "col"), split_axis=0, concat_axis=0, tiled=True)
    (pivot_out,) = call(pivot_body, [shape(piece, size, dtype=f32)], [spread], 0, "pivot")

    (update,) = call(
        update_body,
        [shape(row_count, quarters, share, 2 * size, dtype=f32)],
        [pole_shift, panel_h, panel_s, mine, other],
        8 * row_count * width * size * size,
        "update",
    )

    def tiles(body, ins, name, begun=()):
        tile = shape(2, row_count, quarters, share, size)
        return pl.pallas_call(
            body,
            out_shape=tile,
            in_specs=[SMEM] * 2 + [VMEM] * (len(ins) - 2) + [pl.BlockSpec(memory_space=pl.ANY)] * len(begun),
            out_specs=pl.BlockSpec(memory_space=pl.ANY),
            input_output_aliases={len(ins): 0} if begun else {},
            scratch_shapes=[pltpu.VMEM(tile.shape, bf16), pltpu.SemaphoreType.DMA((4,))],
            compiler_params=pltpu.CompilerParams(vmem_limit_bytes=16 * 2**20),
            cost_estimate=pl.CostEstimate(flops=0, bytes_accessed=3 * 2**20, transcendentals=0),
            name=name,
        )(*ins, *begun)

    fixed = [pole_shift, pattern, update]
    schur = tiles(schur_first_body, fixed + [up, down, from_below, from_above], "schur_first")
    schur = tiles(schur_last_body, fixed + [below, above], "schur_last", (schur,))
    return (schur.reshape(1, 2, row_count, 1, width, size), rows_out.T, pivot_out.T)


def solution(mesh):
    in_specs = (
        P(("row", "col"), None),
        P(("row", "col"), None),
        P("row", None),
        P("row", None),
        P(),
        P(),
        P("pole", None),
        P("pole", None),
        P(),
        P("pole", None, None, "col", None, "row"),
    )
    out_specs = (
        P("pole", None, None, "col", None, "row"),
        P(("row", "col"), "pole"),
        P(None, "pole"),
    )
    return jax.shard_map(shards, mesh=mesh, in_specs=in_specs, out_specs=out_specs, check_vma=False)
```

```python
import functools

import jax
import jax.numpy as jnp
from jax import lax
from jax.experimental import pallas as pl
from jax.experimental.pallas import tpu as pltpu
from jax.sharding import PartitionSpec as P

bf16 = jnp.bfloat16
f32 = jnp.float32
VMEM = pl.BlockSpec(memory_space=pltpu.VMEM)
SMEM = pl.BlockSpec(memory_space=pltpu.SMEM)


def call(body, outs, ins, flops, name, grant=16):
    moved = sum(x.size * x.dtype.itemsize for x in list(ins) + list(outs))
    return pl.pallas_call(
        body,
        out_shape=outs,
        in_specs=[SMEM if x.size <= 256 else VMEM for x in ins],
        out_specs=[VMEM] * len(outs),
        compiler_params=pltpu.CompilerParams(vmem_limit_bytes=grant * 2**20),
        cost_estimate=pl.CostEstimate(flops=flops, bytes_accessed=moved, transcendentals=0),
        name=name,
    )(*ins)


def shape(*dims, dtype=bf16):
    return jax.ShapeDtypeStruct(dims, dtype)


def dot(left, right):
    return jnp.dot(left, right, preferred_element_type=f32)


def contract(left, right, axis_left, axis_right):
    dims = (((axis_left,), (axis_right,)), ((), ()))
    return lax.dot_general(left, right, dims, preferred_element_type=f32)


def split(value):
    high = value.astype(bf16)
    return high, (value - high.astype(f32)).astype(bf16)


def product(left, right):
    return dot(left[0], right[0]) + (dot(left[0], right[1]) + dot(left[1], right[0]))


def block(wide):
    size = wide.shape[1] // 2
    real, imag = wide[:, :size], wide[:, size:]
    return jnp.concatenate([wide, jnp.concatenate([-imag, real], axis=1)], axis=0)


def both_of(pair, form):
    return form(pair[0]), form(pair[1])


def couple(rows_h, rows_s, shift_real, shift_imag):
    margin = rows_s.astype(f32)
    real = (rows_h.astype(f32) - shift_real * margin).astype(bf16)
    imag = (-shift_imag * margin).astype(bf16)
    return real, imag


def invert_body(shift, pivot_h, pivot_s, inverse):
    size = pivot_h.shape[0]
    shift_real, shift_imag = shift[0, 0], shift[0, 1]
    margin = pivot_s[...].astype(f32)
    real = pivot_h[...].astype(f32) - shift_real * margin
    imag = -shift_imag * margin
    on_diag = lax.broadcasted_iota(jnp.int32, (size, size), 0) == lax.broadcasted_iota(
        jnp.int32, (size, size), 1
    )

    def scales(axis):
        diag_real = jnp.sum(jnp.where(on_diag, real, 0.0), axis=axis, keepdims=True)
        diag_imag = jnp.sum(jnp.where(on_diag, imag, 0.0), axis=axis, keepdims=True)
        denom = diag_real * diag_real + diag_imag * diag_imag
        return diag_real / denom, -diag_imag / denom

    col_real, col_imag = scales(0)
    err_real = jnp.where(on_diag, 0.0, imag * col_imag - real * col_real)
    err_imag = jnp.where(on_diag, 0.0, -(real * col_imag + imag * col_real))
    one = jnp.concatenate([jnp.where(on_diag, 1.0, 0.0), jnp.zeros((size, size), f32)], axis=1)
    err = jnp.concatenate([err_real, err_imag], axis=1)
    err_pair = split(err)
    err2 = product(err_pair, both_of(err_pair, block))
    err2_pair = split(err2)
    square = both_of(err2_pair, block)
    err3 = product(err_pair, square)
    err4_pair = split(product(err2_pair, square))
    first = one + err + err2 + err3
    fourth = both_of(err4_pair, block)
    second = first + product(split(first), fourth)
    err8_pair = split(product(err4_pair, fourth))
    total = second + product(split(second), both_of(err8_pair, block))
    sum_real, sum_imag = total[:, :size], total[:, size:]
    row_real, row_imag = scales(1)
    inv_real = row_real * sum_real - row_imag * sum_imag
    inv_imag = row_real * sum_imag + row_imag * sum_real
    inverse[0], inverse[1] = split(jnp.concatenate([inv_real, inv_imag], axis=1))


def solve(rows_h, rows_s, shift, inverse):
    coupling = jnp.concatenate(couple(rows_h, rows_s, shift[0, 0], shift[0, 1]), axis=1)
    return (dot(coupling, block(inverse[0])) + dot(coupling, block(inverse[1]))).astype(bf16)


def local_body(shift, weight, panel_h, panel_s, inverse, right, base):
    size = panel_h.shape[1]
    solved = solve(panel_h[...], panel_s[...], shift, inverse)
    right[:size] = solved[:, :size]
    right[size:] = solved[:, size:]
    whole = inverse[0].astype(f32) + inverse[1].astype(f32)
    density = weight[0, 0] * whole[:, size:] + weight[0, 1] * whole[:, :size]
    first_device = (lax.axis_index("row") == 0) & (lax.axis_index("col") == 0)
    base[...] = jnp.where(first_device, density.T, 0.0)


def pack_body(panel_h, panel_s, front_h, front_s, out, panels, fronts, buffer, sems):
    half = panels.shape[1] // 2
    share, size = fronts.shape[1], out.shape[2]
    shares = panels.shape[1] // share
    at = pl.ds(pl.multiple_of(lax.axis_index("col") * 2 * half, 2 * half), 2 * half)
    of = pl.ds(pl.multiple_of(lax.rem(lax.axis_index("pole"), shares) * share, share), share)
    loads = [
        pltpu.make_async_copy(panel_h.at[at], panels.at[0], sems.at[0]),
        pltpu.make_async_copy(panel_s.at[at], panels.at[1], sems.at[1]),
        pltpu.make_async_copy(front_h.at[of], fronts.at[0], sems.at[2]),
        pltpu.make_async_copy(front_s.at[of], fronts.at[1], sems.at[3]),
    ]
    panel_rows, front_rows = pl.ds(0, 2 * half), pl.ds(2 * half, 2 * share)
    stores = [
        pltpu.make_async_copy(buffer.at[:, rows], out.at[:, rows], sems.at[4 + index])
        for index, rows in enumerate((panel_rows, front_rows))
    ]
    for load in loads:
        load.start()
    loads[0].wait()
    loads[1].wait()
    for row in range(out.shape[0]):
        core = row % 2
        for part in range(2):
            low = part * half
            buffer[row, low : low + half] = panels[part, core * half : (core + 1) * half]
    stores[0].start()
    loads[2].wait()
    loads[3].wait()
    for row in range(out.shape[0]):
        for part in range(2):
            low = 2 * half + part * share
            buffer[row, low : low + share] = fronts[part, :, row * size : (row + 1) * size]
    stores[1].start()
    for store in stores:
        store.wait()


def solve_body(shift, received, inverse, solved, up, down):
    strips, rows, size = received.shape
    half = solved.shape[0] // strips
    rows_h = received[:, :half].reshape(strips * half, size)
    rows_s = received[:, half : 2 * half].reshape(strips * half, size)
    solved[...] = solve(rows_h, rows_s, shift, inverse)
    up[...] = received[: up.shape[0], 2 * half :]
    down[...] = received[strips - down.shape[0] :, 2 * half :]


def ordered(mine, other):
    low = lax.rem(lax.axis_index("row"), 2) == 0
    return jnp.where(low, mine, other), jnp.where(low, other, mine)


def fold(member, out, at):
    pieces = out.shape[0]
    half = out.shape[1] // 2
    cols = 2 * member.shape[1] // 128
    low_lane = lax.broadcasted_iota(jnp.int32, (half, 128), 1) < 64
    for pole in range(pieces // cols):
        for pair in range(cols // 2):
            rows = pole * 2 * half
            top = member[rows : rows + half, pair * 128 : pair * 128 + 128]
            bottom = member[rows + half : rows + 2 * half, pair * 128 : pair * 128 + 128]
            even = jnp.where(low_lane, top, pltpu.roll(bottom, 64, 1))
            odd = jnp.where(low_lane, pltpu.roll(top, 64, 1), bottom)
            poles = pieces // cols
            out[2 * pair * poles + pole, at : at + half] = even.astype(out.dtype)
            out[(2 * pair + 1) * poles + pole, at : at + half] = odd.astype(out.dtype)


def half_column(solved, ancestor, core):
    strips, half, size = ancestor.shape[1], ancestor.shape[2] // 2, ancestor.shape[3]
    at = pl.ds(pl.multiple_of(core * half, half), half)
    rows = solved[...]
    by_real = contract(rows, ancestor[0, :, at, :].reshape(strips * half, size), 0, 0)
    by_imag = contract(rows, ancestor[1, :, at, :].reshape(strips * half, size), 0, 0)
    return by_real[:size] - by_imag[size:], by_real[size:] + by_imag[:size]


def own_column_body(mine, ancestor, part):
    size = part.shape[1]
    part[:size], part[size:] = half_column(mine, ancestor, lax.rem(lax.axis_index("row"), 2))


def column_body(weight, other, ancestor, part, right, base, out, buffer, sems):
    size = part.shape[1]
    half = out.shape[1] // 2
    part_real, part_imag = half_column(other, ancestor, 1 - lax.rem(lax.axis_index("row"), 2))
    part_real += part[:size]
    part_imag += part[size:]
    stores = [
        pltpu.make_async_copy(buffer.at[:, rows], out.at[:, rows], sems.at[index])
        for index, rows in enumerate((pl.ds(0, half), pl.ds(half, half)))
    ]
    weight_real, weight_imag = weight[0, 0], weight[0, 1]
    density = -(weight_real * part_imag + weight_imag * part_real)
    fold(density, buffer, 0)
    stores[0].start()
    twin = -(weight_real * part_real - weight_imag * part_imag)
    high, low = split(jnp.concatenate([density, twin], axis=1))
    pivot = base[...] - (dot(high, right[...]) + dot(low, right[...]))
    fold(pivot, buffer, half)
    stores[1].start()
    for store in stores:
        store.wait()


def sums_body(parts, spread, rows):
    half, width = parts.shape[1] // 2, rows.shape[1]
    total = jnp.sum(parts[...].astype(f32), axis=0)
    rows[:half] = total[:half, :width]
    rows[half:] = total[:half, width:]
    spread[...] = jnp.broadcast_to(total[None, half:].astype(spread.dtype), spread.shape)


def pivot_body(parts, out):
    half = parts.shape[1]
    width = 64
    cols = out.shape[1] // width
    total = jnp.sum(parts[...].astype(f32).reshape(-1, cols, half, 128), axis=0)
    for index in range(128 // width):
        lanes = slice(index * width, (index + 1) * width)
        strips = [total[col][:, lanes] for col in range(cols)]
        out[index * half : (index + 1) * half] = jnp.concatenate(strips, axis=1)


def update_body(shift, panel_h, panel_s, mine, other, out):
    strips, rows = out.shape[0], out.shape[1] * out.shape[2]
    half = mine.shape[0] // strips
    group = 4
    top, bottom = ordered(mine[...], other[...])
    real, imag = couple(panel_h[...], panel_s[...], shift[0, 0], shift[0, 1])
    wide = jnp.concatenate(
        [jnp.concatenate([real, -imag], axis=1), jnp.concatenate([imag, real], axis=1)], axis=0
    )
    for first in range(0, strips, group):
        solved = jnp.concatenate(
            [
                member[strip * half : (strip + 1) * half]
                for strip in range(first, first + group)
                for member in (top, bottom)
            ],
            axis=0,
        )
        update = contract(solved, wide, 1, 1)
        out[first : first + group] = update.reshape((group,) + out.shape[1:])


def relay_body(up, down, from_below, from_above, below, above):
    more = up.shape[0]
    less = more // 3
    half = more - less
    below[:less] = down[half:]
    below[less:] = from_below[:half]
    above[:less] = up[:less]
    above[less:] = from_above[less:]


def schur_tiles(shift, pattern, update, members, buffer, out, sems):
    strips, count, share, size = out.shape[1:]
    pole = lax.axis_index("pole")
    row = lax.axis_index("row")
    shift_real, shift_imag = shift[0, 0], shift[0, 1]
    copies = []
    for member, start, length, step, first in members:
        at = lax.rem(pole + count + step, count)
        for index in range(length):
            strip = first + index
            mask = pattern[strip, row].astype(f32)
            margin = mask * member[start + index, share:].astype(f32)
            real = mask * member[start + index, :share].astype(f32) - shift_real * margin
            buffer[0, strip, at] = (real - update[strip, at, :, :size]).astype(bf16)
            buffer[1, strip, at] = (-shift_imag * margin - update[strip, at, :, size:]).astype(bf16)
        where = (slice(None), pl.ds(first, length), at)
        copies.append(pltpu.make_async_copy(buffer.at[where], out.at[where], sems.at[len(copies)]))
        copies[-1].start()
    for copy in copies:
        copy.wait()


def schur_first_body(shift, pattern, update, up, down, from_below, from_above, out, buffer, sems):
    more, less = up.shape[0], out.shape[1] - up.shape[0]
    members = (
        (up, 0, more, 0, 0),
        (down, more - less, less, 0, more),
        (from_below, 0, more, -1, 0),
        (from_above, 0, more, 1, less),
    )
    schur_tiles(shift, pattern, update, members, buffer, out, sems)


def schur_last_body(shift, pattern, update, below, above, begun, out, buffer, sems):
    del begun
    half = out.shape[1] // 2
    less = below.shape[0] - half
    members = (
        (below, 0, less, -1, 2 * half - less),
        (below, less, half, -2, 0),
        (above, 0, less, 1, 0),
        (above, less, half, 2, half),
    )
    schur_tiles(shift, pattern, update, members, buffer, out, sems)


def shards(
    front_h,
    front_s,
    panel_h,
    panel_s,
    pivot_h,
    pivot_s,
    pole_shift,
    pole_weight,
    pattern,
    ancestor_inverse,
):
    row_count = lax.axis_size("row")
    col_count = lax.axis_size("col")
    pole_count = lax.axis_size("pole")
    col_index = lax.axis_index("col")
    size = pivot_h.shape[0]
    width = size // col_count
    piece = size // pole_count
    half = width // 2
    neighbour = [(i, i ^ 1) for i in range(row_count)]

    quarters = 4
    share = width // quarters

    (sent,) = pl.pallas_call(
        pack_body,
        out_shape=[shape(row_count, width + 2 * share, size)],
        in_specs=[pl.BlockSpec(memory_space=pl.ANY)] * 4,
        out_specs=[pl.BlockSpec(memory_space=pl.ANY)],
        scratch_shapes=[
            pltpu.VMEM((2, width, size), bf16),
            pltpu.VMEM((2, share, row_count * size), bf16),
            pltpu.VMEM((row_count, width + 2 * share, size), bf16),
            pltpu.SemaphoreType.DMA((6,)),
        ],
        cost_estimate=pl.CostEstimate(flops=0, bytes_accessed=2**20, transcendentals=0),
        name="pack",
    )(panel_h, panel_s, front_h, front_s)
    received = lax.all_to_all(sent, "row", split_axis=0, concat_axis=0, tiled=True)

    (inverse,) = call(
        invert_body,
        [shape(2, size, 2 * size)],
        [pole_shift, pivot_h, pivot_s],
        6 * 4 * 3 * 2 * size**3,
        "pivot_inverse",
    )
    right, base = call(
        local_body,
        [shape(2 * size, size), shape(size, size, dtype=f32)],
        [pole_shift, pole_weight, panel_h, panel_s, inverse],
        2 * 8 * size**3,
        "local_rows",
    )
    inverse, right, base = lax.optimization_barrier((inverse, right, base))
    less = row_count // 4
    more = row_count - less
    mine, up, down = call(
        solve_body,
        [shape(row_count * half, 2 * size)] + [shape(more, 2 * share, size)] * 2,
        [pole_shift, received, inverse],
        2 * 8 * row_count * half * size * size,
        "solved_rows",
    )
    other = lax.ppermute(mine, "row", neighbour)
    ancestor = ancestor_inverse.reshape(2, row_count, width, size)
    (part,) = call(
        own_column_body,
        [shape(2 * size, size, dtype=f32)],
        [mine, ancestor],
        4 * row_count * width * size * size,
        "own_column",
    )
    folded = (col_count * pole_count, piece, 128)
    (both,) = pl.pallas_call(
        column_body,
        out_shape=[shape(*folded)],
        in_specs=[SMEM] + [VMEM] * 5,
        out_specs=[pl.BlockSpec(memory_space=pl.ANY)],
        scratch_shapes=[pltpu.VMEM(folded, bf16), pltpu.SemaphoreType.DMA((2,))],
        compiler_params=pltpu.CompilerParams(vmem_limit_bytes=16 * 2**20),
        cost_estimate=pl.CostEstimate(
            flops=4 * row_count * width * size * size, bytes_accessed=2 * 2**20, transcendentals=0
        ),
        name="column",
    )(pole_weight, other, ancestor, part, right, base)

    onward = [(i, (i + 1) % pole_count) for i in range(pole_count)]
    back = [(i, (i - 1) % pole_count) for i in range(pole_count)]
    up, down, both = lax.optimization_barrier((up, down, both))
    from_below = lax.ppermute(up, "pole", onward)
    from_above = lax.ppermute(down, "pole", back)

    both = lax.all_to_all(both, ("col", "pole"), split_axis=0, concat_axis=0, tiled=True)
    spread, rows_out = call(
        sums_body,
        [
            shape(row_count * col_count, piece // 2, 128),
            shape(piece, width, dtype=f32),
        ],
        [both],
        0,
        "sums",
    )
    from_below, from_above, spread = lax.optimization_barrier((from_below, from_above, spread))
    below, above = call(
        relay_body,
        [shape(more, 2 * share, size)] * 2,
        [up, down, from_below, from_above],
        0,
        "relay",
    )
    below = lax.ppermute(below, "pole", onward)
    above = lax.ppermute(above, "pole", back)
    spread = lax.all_to_all(spread, ("row", "col"), split_axis=0, concat_axis=0, tiled=True)
    (pivot_out,) = call(pivot_body, [shape(piece, size, dtype=f32)], [spread], 0, "pivot")

    (update,) = call(
        update_body,
        [shape(row_count, quarters, share, 2 * size, dtype=f32)],
        [pole_shift, panel_h, panel_s, mine, other],
        8 * row_count * width * size * size,
        "update",
    )

    def tiles(body, ins, name, begun=()):
        tile = shape(2, row_count, quarters, share, size)
        return pl.pallas_call(
            body,
            out_shape=tile,
            in_specs=[SMEM] * 2 + [VMEM] * (len(ins) - 2) + [pl.BlockSpec(memory_space=pl.ANY)] * len(begun),
            out_specs=pl.BlockSpec(memory_space=pl.ANY),
            input_output_aliases={len(ins): 0} if begun else {},
            scratch_shapes=[pltpu.VMEM(tile.shape, bf16), pltpu.SemaphoreType.DMA((4,))],
            compiler_params=pltpu.CompilerParams(vmem_limit_bytes=16 * 2**20),
            cost_estimate=pl.CostEstimate(flops=0, bytes_accessed=3 * 2**20, transcendentals=0),
            name=name,
        )(*ins, *begun)

    fixed = [pole_shift, pattern, update]
    schur = tiles(schur_first_body, fixed + [up, down, from_below, from_above], "schur_first")
    schur = tiles(schur_last_body, fixed + [below, above], "schur_last", (schur,))
    return (schur.reshape(1, 2, row_count, 1, width, size), rows_out.T, pivot_out.T)


def solution(mesh):
    in_specs = (
        P(("row", "col"), None),
        P(("row", "col"), None),
        P("row", None),
        P("row", None),
        P(),
        P(),
        P("pole", None),
        P("pole", None),
        P(),
        P("pole", None, None, "col", None, "row"),
    )
    out_specs = (
        P("pole", None, None, "col", None, "row"),
        P(("row", "col"), "pole"),
        P(None, "pole"),
    )
    return jax.shard_map(shards, mesh=mesh, in_specs=in_specs, out_specs=out_specs, check_vma=False)
```

```python
import functools

import jax
import jax.numpy as jnp
from jax import lax
from jax.experimental import pallas as pl
from jax.experimental.pallas import tpu as pltpu
from jax.sharding import PartitionSpec as P

bf16 = jnp.bfloat16
f32 = jnp.float32
VMEM = pl.BlockSpec(memory_space=pltpu.VMEM)
SMEM = pl.BlockSpec(memory_space=pltpu.SMEM)


def call(body, outs, ins, flops, name, grant=16):
    moved = sum(x.size * x.dtype.itemsize for x in list(ins) + list(outs))
    return pl.pallas_call(
        body,
        out_shape=outs,
        in_specs=[SMEM if x.size <= 256 else VMEM for x in ins],
        out_specs=[VMEM] * len(outs),
        compiler_params=pltpu.CompilerParams(vmem_limit_bytes=grant * 2**20),
        cost_estimate=pl.CostEstimate(flops=flops, bytes_accessed=moved, transcendentals=0),
        name=name,
    )(*ins)


def shape(*dims, dtype=bf16):
    return jax.ShapeDtypeStruct(dims, dtype)


def dot(left, right):
    return jnp.dot(left, right, preferred_element_type=f32)


def contract(left, right, axis_left, axis_right):
    dims = (((axis_left,), (axis_right,)), ((), ()))
    return lax.dot_general(left, right, dims, preferred_element_type=f32)


def split(value):
    high = value.astype(bf16)
    return high, (value - high.astype(f32)).astype(bf16)


def product(left, right):
    return dot(left[0], right[0]) + (dot(left[0], right[1]) + dot(left[1], right[0]))


def block(wide):
    size = wide.shape[1] // 2
    real, imag = wide[:, :size], wide[:, size:]
    return jnp.concatenate([wide, jnp.concatenate([-imag, real], axis=1)], axis=0)


def both_of(pair, form):
    return form(pair[0]), form(pair[1])


def couple(rows_h, rows_s, shift_real, shift_imag):
    margin = rows_s.astype(f32)
    real = (rows_h.astype(f32) - shift_real * margin).astype(bf16)
    imag = (-shift_imag * margin).astype(bf16)
    return real, imag


def invert_body(shift, pivot_h, pivot_s, inverse):
    size = pivot_h.shape[0]
    shift_real, shift_imag = shift[0, 0], shift[0, 1]
    margin = pivot_s[...].astype(f32)
    real = pivot_h[...].astype(f32) - shift_real * margin
    imag = -shift_imag * margin
    on_diag = lax.broadcasted_iota(jnp.int32, (size, size), 0) == lax.broadcasted_iota(
        jnp.int32, (size, size), 1
    )

    def scales(axis):
        diag_real = jnp.sum(jnp.where(on_diag, real, 0.0), axis=axis, keepdims=True)
        diag_imag = jnp.sum(jnp.where(on_diag, imag, 0.0), axis=axis, keepdims=True)
        denom = diag_real * diag_real + diag_imag * diag_imag
        return diag_real / denom, -diag_imag / denom

    col_real, col_imag = scales(0)
    err_real = jnp.where(on_diag, 0.0, imag * col_imag - real * col_real)
    err_imag = jnp.where(on_diag, 0.0, -(real * col_imag + imag * col_real))
    one = jnp.concatenate([jnp.where(on_diag, 1.0, 0.0), jnp.zeros((size, size), f32)], axis=1)
    err = jnp.concatenate([err_real, err_imag], axis=1)
    err_pair = split(err)
    err2 = product(err_pair, both_of(err_pair, block))
    err2_pair = split(err2)
    square = both_of(err2_pair, block)
    err3 = product(err_pair, square)
    err4_pair = split(product(err2_pair, square))
    first = one + err + err2 + err3
    fourth = both_of(err4_pair, block)
    second = first + product(split(first), fourth)
    err8_pair = split(product(err4_pair, fourth))
    total = second + product(split(second), both_of(err8_pair, block))
    sum_real, sum_imag = total[:, :size], total[:, size:]
    row_real, row_imag = scales(1)
    inv_real = row_real * sum_real - row_imag * sum_imag
    inv_imag = row_real * sum_imag + row_imag * sum_real
    inverse[0], inverse[1] = split(jnp.concatenate([inv_real, inv_imag], axis=1))


def solve(rows_h, rows_s, shift, inverse):
    coupling = jnp.concatenate(couple(rows_h, rows_s, shift[0, 0], shift[0, 1]), axis=1)
    return (dot(coupling, block(inverse[0])) + dot(coupling, block(inverse[1]))).astype(bf16)


def local_body(shift, weight, panel_h, panel_s, inverse, right, base):
    size = panel_h.shape[1]
    solved = solve(panel_h[...], panel_s[...], shift, inverse)
    right[:size] = solved[:, :size]
    right[size:] = solved[:, size:]
    whole = inverse[0].astype(f32) + inverse[1].astype(f32)
    density = weight[0, 0] * whole[:, size:] + weight[0, 1] * whole[:, :size]
    first_device = (lax.axis_index("row") == 0) & (lax.axis_index("col") == 0)
    base[...] = jnp.where(first_device, density.T, 0.0)


def pack_body(panel_h, panel_s, front_h, front_s, out, panels, fronts, buffer, sems):
    half = panels.shape[1] // 2
    share, size = fronts.shape[1], out.shape[2]
    shares = panels.shape[1] // share
    at = pl.ds(pl.multiple_of(lax.axis_index("col") * 2 * half, 2 * half), 2 * half)
    of = pl.ds(pl.multiple_of(lax.rem(lax.axis_index("pole"), shares) * share, share), share)
    loads = [
        pltpu.make_async_copy(panel_h.at[at], panels.at[0], sems.at[0]),
        pltpu.make_async_copy(panel_s.at[at], panels.at[1], sems.at[1]),
        pltpu.make_async_copy(front_h.at[of], fronts.at[0], sems.at[2]),
        pltpu.make_async_copy(front_s.at[of], fronts.at[1], sems.at[3]),
    ]
    panel_rows, front_rows = pl.ds(0, 2 * half), pl.ds(2 * half, 2 * share)
    stores = [
        pltpu.make_async_copy(buffer.at[:, rows], out.at[:, rows], sems.at[4 + index])
        for index, rows in enumerate((panel_rows, front_rows))
    ]
    for load in loads:
        load.start()
    loads[0].wait()
    loads[1].wait()
    for row in range(out.shape[0]):
        core = row % 2
        for part in range(2):
            low = part * half
            buffer[row, low : low + half] = panels[part, core * half : (core + 1) * half]
    stores[0].start()
    loads[2].wait()
    loads[3].wait()
    for row in range(out.shape[0]):
        for part in range(2):
            low = 2 * half + part * share
            buffer[row, low : low + share] = fronts[part, :, row * size : (row + 1) * size]
    stores[1].start()
    for store in stores:
        store.wait()


def solve_body(shift, received, inverse, solved, up, down):
    strips, rows, size = received.shape
    half = solved.shape[0] // strips
    rows_h = received[:, :half].reshape(strips * half, size)
    rows_s = received[:, half : 2 * half].reshape(strips * half, size)
    solved[...] = solve(rows_h, rows_s, shift, inverse)
    up[...] = received[: up.shape[0], 2 * half :]
    down[...] = received[strips - down.shape[0] :, 2 * half :]


def ordered(mine, other):
    low = lax.rem(lax.axis_index("row"), 2) == 0
    return jnp.where(low, mine, other), jnp.where(low, other, mine)


def fold(member, out, at):
    pieces = out.shape[0]
    half = out.shape[1] // 2
    cols = 2 * member.shape[1] // 128
    low_lane = lax.broadcasted_iota(jnp.int32, (half, 128), 1) < 64
    for pole in range(pieces // cols):
        for pair in range(cols // 2):
            rows = pole * 2 * half
            top = member[rows : rows + half, pair * 128 : pair * 128 + 128]
            bottom = member[rows + half : rows + 2 * half, pair * 128 : pair * 128 + 128]
            even = jnp.where(low_lane, top, pltpu.roll(bottom, 64, 1))
            odd = jnp.where(low_lane, pltpu.roll(top, 64, 1), bottom)
            poles = pieces // cols
            out[2 * pair * poles + pole, at : at + half] = even.astype(out.dtype)
            out[(2 * pair + 1) * poles + pole, at : at + half] = odd.astype(out.dtype)


def half_column(solved, ancestor, core):
    strips, half, size = ancestor.shape[1], ancestor.shape[2] // 2, ancestor.shape[3]
    at = pl.ds(pl.multiple_of(core * half, half), half)
    rows = solved[...]
    by_real = contract(rows, ancestor[0, :, at, :].reshape(strips * half, size), 0, 0)
    by_imag = contract(rows, ancestor[1, :, at, :].reshape(strips * half, size), 0, 0)
    return by_real[:size] - by_imag[size:], by_real[size:] + by_imag[:size]


def own_column_body(mine, ancestor, part):
    size = part.shape[1]
    part[:size], part[size:] = half_column(mine, ancestor, lax.rem(lax.axis_index("row"), 2))


def column_body(weight, other, ancestor, part, right, base, out, buffer, sems):
    size = part.shape[1]
    half = out.shape[1] // 2
    part_real, part_imag = half_column(other, ancestor, 1 - lax.rem(lax.axis_index("row"), 2))
    part_real += part[:size]
    part_imag += part[size:]
    stores = [
        pltpu.make_async_copy(buffer.at[:, rows], out.at[:, rows], sems.at[index])
        for index, rows in enumerate((pl.ds(0, half), pl.ds(half, half)))
    ]
    weight_real, weight_imag = weight[0, 0], weight[0, 1]
    density = -(weight_real * part_imag + weight_imag * part_real)
    fold(density, buffer, 0)
    stores[0].start()
    twin = -(weight_real * part_real - weight_imag * part_imag)
    high, low = split(jnp.concatenate([density, twin], axis=1))
    pivot = base[...] - (dot(high, right[...]) + dot(low, right[...]))
    fold(pivot, buffer, half)
    stores[1].start()
    for store in stores:
        store.wait()


def sums_body(parts, spread, rows):
    half, width = parts.shape[1] // 2, rows.shape[1]
    total = jnp.sum(parts[...].astype(f32), axis=0)
    rows[:half] = total[:half, :width]
    rows[half:] = total[:half, width:]
    spread[...] = jnp.broadcast_to(total[None, half:].astype(spread.dtype), spread.shape)


def pivot_body(parts, out):
    half = parts.shape[1]
    width = 64
    cols = out.shape[1] // width
    total = jnp.sum(parts[...].astype(f32).reshape(-1, cols, half, 128), axis=0)
    for index in range(128 // width):
        lanes = slice(index * width, (index + 1) * width)
        strips = [total[col][:, lanes] for col in range(cols)]
        out[index * half : (index + 1) * half] = jnp.concatenate(strips, axis=1)


def update_body(shift, panel_h, panel_s, mine, other, out):
    strips, rows = out.shape[0], out.shape[1] * out.shape[2]
    half = mine.shape[0] // strips
    group = 4
    top, bottom = ordered(mine[...], other[...])
    real, imag = couple(panel_h[...], panel_s[...], shift[0, 0], shift[0, 1])
    wide = jnp.concatenate(
        [jnp.concatenate([real, -imag], axis=1), jnp.concatenate([imag, real], axis=1)], axis=0
    )
    for first in range(0, strips, group):
        solved = jnp.concatenate(
            [
                member[strip * half : (strip + 1) * half]
                for strip in range(first, first + group)
                for member in (top, bottom)
            ],
            axis=0,
        )
        update = contract(solved, wide, 1, 1)
        out[first : first + group] = update.reshape((group,) + out.shape[1:])


def relay_body(up, down, from_below, from_above, below, above):
    more = up.shape[0]
    less = more // 3
    half = more - less
    below[:less] = down[half:]
    below[less:] = from_below[:half]
    above[:less] = up[:less]
    above[less:] = from_above[less:]


def schur_tiles(shift, pattern, update, members, buffer, out, sems):
    strips, count, share, size = out.shape[1:]
    pole = lax.axis_index("pole")
    row = lax.axis_index("row")
    shift_real, shift_imag = shift[0, 0], shift[0, 1]
    copies = []
    for member, start, length, step, first in members:
        at = lax.rem(pole + count + step, count)
        for index in range(length):
            strip = first + index
            mask = pattern[strip, row].astype(f32)
            margin = mask * member[start + index, share:].astype(f32)
            real = mask * member[start + index, :share].astype(f32) - shift_real * margin
            buffer[0, strip, at] = (real - update[strip, at, :, :size]).astype(bf16)
            buffer[1, strip, at] = (-shift_imag * margin - update[strip, at, :, size:]).astype(bf16)
        where = (slice(None), pl.ds(first, length), at)
        copies.append(pltpu.make_async_copy(buffer.at[where], out.at[where], sems.at[len(copies)]))
        copies[-1].start()
    for copy in copies:
        copy.wait()


def schur_first_body(shift, pattern, update, up, down, from_below, from_above, out, buffer, sems):
    more, less = up.shape[0], out.shape[1] - up.shape[0]
    members = (
        (up, 0, more, 0, 0),
        (down, more - less, less, 0, more),
        (from_below, 0, more, -1, 0),
        (from_above, 0, more, 1, less),
    )
    schur_tiles(shift, pattern, update, members, buffer, out, sems)


def schur_below_body(shift, pattern, update, below, begun, out, buffer, sems):
    del begun
    half = out.shape[1] // 2
    less = below.shape[0] - half
    members = ((below, 0, less, -1, 2 * half - less), (below, less, half, -2, 0))
    schur_tiles(shift, pattern, update, members, buffer, out, sems)


def schur_above_body(shift, pattern, update, above, begun, out, buffer, sems):
    del begun
    half = out.shape[1] // 2
    less = above.shape[0] - half
    members = ((above, 0, less, 1, 0), (above, less, half, 2, half))
    schur_tiles(shift, pattern, update, members, buffer, out, sems)


def shards(
    front_h,
    front_s,
    panel_h,
    panel_s,
    pivot_h,
    pivot_s,
    pole_shift,
    pole_weight,
    pattern,
    ancestor_inverse,
):
    row_count = lax.axis_size("row")
    col_count = lax.axis_size("col")
    pole_count = lax.axis_size("pole")
    col_index = lax.axis_index("col")
    size = pivot_h.shape[0]
    width = size // col_count
    piece = size // pole_count
    half = width // 2
    neighbour = [(i, i ^ 1) for i in range(row_count)]

    quarters = 4
    share = width // quarters

    (sent,) = pl.pallas_call(
        pack_body,
        out_shape=[shape(row_count, width + 2 * share, size)],
        in_specs=[pl.BlockSpec(memory_space=pl.ANY)] * 4,
        out_specs=[pl.BlockSpec(memory_space=pl.ANY)],
        scratch_shapes=[
            pltpu.VMEM((2, width, size), bf16),
            pltpu.VMEM((2, share, row_count * size), bf16),
            pltpu.VMEM((row_count, width + 2 * share, size), bf16),
            pltpu.SemaphoreType.DMA((6,)),
        ],
        cost_estimate=pl.CostEstimate(flops=0, bytes_accessed=2**20, transcendentals=0),
        name="pack",
    )(panel_h, panel_s, front_h, front_s)
    received = lax.all_to_all(sent, "row", split_axis=0, concat_axis=0, tiled=True)

    (inverse,) = call(
        invert_body,
        [shape(2, size, 2 * size)],
        [pole_shift, pivot_h, pivot_s],
        6 * 4 * 3 * 2 * size**3,
        "pivot_inverse",
    )
    right, base = call(
        local_body,
        [shape(2 * size, size), shape(size, size, dtype=f32)],
        [pole_shift, pole_weight, panel_h, panel_s, inverse],
        2 * 8 * size**3,
        "local_rows",
    )
    inverse, right, base = lax.optimization_barrier((inverse, right, base))
    less = row_count // 4
    more = row_count - less
    mine, up, down = call(
        solve_body,
        [shape(row_count * half, 2 * size)] + [shape(more, 2 * share, size)] * 2,
        [pole_shift, received, inverse],
        2 * 8 * row_count * half * size * size,
        "solved_rows",
    )
    other = lax.ppermute(mine, "row", neighbour)
    ancestor = ancestor_inverse.reshape(2, row_count, width, size)
    (part,) = call(
        own_column_body,
        [shape(2 * size, size, dtype=f32)],
        [mine, ancestor],
        4 * row_count * width * size * size,
        "own_column",
    )
    folded = (col_count * pole_count, piece, 128)
    (both,) = pl.pallas_call(
        column_body,
        out_shape=[shape(*folded)],
        in_specs=[SMEM] + [VMEM] * 5,
        out_specs=[pl.BlockSpec(memory_space=pl.ANY)],
        scratch_shapes=[pltpu.VMEM(folded, bf16), pltpu.SemaphoreType.DMA((2,))],
        compiler_params=pltpu.CompilerParams(vmem_limit_bytes=16 * 2**20),
        cost_estimate=pl.CostEstimate(
            flops=4 * row_count * width * size * size, bytes_accessed=2 * 2**20, transcendentals=0
        ),
        name="column",
    )(pole_weight, other, ancestor, part, right, base)

    onward = [(i, (i + 1) % pole_count) for i in range(pole_count)]
    back = [(i, (i - 1) % pole_count) for i in range(pole_count)]
    up, down, both = lax.optimization_barrier((up, down, both))
    from_below = lax.ppermute(up, "pole", onward)
    from_above = lax.ppermute(down, "pole", back)

    both = lax.all_to_all(both, ("col", "pole"), split_axis=0, concat_axis=0, tiled=True)
    spread, rows_out = call(
        sums_body,
        [
            shape(row_count * col_count, piece // 2, 128),
            shape(piece, width, dtype=f32),
        ],
        [both],
        0,
        "sums",
    )
    below, above = call(
        relay_body,
        [shape(more, 2 * share, size)] * 2,
        [up, down, from_below, from_above],
        10**11,
        "relay",
    )
    below = lax.ppermute(below, "pole", onward)
    above = lax.ppermute(above, "pole", back)
    spread = lax.all_to_all(spread, ("row", "col"), split_axis=0, concat_axis=0, tiled=True)
    (pivot_out,) = call(pivot_body, [shape(piece, size, dtype=f32)], [spread], 0, "pivot")

    (update,) = call(
        update_body,
        [shape(row_count, quarters, share, 2 * size, dtype=f32)],
        [pole_shift, panel_h, panel_s, mine, other],
        8 * row_count * width * size * size,
        "update",
    )

    def tiles(body, ins, name, begun=()):
        tile = shape(2, row_count, quarters, share, size)
        return pl.pallas_call(
            body,
            out_shape=tile,
            in_specs=[SMEM] * 2 + [VMEM] * (len(ins) - 2) + [pl.BlockSpec(memory_space=pl.ANY)] * len(begun),
            out_specs=pl.BlockSpec(memory_space=pl.ANY),
            input_output_aliases={len(ins): 0} if begun else {},
            scratch_shapes=[pltpu.VMEM(tile.shape, bf16), pltpu.SemaphoreType.DMA((4,))],
            compiler_params=pltpu.CompilerParams(vmem_limit_bytes=16 * 2**20),
            cost_estimate=pl.CostEstimate(flops=0, bytes_accessed=3 * 2**20, transcendentals=0),
            name=name,
        )(*ins, *begun)

    fixed = [pole_shift, pattern, update]
    schur = tiles(schur_first_body, fixed + [up, down, from_below, from_above], "schur_first")
    schur = tiles(schur_below_body, fixed + [below], "schur_below", (schur,))
    schur = tiles(schur_above_body, fixed + [above], "schur_above", (schur,))
    return (schur.reshape(1, 2, row_count, 1, width, size), rows_out.T, pivot_out.T)


def solution(mesh):
    in_specs = (
        P(("row", "col"), None),
        P(("row", "col"), None),
        P("row", None),
        P("row", None),
        P(),
        P(),
        P("pole", None),
        P("pole", None),
        P(),
        P("pole", None, None, "col", None, "row"),
    )
    out_specs = (
        P("pole", None, None, "col", None, "row"),
        P(("row", "col"), "pole"),
        P(None, "pole"),
    )
    return jax.shard_map(shards, mesh=mesh, in_specs=in_specs, out_specs=out_specs, check_vma=False)
```

```python
import functools

import jax
import jax.numpy as jnp
from jax import lax
from jax.experimental import pallas as pl
from jax.experimental.pallas import tpu as pltpu
from jax.sharding import PartitionSpec as P

bf16 = jnp.bfloat16
f32 = jnp.float32
VMEM = pl.BlockSpec(memory_space=pltpu.VMEM)
SMEM = pl.BlockSpec(memory_space=pltpu.SMEM)


def call(body, outs, ins, flops, name, grant=16):
    moved = sum(x.size * x.dtype.itemsize for x in list(ins) + list(outs))
    return pl.pallas_call(
        body,
        out_shape=outs,
        in_specs=[SMEM if x.size <= 256 else VMEM for x in ins],
        out_specs=[VMEM] * len(outs),
        compiler_params=pltpu.CompilerParams(vmem_limit_bytes=grant * 2**20),
        cost_estimate=pl.CostEstimate(flops=flops, bytes_accessed=moved, transcendentals=0),
        name=name,
    )(*ins)


def shape(*dims, dtype=bf16):
    return jax.ShapeDtypeStruct(dims, dtype)


def dot(left, right):
    return jnp.dot(left, right, preferred_element_type=f32)


def contract(left, right, axis_left, axis_right):
    dims = (((axis_left,), (axis_right,)), ((), ()))
    return lax.dot_general(left, right, dims, preferred_element_type=f32)


def split(value):
    high = value.astype(bf16)
    return high, (value - high.astype(f32)).astype(bf16)


def product(left, right):
    return dot(left[0], right[0]) + (dot(left[0], right[1]) + dot(left[1], right[0]))


def block(wide):
    size = wide.shape[1] // 2
    real, imag = wide[:, :size], wide[:, size:]
    return jnp.concatenate([wide, jnp.concatenate([-imag, real], axis=1)], axis=0)


def both_of(pair, form):
    return form(pair[0]), form(pair[1])


def couple(rows_h, rows_s, shift_real, shift_imag):
    margin = rows_s.astype(f32)
    real = (rows_h.astype(f32) - shift_real * margin).astype(bf16)
    imag = (-shift_imag * margin).astype(bf16)
    return real, imag


def invert_body(shift, pivot_h, pivot_s, inverse):
    size = pivot_h.shape[0]
    shift_real, shift_imag = shift[0, 0], shift[0, 1]
    margin = pivot_s[...].astype(f32)
    real = pivot_h[...].astype(f32) - shift_real * margin
    imag = -shift_imag * margin
    on_diag = lax.broadcasted_iota(jnp.int32, (size, size), 0) == lax.broadcasted_iota(
        jnp.int32, (size, size), 1
    )

    def scales(axis):
        diag_real = jnp.sum(jnp.where(on_diag, real, 0.0), axis=axis, keepdims=True)
        diag_imag = jnp.sum(jnp.where(on_diag, imag, 0.0), axis=axis, keepdims=True)
        denom = diag_real * diag_real + diag_imag * diag_imag
        return diag_real / denom, -diag_imag / denom

    col_real, col_imag = scales(0)
    err_real = jnp.where(on_diag, 0.0, imag * col_imag - real * col_real)
    err_imag = jnp.where(on_diag, 0.0, -(real * col_imag + imag * col_real))
    one = jnp.concatenate([jnp.where(on_diag, 1.0, 0.0), jnp.zeros((size, size), f32)], axis=1)
    err = jnp.concatenate([err_real, err_imag], axis=1)
    err_pair = split(err)
    err2 = product(err_pair, both_of(err_pair, block))
    err2_pair = split(err2)
    square = both_of(err2_pair, block)
    err3 = product(err_pair, square)
    err4_pair = split(product(err2_pair, square))
    first = one + err + err2 + err3
    fourth = both_of(err4_pair, block)
    second = first + product(split(first), fourth)
    err8_pair = split(product(err4_pair, fourth))
    total = second + product(split(second), both_of(err8_pair, block))
    sum_real, sum_imag = total[:, :size], total[:, size:]
    row_real, row_imag = scales(1)
    inv_real = row_real * sum_real - row_imag * sum_imag
    inv_imag = row_real * sum_imag + row_imag * sum_real
    inverse[0], inverse[1] = split(jnp.concatenate([inv_real, inv_imag], axis=1))


def solve(rows_h, rows_s, shift, inverse):
    coupling = jnp.concatenate(couple(rows_h, rows_s, shift[0, 0], shift[0, 1]), axis=1)
    return (dot(coupling, block(inverse[0])) + dot(coupling, block(inverse[1]))).astype(bf16)


def local_body(shift, weight, panel_h, panel_s, inverse, right, base, rights, bases, sems):
    size = panel_h.shape[1]
    solved = solve(panel_h[...], panel_s[...], shift, inverse)
    rights[:size] = solved[:, :size]
    rights[size:] = solved[:, size:]
    whole = inverse[0].astype(f32) + inverse[1].astype(f32)
    density = weight[0, 0] * whole[:, size:] + weight[0, 1] * whole[:, :size]
    first_device = (lax.axis_index("row") == 0) & (lax.axis_index("col") == 0)
    bases[...] = jnp.where(first_device, density.T, 0.0)
    stores = [
        pltpu.make_async_copy(rights, right, sems.at[0]),
        pltpu.make_async_copy(bases, base, sems.at[1]),
    ]
    for store in stores:
        store.start()
    for store in stores:
        store.wait()


def pack_body(panel_h, panel_s, front_h, front_s, out, panels, fronts, buffer, sems):
    half = panels.shape[1] // 2
    share, size = fronts.shape[1], out.shape[2]
    shares = panels.shape[1] // share
    at = pl.ds(pl.multiple_of(lax.axis_index("col") * 2 * half, 2 * half), 2 * half)
    of = pl.ds(pl.multiple_of(lax.rem(lax.axis_index("pole"), shares) * share, share), share)
    loads = [
        pltpu.make_async_copy(panel_h.at[at], panels.at[0], sems.at[0]),
        pltpu.make_async_copy(panel_s.at[at], panels.at[1], sems.at[1]),
        pltpu.make_async_copy(front_h.at[of], fronts.at[0], sems.at[2]),
        pltpu.make_async_copy(front_s.at[of], fronts.at[1], sems.at[3]),
    ]
    panel_rows, front_rows = pl.ds(0, 2 * half), pl.ds(2 * half, 2 * share)
    stores = [
        pltpu.make_async_copy(buffer.at[:, rows], out.at[:, rows], sems.at[4 + index])
        for index, rows in enumerate((panel_rows, front_rows))
    ]
    for load in loads:
        load.start()
    loads[0].wait()
    loads[1].wait()
    for row in range(out.shape[0]):
        core = row % 2
        for part in range(2):
            low = part * half
            buffer[row, low : low + half] = panels[part, core * half : (core + 1) * half]
    stores[0].start()
    loads[2].wait()
    loads[3].wait()
    for row in range(out.shape[0]):
        for part in range(2):
            low = 2 * half + part * share
            buffer[row, low : low + share] = fronts[part, :, row * size : (row + 1) * size]
    stores[1].start()
    for store in stores:
        store.wait()


def solve_body(shift, received, inverse, solved, fronts):
    strips, rows, size = received.shape
    half = solved.shape[0] // strips
    rows_h = received[:, :half].reshape(strips * half, size)
    rows_s = received[:, half : 2 * half].reshape(strips * half, size)
    solved[...] = solve(rows_h, rows_s, shift, inverse)
    fronts[...] = received[:, 2 * half :]


def ordered(mine, other):
    low = lax.rem(lax.axis_index("row"), 2) == 0
    return jnp.where(low, mine, other), jnp.where(low, other, mine)


def fold(member, out, at):
    pieces = out.shape[0]
    half = out.shape[1] // 2
    cols = 2 * member.shape[1] // 128
    low_lane = lax.broadcasted_iota(jnp.int32, (half, 128), 1) < 64
    for pole in range(pieces // cols):
        for pair in range(cols // 2):
            rows = pole * 2 * half
            top = member[rows : rows + half, pair * 128 : pair * 128 + 128]
            bottom = member[rows + half : rows + 2 * half, pair * 128 : pair * 128 + 128]
            even = jnp.where(low_lane, top, pltpu.roll(bottom, 64, 1))
            odd = jnp.where(low_lane, pltpu.roll(top, 64, 1), bottom)
            poles = pieces // cols
            out[2 * pair * poles + pole, at : at + half] = even.astype(out.dtype)
            out[(2 * pair + 1) * poles + pole, at : at + half] = odd.astype(out.dtype)


def half_column(solved, ancestor, core):
    strips, half, size = ancestor.shape[1], ancestor.shape[2] // 2, ancestor.shape[3]
    at = pl.ds(pl.multiple_of(core * half, half), half)
    rows = solved[...]
    by_real = contract(rows, ancestor[0, :, at, :].reshape(strips * half, size), 0, 0)
    by_imag = contract(rows, ancestor[1, :, at, :].reshape(strips * half, size), 0, 0)
    return by_real[:size] - by_imag[size:], by_real[size:] + by_imag[:size]


def own_column_body(mine, ancestor, part):
    size = part.shape[1]
    part[:size], part[size:] = half_column(mine, ancestor, lax.rem(lax.axis_index("row"), 2))


def column_body(weight, other, ancestor, part, right, base, out, buffer, sems):
    size = part.shape[1]
    half = out.shape[1] // 2
    part_real, part_imag = half_column(other, ancestor, 1 - lax.rem(lax.axis_index("row"), 2))
    part_real += part[:size]
    part_imag += part[size:]
    stores = [
        pltpu.make_async_copy(buffer.at[:, rows], out.at[:, rows], sems.at[index])
        for index, rows in enumerate((pl.ds(0, half), pl.ds(half, half)))
    ]
    weight_real, weight_imag = weight[0, 0], weight[0, 1]
    density = -(weight_real * part_imag + weight_imag * part_real)
    fold(density, buffer, 0)
    stores[0].start()
    twin = -(weight_real * part_real - weight_imag * part_imag)
    high, low = split(jnp.concatenate([density, twin], axis=1))
    pivot = base[...] - (dot(high, right[...]) + dot(low, right[...]))
    fold(pivot, buffer, half)
    stores[1].start()
    for store in stores:
        store.wait()


def sums_body(parts, spread, rows):
    half, width = parts.shape[1] // 2, rows.shape[1]
    total = jnp.sum(parts[...].astype(f32), axis=0)
    rows[:half] = total[:half, :width]
    rows[half:] = total[:half, width:]
    spread[...] = jnp.broadcast_to(total[None, half:].astype(spread.dtype), spread.shape)


def pivot_body(parts, out):
    half = parts.shape[1]
    width = 64
    cols = out.shape[1] // width
    total = jnp.sum(parts[...].astype(f32).reshape(-1, cols, half, 128), axis=0)
    for index in range(128 // width):
        lanes = slice(index * width, (index + 1) * width)
        strips = [total[col][:, lanes] for col in range(cols)]
        out[index * half : (index + 1) * half] = jnp.concatenate(strips, axis=1)


def update_body(shift, panel_h, panel_s, mine, other, out):
    strips, rows = out.shape[0], out.shape[1] * out.shape[2]
    half = mine.shape[0] // strips
    group = 4
    top, bottom = ordered(mine[...], other[...])
    real, imag = couple(panel_h[...], panel_s[...], shift[0, 0], shift[0, 1])
    wide = jnp.concatenate(
        [jnp.concatenate([real, -imag], axis=1), jnp.concatenate([imag, real], axis=1)], axis=0
    )
    for first in range(0, strips, group):
        solved = jnp.concatenate(
            [
                member[strip * half : (strip + 1) * half]
                for strip in range(first, first + group)
                for member in (top, bottom)
            ],
            axis=0,
        )
        update = contract(solved, wide, 1, 1)
        out[first : first + group] = update.reshape((group,) + out.shape[1:])


def relay_body(from_below, from_above, below, above):
    half = below.shape[0]
    below[...] = from_below[:half]
    above[...] = from_above[half:]


def schur_tiles(shift, pattern, update, members, buffer, out, sems):
    strips, count, share, size = out.shape[1:]
    pole = lax.axis_index("pole")
    row = lax.axis_index("row")
    shift_real, shift_imag = shift[0, 0], shift[0, 1]
    copies = []
    for member, start, length, step, first in members:
        at = lax.rem(pole + count + step, count)
        for index in range(length):
            strip = first + index
            mask = pattern[strip, row].astype(f32)
            margin = mask * member[start + index, share:].astype(f32)
            real = mask * member[start + index, :share].astype(f32) - shift_real * margin
            buffer[0, strip, at] = (real - update[strip, at, :, :size]).astype(bf16)
            buffer[1, strip, at] = (-shift_imag * margin - update[strip, at, :, size:]).astype(bf16)
        where = (slice(None), pl.ds(first, length), at)
        copies.append(pltpu.make_async_copy(buffer.at[where], out.at[where], sems.at[len(copies)]))
        copies[-1].start()
    for copy in copies:
        copy.wait()


def schur_first_body(shift, pattern, update, fronts, from_below, from_above, out, buffer, sems):
    strips = out.shape[1]
    members = (
        (fronts, 0, strips, 0, 0),
        (from_below, 0, strips, -1, 0),
        (from_above, 0, strips, 1, 0),
    )
    schur_tiles(shift, pattern, update, members, buffer, out, sems)


def schur_last_body(shift, pattern, update, below, above, begun, out, buffer, sems):
    del begun
    half = below.shape[0]
    members = ((below, 0, half, -2, 0), (above, 0, half, 2, half))
    schur_tiles(shift, pattern, update, members, buffer, out, sems)


def shards(
    front_h,
    front_s,
    panel_h,
    panel_s,
    pivot_h,
    pivot_s,
    pole_shift,
    pole_weight,
    pattern,
    ancestor_inverse,
):
    row_count = lax.axis_size("row")
    col_count = lax.axis_size("col")
    pole_count = lax.axis_size("pole")
    col_index = lax.axis_index("col")
    size = pivot_h.shape[0]
    width = size // col_count
    piece = size // pole_count
    half = width // 2
    neighbour = [(i, i ^ 1) for i in range(row_count)]

    quarters = 4
    share = width // quarters

    (sent,) = pl.pallas_call(
        pack_body,
        out_shape=[shape(row_count, width + 2 * share, size)],
        in_specs=[pl.BlockSpec(memory_space=pl.ANY)] * 4,
        out_specs=[pl.BlockSpec(memory_space=pl.ANY)],
        scratch_shapes=[
            pltpu.VMEM((2, width, size), bf16),
            pltpu.VMEM((2, share, row_count * size), bf16),
            pltpu.VMEM((row_count, width + 2 * share, size), bf16),
            pltpu.SemaphoreType.DMA((6,)),
        ],
        cost_estimate=pl.CostEstimate(flops=0, bytes_accessed=2**20, transcendentals=0),
        name="pack",
    )(panel_h, panel_s, front_h, front_s)
    received = lax.all_to_all(sent, "row", split_axis=0, concat_axis=0, tiled=True)

    (inverse,) = call(
        invert_body,
        [shape(2, size, 2 * size)],
        [pole_shift, pivot_h, pivot_s],
        6 * 4 * 3 * 2 * size**3,
        "pivot_inverse",
    )
    right, base = pl.pallas_call(
        local_body,
        out_shape=[shape(2 * size, size), shape(size, size, dtype=f32)],
        in_specs=[SMEM] * 2 + [VMEM] * 3,
        out_specs=[pl.BlockSpec(memory_space=pltpu.HBM)] * 2,
        scratch_shapes=[
            pltpu.VMEM((2 * size, size), bf16),
            pltpu.VMEM((size, size), f32),
            pltpu.SemaphoreType.DMA((2,)),
        ],
        compiler_params=pltpu.CompilerParams(vmem_limit_bytes=16 * 2**20),
        cost_estimate=pl.CostEstimate(
            flops=2 * 8 * size**3, bytes_accessed=2**20, transcendentals=0
        ),
        name="local_rows",
    )(pole_shift, pole_weight, panel_h, panel_s, inverse)
    inverse, right, base = lax.optimization_barrier((inverse, right, base))
    mine, fronts = call(
        solve_body,
        [shape(row_count * half, 2 * size), shape(row_count, 2 * share, size)],
        [pole_shift, received, inverse],
        2 * 8 * row_count * half * size * size,
        "solved_rows",
    )
    other = lax.ppermute(mine, "row", neighbour)
    ancestor = ancestor_inverse.reshape(2, row_count, width, size)
    (part,) = call(
        own_column_body,
        [shape(2 * size, size, dtype=f32)],
        [mine, ancestor],
        4 * row_count * width * size * size,
        "own_column",
    )
    folded = (col_count * pole_count, piece, 128)
    (both,) = pl.pallas_call(
        column_body,
        out_shape=[shape(*folded)],
        in_specs=[SMEM] + [VMEM] * 5,
        out_specs=[pl.BlockSpec(memory_space=pl.ANY)],
        scratch_shapes=[pltpu.VMEM(folded, bf16), pltpu.SemaphoreType.DMA((2,))],
        compiler_params=pltpu.CompilerParams(vmem_limit_bytes=16 * 2**20),
        cost_estimate=pl.CostEstimate(
            flops=4 * row_count * width * size * size, bytes_accessed=2 * 2**20, transcendentals=0
        ),
        name="column",
    )(pole_weight, other, ancestor, part, right, base)

    onward = [(i, (i + 1) % pole_count) for i in range(pole_count)]
    back = [(i, (i - 1) % pole_count) for i in range(pole_count)]
    fronts, both = lax.optimization_barrier((fronts, both))
    from_below = lax.ppermute(fronts, "pole", onward)
    from_above = lax.ppermute(fronts, "pole", back)

    (update,) = call(
        update_body,
        [shape(row_count, quarters, share, 2 * size, dtype=f32)],
        [pole_shift, panel_h, panel_s, mine, other],
        8 * row_count * width * size * size,
        "update",
    )
    both = lax.all_to_all(both, ("col", "pole"), split_axis=0, concat_axis=0, tiled=True)
    both, update = lax.optimization_barrier((both, update))
    spread, rows_out = call(
        sums_body,
        [
            shape(row_count * col_count, piece // 2, 128),
            shape(piece, width, dtype=f32),
        ],
        [both],
        0,
        "sums",
    )
    below, above = call(
        relay_body,
        [shape(row_count // 2, 2 * share, size)] * 2,
        [from_below, from_above],
        10**11,
        "relay",
    )
    below = lax.ppermute(below, "pole", onward)
    above = lax.ppermute(above, "pole", back)
    spread = lax.all_to_all(spread, ("row", "col"), split_axis=0, concat_axis=0, tiled=True)
    (pivot_out,) = call(pivot_body, [shape(piece, size, dtype=f32)], [spread], 0, "pivot")

    def tiles(body, ins, name, begun=()):
        tile = shape(2, row_count, quarters, share, size)
        return pl.pallas_call(
            body,
            out_shape=tile,
            in_specs=[SMEM] * 2 + [VMEM] * (len(ins) - 2) + [pl.BlockSpec(memory_space=pl.ANY)] * len(begun),
            out_specs=pl.BlockSpec(memory_space=pl.ANY),
            input_output_aliases={len(ins): 0} if begun else {},
            scratch_shapes=[pltpu.VMEM(tile.shape, bf16), pltpu.SemaphoreType.DMA((4,))],
            compiler_params=pltpu.CompilerParams(vmem_limit_bytes=16 * 2**20),
            cost_estimate=pl.CostEstimate(flops=0, bytes_accessed=3 * 2**20, transcendentals=0),
            name=name,
        )(*ins, *begun)

    fixed = [pole_shift, pattern, update]
    schur = tiles(schur_first_body, fixed + [fronts, from_below, from_above], "schur_first")
    schur = tiles(schur_last_body, fixed + [below, above], "schur_last", (schur,))
    return (schur.reshape(1, 2, row_count, 1, width, size), rows_out.T, pivot_out.T)


def solution(mesh):
    in_specs = (
        P(("row", "col"), None),
        P(("row", "col"), None),
        P("row", None),
        P("row", None),
        P(),
        P(),
        P("pole", None),
        P("pole", None),
        P(),
        P("pole", None, None, "col", None, "row"),
    )
    out_specs = (
        P("pole", None, None, "col", None, "row"),
        P(("row", "col"), "pole"),
        P(None, "pole"),
    )
    return jax.shard_map(shards, mesh=mesh, in_specs=in_specs, out_specs=out_specs, check_vma=False)
```

```python
import functools

import jax
import jax.numpy as jnp
from jax import lax
from jax.experimental import pallas as pl
from jax.experimental.pallas import tpu as pltpu
from jax.sharding import PartitionSpec as P

bf16 = jnp.bfloat16
f32 = jnp.float32
VMEM = pl.BlockSpec(memory_space=pltpu.VMEM)
SMEM = pl.BlockSpec(memory_space=pltpu.SMEM)


def call(body, outs, ins, flops, name, grant=16):
    moved = sum(x.size * x.dtype.itemsize for x in list(ins) + list(outs))
    return pl.pallas_call(
        body,
        out_shape=outs,
        in_specs=[SMEM if x.size <= 256 else VMEM for x in ins],
        out_specs=[VMEM] * len(outs),
        compiler_params=pltpu.CompilerParams(vmem_limit_bytes=grant * 2**20),
        cost_estimate=pl.CostEstimate(flops=flops, bytes_accessed=moved, transcendentals=0),
        name=name,
    )(*ins)


def shape(*dims, dtype=bf16):
    return jax.ShapeDtypeStruct(dims, dtype)


def dot(left, right):
    return jnp.dot(left, right, preferred_element_type=f32)


def contract(left, right, axis_left, axis_right):
    dims = (((axis_left,), (axis_right,)), ((), ()))
    return lax.dot_general(left, right, dims, preferred_element_type=f32)


def split(value):
    high = value.astype(bf16)
    return high, (value - high.astype(f32)).astype(bf16)


def product(left, right):
    return dot(left[0], right[0]) + (dot(left[0], right[1]) + dot(left[1], right[0]))


def block(wide):
    size = wide.shape[1] // 2
    real, imag = wide[:, :size], wide[:, size:]
    return jnp.concatenate([wide, jnp.concatenate([-imag, real], axis=1)], axis=0)


def both_of(pair, form):
    return form(pair[0]), form(pair[1])


def couple(rows_h, rows_s, shift_real, shift_imag):
    margin = rows_s.astype(f32)
    real = (rows_h.astype(f32) - shift_real * margin).astype(bf16)
    imag = (-shift_imag * margin).astype(bf16)
    return real, imag


def invert_body(shift, pivot_h, pivot_s, inverse):
    size = pivot_h.shape[0]
    shift_real, shift_imag = shift[0, 0], shift[0, 1]
    margin = pivot_s[...].astype(f32)
    real = pivot_h[...].astype(f32) - shift_real * margin
    imag = -shift_imag * margin
    on_diag = lax.broadcasted_iota(jnp.int32, (size, size), 0) == lax.broadcasted_iota(
        jnp.int32, (size, size), 1
    )

    def scales(axis):
        diag_real = jnp.sum(jnp.where(on_diag, real, 0.0), axis=axis, keepdims=True)
        diag_imag = jnp.sum(jnp.where(on_diag, imag, 0.0), axis=axis, keepdims=True)
        denom = diag_real * diag_real + diag_imag * diag_imag
        return diag_real / denom, -diag_imag / denom

    col_real, col_imag = scales(0)
    err_real = jnp.where(on_diag, 0.0, imag * col_imag - real * col_real)
    err_imag = jnp.where(on_diag, 0.0, -(real * col_imag + imag * col_real))
    one = jnp.concatenate([jnp.where(on_diag, 1.0, 0.0), jnp.zeros((size, size), f32)], axis=1)
    err = jnp.concatenate([err_real, err_imag], axis=1)
    err_pair = split(err)
    err2 = product(err_pair, both_of(err_pair, block))
    err2_pair = split(err2)
    square = both_of(err2_pair, block)
    err3 = product(err_pair, square)
    err4_pair = split(product(err2_pair, square))
    first = one + err + err2 + err3
    fourth = both_of(err4_pair, block)
    second = first + product(split(first), fourth)
    err8_pair = split(product(err4_pair, fourth))
    total = second + product(split(second), both_of(err8_pair, block))
    sum_real, sum_imag = total[:, :size], total[:, size:]
    row_real, row_imag = scales(1)
    inv_real = row_real * sum_real - row_imag * sum_imag
    inv_imag = row_real * sum_imag + row_imag * sum_real
    inverse[0], inverse[1] = split(jnp.concatenate([inv_real, inv_imag], axis=1))


def solve(rows_h, rows_s, shift, inverse):
    coupling = jnp.concatenate(couple(rows_h, rows_s, shift[0, 0], shift[0, 1]), axis=1)
    return (dot(coupling, block(inverse[0])) + dot(coupling, block(inverse[1]))).astype(bf16)


def local_body(shift, weight, panel_h, panel_s, inverse, right, base, rights, bases, sems):
    size = panel_h.shape[1]
    solved = solve(panel_h[...], panel_s[...], shift, inverse)
    rights[:size] = solved[:, :size]
    rights[size:] = solved[:, size:]
    whole = inverse[0].astype(f32) + inverse[1].astype(f32)
    density = weight[0, 0] * whole[:, size:] + weight[0, 1] * whole[:, :size]
    first_device = (lax.axis_index("row") == 0) & (lax.axis_index("col") == 0)
    bases[...] = jnp.where(first_device, density.T, 0.0)
    stores = [
        pltpu.make_async_copy(rights, right, sems.at[0]),
        pltpu.make_async_copy(bases, base, sems.at[1]),
    ]
    for store in stores:
        store.start()
    for store in stores:
        store.wait()


def pack_body(panel_h, panel_s, front_h, front_s, out, panels, fronts, buffer, sems):
    half = panels.shape[1] // 2
    share, size = fronts.shape[1], out.shape[2]
    shares = panels.shape[1] // share
    at = pl.ds(pl.multiple_of(lax.axis_index("col") * 2 * half, 2 * half), 2 * half)
    of = pl.ds(pl.multiple_of(lax.rem(lax.axis_index("pole"), shares) * share, share), share)
    loads = [
        pltpu.make_async_copy(panel_h.at[at], panels.at[0], sems.at[0]),
        pltpu.make_async_copy(panel_s.at[at], panels.at[1], sems.at[1]),
        pltpu.make_async_copy(front_h.at[of], fronts.at[0], sems.at[2]),
        pltpu.make_async_copy(front_s.at[of], fronts.at[1], sems.at[3]),
    ]
    panel_rows, front_rows = pl.ds(0, 2 * half), pl.ds(2 * half, 2 * share)
    stores = [
        pltpu.make_async_copy(buffer.at[:, rows], out.at[:, rows], sems.at[4 + index])
        for index, rows in enumerate((panel_rows, front_rows))
    ]
    for load in loads:
        load.start()
    loads[0].wait()
    loads[1].wait()
    for row in range(out.shape[0]):
        core = row % 2
        for part in range(2):
            low = part * half
            buffer[row, low : low + half] = panels[part, core * half : (core + 1) * half]
    stores[0].start()
    loads[2].wait()
    loads[3].wait()
    for row in range(out.shape[0]):
        for part in range(2):
            low = 2 * half + part * share
            buffer[row, low : low + share] = fronts[part, :, row * size : (row + 1) * size]
    stores[1].start()
    for store in stores:
        store.wait()


def fronts_body(received, fronts):
    fronts[...] = received[:, received.shape[1] - fronts.shape[1] :]


def solve_body(shift, received, inverse, solved):
    strips, rows, size = received.shape
    half = solved.shape[0] // strips
    rows_h = received[:, :half].reshape(strips * half, size)
    rows_s = received[:, half : 2 * half].reshape(strips * half, size)
    solved[...] = solve(rows_h, rows_s, shift, inverse)


def ordered(mine, other):
    low = lax.rem(lax.axis_index("row"), 2) == 0
    return jnp.where(low, mine, other), jnp.where(low, other, mine)


def fold(member, out, at):
    pieces = out.shape[0]
    half = out.shape[1] // 2
    cols = 2 * member.shape[1] // 128
    low_lane = lax.broadcasted_iota(jnp.int32, (half, 128), 1) < 64
    for pole in range(pieces // cols):
        for pair in range(cols // 2):
            rows = pole * 2 * half
            top = member[rows : rows + half, pair * 128 : pair * 128 + 128]
            bottom = member[rows + half : rows + 2 * half, pair * 128 : pair * 128 + 128]
            even = jnp.where(low_lane, top, pltpu.roll(bottom, 64, 1))
            odd = jnp.where(low_lane, pltpu.roll(top, 64, 1), bottom)
            poles = pieces // cols
            out[2 * pair * poles + pole, at : at + half] = even.astype(out.dtype)
            out[(2 * pair + 1) * poles + pole, at : at + half] = odd.astype(out.dtype)


def half_column(solved, ancestor, core):
    strips, half, size = ancestor.shape[1], ancestor.shape[2] // 2, ancestor.shape[3]
    at = pl.ds(pl.multiple_of(core * half, half), half)
    rows = solved[...]
    by_real = contract(rows, ancestor[0, :, at, :].reshape(strips * half, size), 0, 0)
    by_imag = contract(rows, ancestor[1, :, at, :].reshape(strips * half, size), 0, 0)
    return by_real[:size] - by_imag[size:], by_real[size:] + by_imag[:size]


def own_column_body(mine, ancestor, part):
    size = part.shape[1]
    part[:size], part[size:] = half_column(mine, ancestor, lax.rem(lax.axis_index("row"), 2))


def column_body(weight, other, ancestor, part, right, base, out, buffer, sems):
    size = part.shape[1]
    half = out.shape[1] // 2
    part_real, part_imag = half_column(other, ancestor, 1 - lax.rem(lax.axis_index("row"), 2))
    part_real += part[:size]
    part_imag += part[size:]
    stores = [
        pltpu.make_async_copy(buffer.at[:, rows], out.at[:, rows], sems.at[index])
        for index, rows in enumerate((pl.ds(0, half), pl.ds(half, half)))
    ]
    weight_real, weight_imag = weight[0, 0], weight[0, 1]
    density = -(weight_real * part_imag + weight_imag * part_real)
    fold(density, buffer, 0)
    stores[0].start()
    twin = -(weight_real * part_real - weight_imag * part_imag)
    high, low = split(jnp.concatenate([density, twin], axis=1))
    pivot = base[...] - (dot(high, right[...]) + dot(low, right[...]))
    fold(pivot, buffer, half)
    stores[1].start()
    for store in stores:
        store.wait()


def sums_body(parts, spread, rows):
    half, width = parts.shape[1] // 2, rows.shape[1]
    total = jnp.sum(parts[...].astype(f32), axis=0)
    rows[:half] = total[:half, :width]
    rows[half:] = total[:half, width:]
    spread[...] = jnp.broadcast_to(total[None, half:].astype(spread.dtype), spread.shape)


def pivot_body(parts, out):
    half = parts.shape[1]
    width = 64
    cols = out.shape[1] // width
    total = jnp.sum(parts[...].astype(f32).reshape(-1, cols, half, 128), axis=0)
    for index in range(128 // width):
        lanes = slice(index * width, (index + 1) * width)
        strips = [total[col][:, lanes] for col in range(cols)]
        out[index * half : (index + 1) * half] = jnp.concatenate(strips, axis=1)


def update_body(shift, panel_h, panel_s, mine, other, out):
    strips, rows = out.shape[0], out.shape[1] * out.shape[2]
    half = mine.shape[0] // strips
    group = 4
    top, bottom = ordered(mine[...], other[...])
    real, imag = couple(panel_h[...], panel_s[...], shift[0, 0], shift[0, 1])
    wide = jnp.concatenate(
        [jnp.concatenate([real, -imag], axis=1), jnp.concatenate([imag, real], axis=1)], axis=0
    )
    for first in range(0, strips, group):
        solved = jnp.concatenate(
            [
                member[strip * half : (strip + 1) * half]
                for strip in range(first, first + group)
                for member in (top, bottom)
            ],
            axis=0,
        )
        update = contract(solved, wide, 1, 1)
        out[first : first + group] = update.reshape((group,) + out.shape[1:])


def relay_body(from_below, from_above, below, above):
    half = below.shape[0]
    below[...] = from_below[:half]
    above[...] = from_above[half:]


def schur_tiles(shift, pattern, update, members, buffer, out, sems):
    strips, count, share, size = out.shape[1:]
    pole = lax.axis_index("pole")
    row = lax.axis_index("row")
    shift_real, shift_imag = shift[0, 0], shift[0, 1]
    copies = []
    for member, start, length, step, first in members:
        at = lax.rem(pole + count + step, count)
        for index in range(length):
            strip = first + index
            mask = pattern[strip, row].astype(f32)
            margin = mask * member[start + index, share:].astype(f32)
            real = mask * member[start + index, :share].astype(f32) - shift_real * margin
            buffer[0, strip, at] = (real - update[strip, at, :, :size]).astype(bf16)
            buffer[1, strip, at] = (-shift_imag * margin - update[strip, at, :, size:]).astype(bf16)
        where = (slice(None), pl.ds(first, length), at)
        copies.append(pltpu.make_async_copy(buffer.at[where], out.at[where], sems.at[len(copies)]))
        copies[-1].start()
    for copy in copies:
        copy.wait()


def schur_first_body(shift, pattern, update, fronts, from_below, from_above, out, buffer, sems):
    strips = out.shape[1]
    members = (
        (fronts, 0, strips, 0, 0),
        (from_below, 0, strips, -1, 0),
        (from_above, 0, strips, 1, 0),
    )
    schur_tiles(shift, pattern, update, members, buffer, out, sems)


def schur_last_body(shift, pattern, update, below, above, begun, out, buffer, sems):
    del begun
    half = below.shape[0]
    members = ((below, 0, half, -2, 0), (above, 0, half, 2, half))
    schur_tiles(shift, pattern, update, members, buffer, out, sems)


def shards(
    front_h,
    front_s,
    panel_h,
    panel_s,
    pivot_h,
    pivot_s,
    pole_shift,
    pole_weight,
    pattern,
    ancestor_inverse,
):
    row_count = lax.axis_size("row")
    col_count = lax.axis_size("col")
    pole_count = lax.axis_size("pole")
    col_index = lax.axis_index("col")
    size = pivot_h.shape[0]
    width = size // col_count
    piece = size // pole_count
    half = width // 2
    neighbour = [(i, i ^ 1) for i in range(row_count)]

    quarters = 4
    share = width // quarters

    (sent,) = pl.pallas_call(
        pack_body,
        out_shape=[shape(row_count, width + 2 * share, size)],
        in_specs=[pl.BlockSpec(memory_space=pl.ANY)] * 4,
        out_specs=[pl.BlockSpec(memory_space=pl.ANY)],
        scratch_shapes=[
            pltpu.VMEM((2, width, size), bf16),
            pltpu.VMEM((2, share, row_count * size), bf16),
            pltpu.VMEM((row_count, width + 2 * share, size), bf16),
            pltpu.SemaphoreType.DMA((6,)),
        ],
        cost_estimate=pl.CostEstimate(flops=0, bytes_accessed=2**20, transcendentals=0),
        name="pack",
    )(panel_h, panel_s, front_h, front_s)
    received = lax.all_to_all(sent, "row", split_axis=0, concat_axis=0, tiled=True)

    (inverse,) = call(
        invert_body,
        [shape(2, size, 2 * size)],
        [pole_shift, pivot_h, pivot_s],
        6 * 4 * 3 * 2 * size**3,
        "pivot_inverse",
    )
    right, base = pl.pallas_call(
        local_body,
        out_shape=[shape(2 * size, size), shape(size, size, dtype=f32)],
        in_specs=[SMEM] * 2 + [VMEM] * 3,
        out_specs=[pl.BlockSpec(memory_space=pltpu.HBM)] * 2,
        scratch_shapes=[
            pltpu.VMEM((2 * size, size), bf16),
            pltpu.VMEM((size, size), f32),
            pltpu.SemaphoreType.DMA((2,)),
        ],
        compiler_params=pltpu.CompilerParams(vmem_limit_bytes=16 * 2**20),
        cost_estimate=pl.CostEstimate(
            flops=2 * 8 * size**3, bytes_accessed=2**20, transcendentals=0
        ),
        name="local_rows",
    )(pole_shift, pole_weight, panel_h, panel_s, inverse)
    inverse, right, base = lax.optimization_barrier((inverse, right, base))
    (mine,) = call(
        solve_body,
        [shape(row_count * half, 2 * size)],
        [pole_shift, received, inverse],
        2 * 8 * row_count * half * size * size,
        "solved_rows",
    )
    other = lax.ppermute(mine, "row", neighbour)
    (fronts,) = call(
        fronts_body, [shape(row_count, 2 * share, size)], [received], 0, "fronts"
    )
    ancestor = ancestor_inverse.reshape(2, row_count, width, size)
    (part,) = call(
        own_column_body,
        [shape(2 * size, size, dtype=f32)],
        [mine, ancestor],
        4 * row_count * width * size * size,
        "own_column",
    )
    folded = (col_count * pole_count, piece, 128)
    (both,) = pl.pallas_call(
        column_body,
        out_shape=[shape(*folded)],
        in_specs=[SMEM] + [VMEM] * 5,
        out_specs=[pl.BlockSpec(memory_space=pl.ANY)],
        scratch_shapes=[pltpu.VMEM(folded, bf16), pltpu.SemaphoreType.DMA((2,))],
        compiler_params=pltpu.CompilerParams(vmem_limit_bytes=16 * 2**20),
        cost_estimate=pl.CostEstimate(
            flops=4 * row_count * width * size * size, bytes_accessed=2 * 2**20, transcendentals=0
        ),
        name="column",
    )(pole_weight, other, ancestor, part, right, base)

    onward = [(i, (i + 1) % pole_count) for i in range(pole_count)]
    back = [(i, (i - 1) % pole_count) for i in range(pole_count)]
    mine, other, both = lax.optimization_barrier((mine, other, both))
    (update,) = call(
        update_body,
        [shape(row_count, quarters, share, 2 * size, dtype=f32)],
        [pole_shift, panel_h, panel_s, mine, other],
        8 * row_count * width * size * size,
        "update",
    )
    fronts, update = lax.optimization_barrier((fronts, update))
    from_below = lax.ppermute(fronts, "pole", onward)
    from_above = lax.ppermute(fronts, "pole", back)

    both = lax.all_to_all(both, ("col", "pole"), split_axis=0, concat_axis=0, tiled=True)
    both, update = lax.optimization_barrier((both, update))
    spread, rows_out = call(
        sums_body,
        [
            shape(row_count * col_count, piece // 2, 128),
            shape(piece, width, dtype=f32),
        ],
        [both],
        0,
        "sums",
    )
    below, above = call(
        relay_body,
        [shape(row_count // 2, 2 * share, size)] * 2,
        [from_below, from_above],
        10**11,
        "relay",
    )
    below = lax.ppermute(below, "pole", onward)
    above = lax.ppermute(above, "pole", back)
    spread = lax.all_to_all(spread, ("row", "col"), split_axis=0, concat_axis=0, tiled=True)
    (pivot_out,) = call(pivot_body, [shape(piece, size, dtype=f32)], [spread], 0, "pivot")

    def tiles(body, ins, name, begun=()):
        tile = shape(2, row_count, quarters, share, size)
        return pl.pallas_call(
            body,
            out_shape=tile,
            in_specs=[SMEM] * 2 + [VMEM] * (len(ins) - 2) + [pl.BlockSpec(memory_space=pl.ANY)] * len(begun),
            out_specs=pl.BlockSpec(memory_space=pl.ANY),
            input_output_aliases={len(ins): 0} if begun else {},
            scratch_shapes=[pltpu.VMEM(tile.shape, bf16), pltpu.SemaphoreType.DMA((4,))],
            compiler_params=pltpu.CompilerParams(vmem_limit_bytes=16 * 2**20),
            cost_estimate=pl.CostEstimate(flops=0, bytes_accessed=3 * 2**20, transcendentals=0),
            name=name,
        )(*ins, *begun)

    fixed = [pole_shift, pattern, update]
    schur = tiles(schur_first_body, fixed + [fronts, from_below, from_above], "schur_first")
    schur = tiles(schur_last_body, fixed + [below, above], "schur_last", (schur,))
    return (schur.reshape(1, 2, row_count, 1, width, size), rows_out.T, pivot_out.T)


def solution(mesh):
    in_specs = (
        P(("row", "col"), None),
        P(("row", "col"), None),
        P("row", None),
        P("row", None),
        P(),
        P(),
        P("pole", None),
        P("pole", None),
        P(),
        P("pole", None, None, "col", None, "row"),
    )
    out_specs = (
        P("pole", None, None, "col", None, "row"),
        P(("row", "col"), "pole"),
        P(None, "pole"),
    )
    return jax.shard_map(shards, mesh=mesh, in_specs=in_specs, out_specs=out_specs, check_vma=False)
```

```python
import functools

import jax
import jax.numpy as jnp
from jax import lax
from jax.experimental import pallas as pl
from jax.experimental.pallas import tpu as pltpu
from jax.sharding import PartitionSpec as P

bf16 = jnp.bfloat16
f32 = jnp.float32
VMEM = pl.BlockSpec(memory_space=pltpu.VMEM)
SMEM = pl.BlockSpec(memory_space=pltpu.SMEM)


def call(body, outs, ins, flops, name, grant=16):
    moved = sum(x.size * x.dtype.itemsize for x in list(ins) + list(outs))
    return pl.pallas_call(
        body,
        out_shape=outs,
        in_specs=[SMEM if x.size <= 256 else VMEM for x in ins],
        out_specs=[VMEM] * len(outs),
        compiler_params=pltpu.CompilerParams(vmem_limit_bytes=grant * 2**20),
        cost_estimate=pl.CostEstimate(flops=flops, bytes_accessed=moved, transcendentals=0),
        name=name,
    )(*ins)


def shape(*dims, dtype=bf16):
    return jax.ShapeDtypeStruct(dims, dtype)


def dot(left, right):
    return jnp.dot(left, right, preferred_element_type=f32)


def contract(left, right, axis_left, axis_right):
    dims = (((axis_left,), (axis_right,)), ((), ()))
    return lax.dot_general(left, right, dims, preferred_element_type=f32)


def split(value):
    high = value.astype(bf16)
    return high, (value - high.astype(f32)).astype(bf16)


def product(left, right):
    return dot(left[0], right[0]) + (dot(left[0], right[1]) + dot(left[1], right[0]))


def block(wide):
    size = wide.shape[1] // 2
    real, imag = wide[:, :size], wide[:, size:]
    return jnp.concatenate([wide, jnp.concatenate([-imag, real], axis=1)], axis=0)


def both_of(pair, form):
    return form(pair[0]), form(pair[1])


def couple(rows_h, rows_s, shift_real, shift_imag):
    margin = rows_s.astype(f32)
    real = (rows_h.astype(f32) - shift_real * margin).astype(bf16)
    imag = (-shift_imag * margin).astype(bf16)
    return real, imag


def invert_body(shift, pivot_h, pivot_s, inverse):
    size = pivot_h.shape[0]
    shift_real, shift_imag = shift[0, 0], shift[0, 1]
    margin = pivot_s[...].astype(f32)
    real = pivot_h[...].astype(f32) - shift_real * margin
    imag = -shift_imag * margin
    on_diag = lax.broadcasted_iota(jnp.int32, (size, size), 0) == lax.broadcasted_iota(
        jnp.int32, (size, size), 1
    )

    def scales(axis):
        diag_real = jnp.sum(jnp.where(on_diag, real, 0.0), axis=axis, keepdims=True)
        diag_imag = jnp.sum(jnp.where(on_diag, imag, 0.0), axis=axis, keepdims=True)
        denom = diag_real * diag_real + diag_imag * diag_imag
        return diag_real / denom, -diag_imag / denom

    col_real, col_imag = scales(0)
    err_real = jnp.where(on_diag, 0.0, imag * col_imag - real * col_real)
    err_imag = jnp.where(on_diag, 0.0, -(real * col_imag + imag * col_real))
    one = jnp.concatenate([jnp.where(on_diag, 1.0, 0.0), jnp.zeros((size, size), f32)], axis=1)
    err = jnp.concatenate([err_real, err_imag], axis=1)
    err_pair = split(err)
    err2 = product(err_pair, both_of(err_pair, block))
    err2_pair = split(err2)
    square = both_of(err2_pair, block)
    err3 = product(err_pair, square)
    err4_pair = split(product(err2_pair, square))
    first = one + err + err2 + err3
    fourth = both_of(err4_pair, block)
    second = first + product(split(first), fourth)
    err8_pair = split(product(err4_pair, fourth))
    total = second + product(split(second), both_of(err8_pair, block))
    sum_real, sum_imag = total[:, :size], total[:, size:]
    row_real, row_imag = scales(1)
    inv_real = row_real * sum_real - row_imag * sum_imag
    inv_imag = row_real * sum_imag + row_imag * sum_real
    inverse[0], inverse[1] = split(jnp.concatenate([inv_real, inv_imag], axis=1))


def solve(rows_h, rows_s, shift, inverse):
    coupling = jnp.concatenate(couple(rows_h, rows_s, shift[0, 0], shift[0, 1]), axis=1)
    return (dot(coupling, block(inverse[0])) + dot(coupling, block(inverse[1]))).astype(bf16)


def pack_body(panel_h, panel_s, front_h, front_s, out, panels, fronts, buffer, sems):
    half = panels.shape[1] // 2
    share, size = fronts.shape[1], out.shape[2]
    shares = panels.shape[1] // share
    at = pl.ds(pl.multiple_of(lax.axis_index("col") * 2 * half, 2 * half), 2 * half)
    of = pl.ds(pl.multiple_of(lax.rem(lax.axis_index("pole"), shares) * share, share), share)
    loads = [
        pltpu.make_async_copy(panel_h.at[at], panels.at[0], sems.at[0]),
        pltpu.make_async_copy(panel_s.at[at], panels.at[1], sems.at[1]),
        pltpu.make_async_copy(front_h.at[of], fronts.at[0], sems.at[2]),
        pltpu.make_async_copy(front_s.at[of], fronts.at[1], sems.at[3]),
    ]
    panel_rows, front_rows = pl.ds(0, 2 * half), pl.ds(2 * half, 2 * share)
    stores = [
        pltpu.make_async_copy(buffer.at[:, rows], out.at[:, rows], sems.at[4 + index])
        for index, rows in enumerate((panel_rows, front_rows))
    ]
    for load in loads:
        load.start()
    loads[0].wait()
    loads[1].wait()
    for row in range(out.shape[0]):
        core = row % 2
        for part in range(2):
            low = part * half
            buffer[row, low : low + half] = panels[part, core * half : (core + 1) * half]
    stores[0].start()
    loads[2].wait()
    loads[3].wait()
    for row in range(out.shape[0]):
        for part in range(2):
            low = 2 * half + part * share
            buffer[row, low : low + share] = fronts[part, :, row * size : (row + 1) * size]
    stores[1].start()
    for store in stores:
        store.wait()


def solve_body(shift, received, inverse, solved, up, down):
    strips, rows, size = received.shape
    half = solved.shape[0] // strips
    rows_h = received[:, :half].reshape(strips * half, size)
    rows_s = received[:, half : 2 * half].reshape(strips * half, size)
    solved[...] = solve(rows_h, rows_s, shift, inverse)
    up[...] = received[: up.shape[0], 2 * half :]
    down[...] = received[strips - down.shape[0] :, 2 * half :]


def ordered(mine, other):
    low = lax.rem(lax.axis_index("row"), 2) == 0
    return jnp.where(low, mine, other), jnp.where(low, other, mine)


def fold(member, out, at):
    pieces = out.shape[0]
    half = out.shape[1] // 2
    cols = 2 * member.shape[1] // 128
    low_lane = lax.broadcasted_iota(jnp.int32, (half, 128), 1) < 64
    for pole in range(pieces // cols):
        for pair in range(cols // 2):
            rows = pole * 2 * half
            top = member[rows : rows + half, pair * 128 : pair * 128 + 128]
            bottom = member[rows + half : rows + 2 * half, pair * 128 : pair * 128 + 128]
            even = jnp.where(low_lane, top, pltpu.roll(bottom, 64, 1))
            odd = jnp.where(low_lane, pltpu.roll(top, 64, 1), bottom)
            poles = pieces // cols
            out[2 * pair * poles + pole, at : at + half] = even.astype(out.dtype)
            out[(2 * pair + 1) * poles + pole, at : at + half] = odd.astype(out.dtype)


def half_column(solved, ancestor, core):
    strips, half, size = ancestor.shape[1], ancestor.shape[2] // 2, ancestor.shape[3]
    at = pl.ds(pl.multiple_of(core * half, half), half)
    rows = solved[...]
    by_real = contract(rows, ancestor[0, :, at, :].reshape(strips * half, size), 0, 0)
    by_imag = contract(rows, ancestor[1, :, at, :].reshape(strips * half, size), 0, 0)
    return by_real[:size] - by_imag[size:], by_real[size:] + by_imag[:size]


def own_column_body(
    shift, weight, panel_h, panel_s, inverse, mine, ancestor, part, right, base
):
    size = part.shape[1]
    part[:size], part[size:] = half_column(mine, ancestor, lax.rem(lax.axis_index("row"), 2))
    solved = solve(panel_h[...], panel_s[...], shift, inverse)
    right[:size] = solved[:, :size]
    right[size:] = solved[:, size:]
    whole = inverse[0].astype(f32) + inverse[1].astype(f32)
    density = weight[0, 0] * whole[:, size:] + weight[0, 1] * whole[:, :size]
    first_device = (lax.axis_index("row") == 0) & (lax.axis_index("col") == 0)
    base[...] = jnp.where(first_device, density.T, 0.0)


def column_body(weight, other, ancestor, part, right, base, out, buffer, sems):
    size = part.shape[1]
    half = out.shape[1] // 2
    part_real, part_imag = half_column(other, ancestor, 1 - lax.rem(lax.axis_index("row"), 2))
    part_real += part[:size]
    part_imag += part[size:]
    stores = [
        pltpu.make_async_copy(buffer.at[:, rows], out.at[:, rows], sems.at[index])
        for index, rows in enumerate((pl.ds(0, half), pl.ds(half, half)))
    ]
    weight_real, weight_imag = weight[0, 0], weight[0, 1]
    density = -(weight_real * part_imag + weight_imag * part_real)
    fold(density, buffer, 0)
    stores[0].start()
    twin = -(weight_real * part_real - weight_imag * part_imag)
    high, low = split(jnp.concatenate([density, twin], axis=1))
    pivot = base[...] - (dot(high, right[...]) + dot(low, right[...]))
    fold(pivot, buffer, half)
    stores[1].start()
    for store in stores:
        store.wait()


def sums_body(parts, spread, rows):
    half, width = parts.shape[1] // 2, rows.shape[1]
    total = jnp.sum(parts[...].astype(f32), axis=0)
    rows[:half] = total[:half, :width]
    rows[half:] = total[:half, width:]
    spread[...] = jnp.broadcast_to(total[None, half:].astype(spread.dtype), spread.shape)


def pivot_body(parts, out):
    half = parts.shape[1]
    width = 64
    cols = out.shape[1] // width
    total = jnp.sum(parts[...].astype(f32).reshape(-1, cols, half, 128), axis=0)
    for index in range(128 // width):
        lanes = slice(index * width, (index + 1) * width)
        strips = [total[col][:, lanes] for col in range(cols)]
        out[index * half : (index + 1) * half] = jnp.concatenate(strips, axis=1)


def update_body(shift, panel_h, panel_s, mine, other, out):
    strips, rows = out.shape[0], out.shape[1] * out.shape[2]
    half = mine.shape[0] // strips
    group = 4
    top, bottom = ordered(mine[...], other[...])
    real, imag = couple(panel_h[...], panel_s[...], shift[0, 0], shift[0, 1])
    wide = jnp.concatenate(
        [jnp.concatenate([real, -imag], axis=1), jnp.concatenate([imag, real], axis=1)], axis=0
    )
    for first in range(0, strips, group):
        solved = jnp.concatenate(
            [
                member[strip * half : (strip + 1) * half]
                for strip in range(first, first + group)
                for member in (top, bottom)
            ],
            axis=0,
        )
        update = contract(solved, wide, 1, 1)
        out[first : first + group] = update.reshape((group,) + out.shape[1:])


def relay_body(up, down, from_below, from_above, below, above):
    more = up.shape[0]
    less = more // 3
    half = more - less
    below[:less] = down[half:]
    below[less:] = from_below[:half]
    above[:less] = up[:less]
    above[less:] = from_above[less:]


def schur_tiles(shift, pattern, update, members, buffer, out, sems):
    strips, count, share, size = out.shape[1:]
    pole = lax.axis_index("pole")
    row = lax.axis_index("row")
    shift_real, shift_imag = shift[0, 0], shift[0, 1]
    copies = []
    for member, start, length, step, first in members:
        at = lax.rem(pole + count + step, count)
        for index in range(length):
            strip = first + index
            mask = pattern[strip, row].astype(f32)
            margin = mask * member[start + index, share:].astype(f32)
            real = mask * member[start + index, :share].astype(f32) - shift_real * margin
            buffer[0, strip, at] = (real - update[strip, at, :, :size]).astype(bf16)
            buffer[1, strip, at] = (-shift_imag * margin - update[strip, at, :, size:]).astype(bf16)
        where = (slice(None), pl.ds(first, length), at)
        copies.append(pltpu.make_async_copy(buffer.at[where], out.at[where], sems.at[len(copies)]))
        copies[-1].start()
    for copy in copies:
        copy.wait()


def schur_first_body(shift, pattern, update, up, down, from_below, from_above, out, buffer, sems):
    more, less = up.shape[0], out.shape[1] - up.shape[0]
    members = (
        (up, 0, more, 0, 0),
        (down, more - less, less, 0, more),
        (from_below, 0, more, -1, 0),
        (from_above, 0, more, 1, less),
    )
    schur_tiles(shift, pattern, update, members, buffer, out, sems)


def schur_last_body(shift, pattern, update, below, above, begun, out, buffer, sems):
    del begun
    half = out.shape[1] // 2
    less = below.shape[0] - half
    members = (
        (below, 0, less, -1, 2 * half - less),
        (below, less, half, -2, 0),
        (above, 0, less, 1, 0),
        (above, less, half, 2, half),
    )
    schur_tiles(shift, pattern, update, members, buffer, out, sems)


def shards(
    front_h,
    front_s,
    panel_h,
    panel_s,
    pivot_h,
    pivot_s,
    pole_shift,
    pole_weight,
    pattern,
    ancestor_inverse,
):
    row_count = lax.axis_size("row")
    col_count = lax.axis_size("col")
    pole_count = lax.axis_size("pole")
    col_index = lax.axis_index("col")
    size = pivot_h.shape[0]
    width = size // col_count
    piece = size // pole_count
    half = width // 2
    neighbour = [(i, i ^ 1) for i in range(row_count)]

    quarters = 4
    share = width // quarters

    (sent,) = pl.pallas_call(
        pack_body,
        out_shape=[shape(row_count, width + 2 * share, size)],
        in_specs=[pl.BlockSpec(memory_space=pl.ANY)] * 4,
        out_specs=[pl.BlockSpec(memory_space=pl.ANY)],
        scratch_shapes=[
            pltpu.VMEM((2, width, size), bf16),
            pltpu.VMEM((2, share, row_count * size), bf16),
            pltpu.VMEM((row_count, width + 2 * share, size), bf16),
            pltpu.SemaphoreType.DMA((6,)),
        ],
        cost_estimate=pl.CostEstimate(flops=0, bytes_accessed=2**20, transcendentals=0),
        name="pack",
    )(panel_h, panel_s, front_h, front_s)
    received = lax.all_to_all(sent, "row", split_axis=0, concat_axis=0, tiled=True)

    (inverse,) = call(
        invert_body,
        [shape(2, size, 2 * size)],
        [pole_shift, pivot_h, pivot_s],
        6 * 4 * 3 * 2 * size**3,
        "pivot_inverse",
    )
    less = row_count // 4
    more = row_count - less
    mine, up, down = call(
        solve_body,
        [shape(row_count * half, 2 * size)] + [shape(more, 2 * share, size)] * 2,
        [pole_shift, received, inverse],
        2 * 8 * row_count * half * size * size,
        "solved_rows",
    )
    other = lax.ppermute(mine, "row", neighbour)
    ancestor = ancestor_inverse.reshape(2, row_count, width, size)
    part, right, base = call(
        own_column_body,
        [
            shape(2 * size, size, dtype=f32),
            shape(2 * size, size),
            shape(size, size, dtype=f32),
        ],
        [pole_shift, pole_weight, panel_h, panel_s, inverse, mine, ancestor],
        4 * row_count * width * size * size + 2 * 8 * size**3,
        "own_column",
    )
    folded = (col_count * pole_count, piece, 128)
    (both,) = pl.pallas_call(
        column_body,
        out_shape=[shape(*folded)],
        in_specs=[SMEM] + [VMEM] * 5,
        out_specs=[pl.BlockSpec(memory_space=pl.ANY)],
        scratch_shapes=[pltpu.VMEM(folded, bf16), pltpu.SemaphoreType.DMA((2,))],
        compiler_params=pltpu.CompilerParams(vmem_limit_bytes=16 * 2**20),
        cost_estimate=pl.CostEstimate(
            flops=4 * row_count * width * size * size, bytes_accessed=2 * 2**20, transcendentals=0
        ),
        name="column",
    )(pole_weight, other, ancestor, part, right, base)

    onward = [(i, (i + 1) % pole_count) for i in range(pole_count)]
    back = [(i, (i - 1) % pole_count) for i in range(pole_count)]
    up, down, both = lax.optimization_barrier((up, down, both))
    from_below = lax.ppermute(up, "pole", onward)
    from_above = lax.ppermute(down, "pole", back)

    both = lax.all_to_all(both, ("col", "pole"), split_axis=0, concat_axis=0, tiled=True)
    spread, rows_out = call(
        sums_body,
        [
            shape(row_count * col_count, piece // 2, 128),
            shape(piece, width, dtype=f32),
        ],
        [both],
        0,
        "sums",
    )
    below, above = call(
        relay_body,
        [shape(more, 2 * share, size)] * 2,
        [up, down, from_below, from_above],
        10**11,
        "relay",
    )
    below = lax.ppermute(below, "pole", onward)
    above = lax.ppermute(above, "pole", back)
    spread = lax.all_to_all(spread, ("row", "col"), split_axis=0, concat_axis=0, tiled=True)
    (pivot_out,) = call(pivot_body, [shape(piece, size, dtype=f32)], [spread], 0, "pivot")

    (update,) = call(
        update_body,
        [shape(row_count, quarters, share, 2 * size, dtype=f32)],
        [pole_shift, panel_h, panel_s, mine, other],
        8 * row_count * width * size * size,
        "update",
    )

    def tiles(body, ins, name, begun=()):
        tile = shape(2, row_count, quarters, share, size)
        return pl.pallas_call(
            body,
            out_shape=tile,
            in_specs=[SMEM] * 2 + [VMEM] * (len(ins) - 2) + [pl.BlockSpec(memory_space=pl.ANY)] * len(begun),
            out_specs=pl.BlockSpec(memory_space=pl.ANY),
            input_output_aliases={len(ins): 0} if begun else {},
            scratch_shapes=[pltpu.VMEM(tile.shape, bf16), pltpu.SemaphoreType.DMA((4,))],
            compiler_params=pltpu.CompilerParams(vmem_limit_bytes=16 * 2**20),
            cost_estimate=pl.CostEstimate(flops=0, bytes_accessed=3 * 2**20, transcendentals=0),
            name=name,
        )(*ins, *begun)

    fixed = [pole_shift, pattern, update]
    schur = tiles(schur_first_body, fixed + [up, down, from_below, from_above], "schur_first")
    schur = tiles(schur_last_body, fixed + [below, above], "schur_last", (schur,))
    return (schur.reshape(1, 2, row_count, 1, width, size), rows_out.T, pivot_out.T)


def solution(mesh):
    in_specs = (
        P(("row", "col"), None),
        P(("row", "col"), None),
        P("row", None),
        P("row", None),
        P(),
        P(),
        P("pole", None),
        P("pole", None),
        P(),
        P("pole", None, None, "col", None, "row"),
    )
    out_specs = (
        P("pole", None, None, "col", None, "row"),
        P(("row", "col"), "pole"),
        P(None, "pole"),
    )
    return jax.shard_map(shards, mesh=mesh, in_specs=in_specs, out_specs=out_specs, check_vma=False)
```

```python
import functools

import jax
import jax.numpy as jnp
from jax import lax
from jax.experimental import pallas as pl
from jax.experimental.pallas import tpu as pltpu
from jax.sharding import PartitionSpec as P

bf16 = jnp.bfloat16
f32 = jnp.float32
VMEM = pl.BlockSpec(memory_space=pltpu.VMEM)
SMEM = pl.BlockSpec(memory_space=pltpu.SMEM)


def call(body, outs, ins, flops, name, grant=16):
    moved = sum(x.size * x.dtype.itemsize for x in list(ins) + list(outs))
    return pl.pallas_call(
        body,
        out_shape=outs,
        in_specs=[VMEM] * len(ins),
        out_specs=[VMEM] * len(outs),
        compiler_params=pltpu.CompilerParams(vmem_limit_bytes=grant * 2**20),
        cost_estimate=pl.CostEstimate(flops=flops, bytes_accessed=moved, transcendentals=0),
        name=name,
    )(*ins)


def shape(*dims, dtype=bf16):
    return jax.ShapeDtypeStruct(dims, dtype)


def dot(left, right):
    return jnp.dot(left, right, preferred_element_type=f32)


def contract(left, right, axis_left, axis_right):
    dims = (((axis_left,), (axis_right,)), ((), ()))
    return lax.dot_general(left, right, dims, preferred_element_type=f32)


def split(value):
    high = value.astype(bf16)
    return high, (value - high.astype(f32)).astype(bf16)


def product(left, right):
    return dot(left[0], right[0]) + (dot(left[0], right[1]) + dot(left[1], right[0]))


def block(wide):
    size = wide.shape[1] // 2
    real, imag = wide[:, :size], wide[:, size:]
    return jnp.concatenate([wide, jnp.concatenate([-imag, real], axis=1)], axis=0)


def both_of(pair, form):
    return form(pair[0]), form(pair[1])


def couple(rows_h, rows_s, shift_real, shift_imag):
    margin = rows_s.astype(f32)
    real = (rows_h.astype(f32) - shift_real * margin).astype(bf16)
    imag = (-shift_imag * margin).astype(bf16)
    return real, imag


def invert_body(shift, pivot_h, pivot_s, inverse):
    size = pivot_h.shape[0]
    shift_real, shift_imag = shift[:, 0:1], shift[:, 1:2]
    margin = pivot_s[...].astype(f32)
    real = pivot_h[...].astype(f32) - shift_real * margin
    imag = -shift_imag * margin
    on_diag = lax.broadcasted_iota(jnp.int32, (size, size), 0) == lax.broadcasted_iota(
        jnp.int32, (size, size), 1
    )

    def scales(axis):
        diag_real = jnp.sum(jnp.where(on_diag, real, 0.0), axis=axis, keepdims=True)
        diag_imag = jnp.sum(jnp.where(on_diag, imag, 0.0), axis=axis, keepdims=True)
        denom = diag_real * diag_real + diag_imag * diag_imag
        return diag_real / denom, -diag_imag / denom

    col_real, col_imag = scales(0)
    err_real = jnp.where(on_diag, 0.0, imag * col_imag - real * col_real)
    err_imag = jnp.where(on_diag, 0.0, -(real * col_imag + imag * col_real))
    one = jnp.concatenate([jnp.where(on_diag, 1.0, 0.0), jnp.zeros((size, size), f32)], axis=1)
    err = jnp.concatenate([err_real, err_imag], axis=1)
    err_pair = split(err)
    err2 = product(err_pair, both_of(err_pair, block))
    err2_pair = split(err2)
    square = both_of(err2_pair, block)
    err3 = product(err_pair, square)
    err4_pair = split(product(err2_pair, square))
    first = one + err + err2 + err3
    fourth = both_of(err4_pair, block)
    second = first + product(split(first), fourth)
    err8_pair = split(product(err4_pair, fourth))
    total = second + product(split(second), both_of(err8_pair, block))
    sum_real, sum_imag = total[:, :size], total[:, size:]
    row_real, row_imag = scales(1)
    inv_real = row_real * sum_real - row_imag * sum_imag
    inv_imag = row_real * sum_imag + row_imag * sum_real
    inverse[0], inverse[1] = split(jnp.concatenate([inv_real, inv_imag], axis=1))


def solve(rows_h, rows_s, shift, inverse):
    coupling = jnp.concatenate(couple(rows_h, rows_s, shift[:, 0:1], shift[:, 1:2]), axis=1)
    return (dot(coupling, block(inverse[0])) + dot(coupling, block(inverse[1]))).astype(bf16)


def pack_body(panel_h, panel_s, front_h, front_s, out, panels, fronts, buffer, sems):
    half = panels.shape[1] // 2
    share, size = fronts.shape[1], out.shape[2]
    shares = panels.shape[1] // share
    at = pl.ds(pl.multiple_of(lax.axis_index("col") * 2 * half, 2 * half), 2 * half)
    of = pl.ds(pl.multiple_of(lax.rem(lax.axis_index("pole"), shares) * share, share), share)
    loads = [
        pltpu.make_async_copy(panel_h.at[at], panels.at[0], sems.at[0]),
        pltpu.make_async_copy(panel_s.at[at], panels.at[1], sems.at[1]),
        pltpu.make_async_copy(front_h.at[of], fronts.at[0], sems.at[2]),
        pltpu.make_async_copy(front_s.at[of], fronts.at[1], sems.at[3]),
    ]
    panel_rows, front_rows = pl.ds(0, 2 * half), pl.ds(2 * half, 2 * share)
    stores = [
        pltpu.make_async_copy(buffer.at[:, rows], out.at[:, rows], sems.at[4 + index])
        for index, rows in enumerate((panel_rows, front_rows))
    ]
    for load in loads:
        load.start()
    loads[0].wait()
    loads[1].wait()
    for row in range(out.shape[0]):
        core = row % 2
        for part in range(2):
            low = part * half
            buffer[row, low : low + half] = panels[part, core * half : (core + 1) * half]
    stores[0].start()
    loads[2].wait()
    loads[3].wait()
    for row in range(out.shape[0]):
        for part in range(2):
            low = 2 * half + part * share
            buffer[row, low : low + share] = fronts[part, :, row * size : (row + 1) * size]
    stores[1].start()
    for store in stores:
        store.wait()


def solve_body(shift, received, inverse, solved, up, down):
    strips, rows, size = received.shape
    half = solved.shape[0] // strips
    rows_h = received[:, :half].reshape(strips * half, size)
    rows_s = received[:, half : 2 * half].reshape(strips * half, size)
    solved[...] = solve(rows_h, rows_s, shift, inverse)
    up[...] = received[: up.shape[0], 2 * half :]
    down[...] = received[strips - down.shape[0] :, 2 * half :]


def ordered(mine, other):
    low = lax.rem(lax.axis_index("row"), 2) == 0
    return jnp.where(low, mine, other), jnp.where(low, other, mine)


def fold(member, out, at):
    pieces = out.shape[0]
    half = out.shape[1] // 2
    cols = 2 * member.shape[1] // 128
    low_lane = lax.broadcasted_iota(jnp.int32, (half, 128), 1) < 64
    for pole in range(pieces // cols):
        for pair in range(cols // 2):
            rows = pole * 2 * half
            top = member[rows : rows + half, pair * 128 : pair * 128 + 128]
            bottom = member[rows + half : rows + 2 * half, pair * 128 : pair * 128 + 128]
            even = jnp.where(low_lane, top, pltpu.roll(bottom, 64, 1))
            odd = jnp.where(low_lane, pltpu.roll(top, 64, 1), bottom)
            poles = pieces // cols
            out[2 * pair * poles + pole, at : at + half] = even.astype(out.dtype)
            out[(2 * pair + 1) * poles + pole, at : at + half] = odd.astype(out.dtype)


def half_column(solved, ancestor, core):
    strips, half, size = ancestor.shape[1], ancestor.shape[2] // 2, ancestor.shape[3]
    at = pl.ds(pl.multiple_of(core * half, half), half)
    rows = solved[...]
    by_real = contract(rows, ancestor[0, :, at, :].reshape(strips * half, size), 0, 0)
    by_imag = contract(rows, ancestor[1, :, at, :].reshape(strips * half, size), 0, 0)
    return by_real[:size] - by_imag[size:], by_real[size:] + by_imag[:size]


def own_column_body(
    shift, weight, panel_h, panel_s, inverse, mine, ancestor, part, right, base
):
    size = part.shape[1]
    part[:size], part[size:] = half_column(mine, ancestor, lax.rem(lax.axis_index("row"), 2))
    solved = solve(panel_h[...], panel_s[...], shift, inverse)
    right[:size] = solved[:, :size]
    right[size:] = solved[:, size:]
    whole = inverse[0].astype(f32) + inverse[1].astype(f32)
    density = weight[:, 0:1] * whole[:, size:] + weight[:, 1:2] * whole[:, :size]
    first_device = (lax.axis_index("row") == 0) & (lax.axis_index("col") == 0)
    base[...] = jnp.where(first_device, density.T, 0.0)


def column_body(weight, other, ancestor, part, right, base, out, buffer, sems):
    size = part.shape[1]
    half = out.shape[1] // 2
    part_real, part_imag = half_column(other, ancestor, 1 - lax.rem(lax.axis_index("row"), 2))
    part_real += part[:size]
    part_imag += part[size:]
    stores = [
        pltpu.make_async_copy(buffer.at[:, rows], out.at[:, rows], sems.at[index])
        for index, rows in enumerate((pl.ds(0, half), pl.ds(half, half)))
    ]
    weight_real, weight_imag = weight[:, 0:1], weight[:, 1:2]
    density = -(weight_real * part_imag + weight_imag * part_real)
    fold(density, buffer, 0)
    stores[0].start()
    twin = -(weight_real * part_real - weight_imag * part_imag)
    high, low = split(jnp.concatenate([density, twin], axis=1))
    pivot = base[...] - (dot(high, right[...]) + dot(low, right[...]))
    fold(pivot, buffer, half)
    stores[1].start()
    for store in stores:
        store.wait()


def sums_body(parts, spread, rows):
    half, width = parts.shape[1] // 2, rows.shape[1]
    total = jnp.sum(parts[...].astype(f32), axis=0)
    rows[:half] = total[:half, :width]
    rows[half:] = total[:half, width:]
    spread[...] = jnp.broadcast_to(total[None, half:].astype(spread.dtype), spread.shape)


def pivot_body(parts, out):
    half = parts.shape[1]
    width = 64
    cols = out.shape[1] // width
    total = jnp.sum(parts[...].astype(f32).reshape(-1, cols, half, 128), axis=0)
    for index in range(128 // width):
        lanes = slice(index * width, (index + 1) * width)
        strips = [total[col][:, lanes] for col in range(cols)]
        out[index * half : (index + 1) * half] = jnp.concatenate(strips, axis=1)


def update_body(shift, panel_h, panel_s, mine, other, out):
    strips, rows = out.shape[0], out.shape[1] * out.shape[2]
    half = mine.shape[0] // strips
    group = 4
    top, bottom = ordered(mine[...], other[...])
    real, imag = couple(panel_h[...], panel_s[...], shift[:, 0:1], shift[:, 1:2])
    wide = jnp.concatenate(
        [jnp.concatenate([real, -imag], axis=1), jnp.concatenate([imag, real], axis=1)], axis=0
    )
    for first in range(0, strips, group):
        solved = jnp.concatenate(
            [
                member[strip * half : (strip + 1) * half]
                for strip in range(first, first + group)
                for member in (top, bottom)
            ],
            axis=0,
        )
        update = contract(solved, wide, 1, 1)
        out[first : first + group] = update.reshape((group,) + out.shape[1:])


def relay_body(up, down, from_below, from_above, below, above):
    more = up.shape[0]
    less = more // 3
    half = more - less
    below[:less] = down[half:]
    below[less:] = from_below[:half]
    above[:less] = up[:less]
    above[less:] = from_above[less:]


def schur_tiles(shift, pattern, update, members, buffer, out, sems):
    strips, count, share, size = out.shape[1:]
    pole = lax.axis_index("pole")
    row = lax.axis_index("row")
    shift_real, shift_imag = shift[:, 0:1], shift[:, 1:2]
    copies = []
    for member, start, length, step, first in members:
        at = lax.rem(pole + count + step, count)
        for index in range(length):
            strip = first + index
            mask = pattern[strip, row].astype(f32)
            margin = mask * member[start + index, share:].astype(f32)
            real = mask * member[start + index, :share].astype(f32) - shift_real * margin
            buffer[0, strip, at] = (real - update[strip, at, :, :size]).astype(bf16)
            buffer[1, strip, at] = (-shift_imag * margin - update[strip, at, :, size:]).astype(bf16)
        where = (slice(None), pl.ds(first, length), at)
        copies.append(pltpu.make_async_copy(buffer.at[where], out.at[where], sems.at[len(copies)]))
        copies[-1].start()
    for copy in copies:
        copy.wait()


def schur_first_body(shift, pattern, update, up, down, from_below, from_above, out, buffer, sems):
    more, less = up.shape[0], out.shape[1] - up.shape[0]
    members = (
        (up, 0, more, 0, 0),
        (down, more - less, less, 0, more),
        (from_below, 0, more, -1, 0),
        (from_above, 0, more, 1, less),
    )
    schur_tiles(shift, pattern, update, members, buffer, out, sems)


def schur_last_body(shift, pattern, update, below, above, begun, out, buffer, sems):
    del begun
    half = out.shape[1] // 2
    less = below.shape[0] - half
    members = (
        (below, 0, less, -1, 2 * half - less),
        (below, less, half, -2, 0),
        (above, 0, less, 1, 0),
        (above, less, half, 2, half),
    )
    schur_tiles(shift, pattern, update, members, buffer, out, sems)


def shards(
    front_h,
    front_s,
    panel_h,
    panel_s,
    pivot_h,
    pivot_s,
    pole_shift,
    pole_weight,
    pattern,
    ancestor_inverse,
):
    row_count = lax.axis_size("row")
    col_count = lax.axis_size("col")
    pole_count = lax.axis_size("pole")
    col_index = lax.axis_index("col")
    size = pivot_h.shape[0]
    width = size // col_count
    piece = size // pole_count
    half = width // 2
    neighbour = [(i, i ^ 1) for i in range(row_count)]

    quarters = 4
    share = width // quarters

    (sent,) = pl.pallas_call(
        pack_body,
        out_shape=[shape(row_count, width + 2 * share, size)],
        in_specs=[pl.BlockSpec(memory_space=pl.ANY)] * 4,
        out_specs=[pl.BlockSpec(memory_space=pl.ANY)],
        scratch_shapes=[
            pltpu.VMEM((2, width, size), bf16),
            pltpu.VMEM((2, share, row_count * size), bf16),
            pltpu.VMEM((row_count, width + 2 * share, size), bf16),
            pltpu.SemaphoreType.DMA((6,)),
        ],
        cost_estimate=pl.CostEstimate(flops=0, bytes_accessed=2**20, transcendentals=0),
        name="pack",
    )(panel_h, panel_s, front_h, front_s)
    received = lax.all_to_all(sent, "row", split_axis=0, concat_axis=0, tiled=True)

    (inverse,) = call(
        invert_body,
        [shape(2, size, 2 * size)],
        [pole_shift, pivot_h, pivot_s],
        6 * 4 * 3 * 2 * size**3,
        "pivot_inverse",
    )
    less = row_count // 4
    more = row_count - less
    mine, up, down = call(
        solve_body,
        [shape(row_count * half, 2 * size)] + [shape(more, 2 * share, size)] * 2,
        [pole_shift, received, inverse],
        2 * 8 * row_count * half * size * size,
        "solved_rows",
    )
    other = lax.ppermute(mine, "row", neighbour)
    ancestor = ancestor_inverse.reshape(2, row_count, width, size)
    part, right, base = call(
        own_column_body,
        [
            shape(2 * size, size, dtype=f32),
            shape(2 * size, size),
            shape(size, size, dtype=f32),
        ],
        [pole_shift, pole_weight, panel_h, panel_s, inverse, mine, ancestor],
        4 * row_count * width * size * size + 2 * 8 * size**3,
        "own_column",
    )
    folded = (col_count * pole_count, piece, 128)
    (both,) = pl.pallas_call(
        column_body,
        out_shape=[shape(*folded)],
        in_specs=[VMEM] * 6,
        out_specs=[pl.BlockSpec(memory_space=pl.ANY)],
        scratch_shapes=[pltpu.VMEM(folded, bf16), pltpu.SemaphoreType.DMA((2,))],
        compiler_params=pltpu.CompilerParams(vmem_limit_bytes=16 * 2**20),
        cost_estimate=pl.CostEstimate(
            flops=4 * row_count * width * size * size, bytes_accessed=2 * 2**20, transcendentals=0
        ),
        name="column",
    )(pole_weight, other, ancestor, part, right, base)

    onward = [(i, (i + 1) % pole_count) for i in range(pole_count)]
    back = [(i, (i - 1) % pole_count) for i in range(pole_count)]
    up, down, both = lax.optimization_barrier((up, down, both))
    from_below = lax.ppermute(up, "pole", onward)
    from_above = lax.ppermute(down, "pole", back)

    both = lax.all_to_all(both, ("col", "pole"), split_axis=0, concat_axis=0, tiled=True)
    spread, rows_out = call(
        sums_body,
        [
            shape(row_count * col_count, piece // 2, 128),
            shape(piece, width, dtype=f32),
        ],
        [both],
        0,
        "sums",
    )
    below, above = call(
        relay_body,
        [shape(more, 2 * share, size)] * 2,
        [up, down, from_below, from_above],
        10**11,
        "relay",
    )
    below = lax.ppermute(below, "pole", onward)
    above = lax.ppermute(above, "pole", back)
    spread = lax.all_to_all(spread, ("row", "col"), split_axis=0, concat_axis=0, tiled=True)
    (pivot_out,) = call(pivot_body, [shape(piece, size, dtype=f32)], [spread], 0, "pivot")

    (update,) = call(
        update_body,
        [shape(row_count, quarters, share, 2 * size, dtype=f32)],
        [pole_shift, panel_h, panel_s, mine, other],
        8 * row_count * width * size * size,
        "update",
    )

    def tiles(body, ins, name, begun=()):
        tile = shape(2, row_count, quarters, share, size)
        return pl.pallas_call(
            body,
            out_shape=tile,
            in_specs=[VMEM, SMEM] + [VMEM] * (len(ins) - 2) + [pl.BlockSpec(memory_space=pl.ANY)] * len(begun),
            out_specs=pl.BlockSpec(memory_space=pl.ANY),
            input_output_aliases={len(ins): 0} if begun else {},
            scratch_shapes=[pltpu.VMEM(tile.shape, bf16), pltpu.SemaphoreType.DMA((4,))],
            compiler_params=pltpu.CompilerParams(vmem_limit_bytes=16 * 2**20),
            cost_estimate=pl.CostEstimate(flops=0, bytes_accessed=3 * 2**20, transcendentals=0),
            name=name,
        )(*ins, *begun)

    fixed = [pole_shift, pattern, update]
    schur = tiles(schur_first_body, fixed + [up, down, from_below, from_above], "schur_first")
    schur = tiles(schur_last_body, fixed + [below, above], "schur_last", (schur,))
    return (schur.reshape(1, 2, row_count, 1, width, size), rows_out.T, pivot_out.T)


def solution(mesh):
    in_specs = (
        P(("row", "col"), None),
        P(("row", "col"), None),
        P("row", None),
        P("row", None),
        P(),
        P(),
        P("pole", None),
        P("pole", None),
        P(),
        P("pole", None, None, "col", None, "row"),
    )
    out_specs = (
        P("pole", None, None, "col", None, "row"),
        P(("row", "col"), "pole"),
        P(None, "pole"),
    )
    return jax.shard_map(shards, mesh=mesh, in_specs=in_specs, out_specs=out_specs, check_vma=False)
```

```python
import functools

import jax
import jax.numpy as jnp
from jax import lax
from jax.experimental import pallas as pl
from jax.experimental.pallas import tpu as pltpu
from jax.sharding import PartitionSpec as P

bf16 = jnp.bfloat16
f32 = jnp.float32
VMEM = pl.BlockSpec(memory_space=pltpu.VMEM)


def call(body, outs, ins, flops, name, grant=16):
    moved = sum(x.size * x.dtype.itemsize for x in list(ins) + list(outs))
    return pl.pallas_call(
        body,
        out_shape=outs,
        in_specs=[VMEM] * len(ins),
        out_specs=[VMEM] * len(outs),
        compiler_params=pltpu.CompilerParams(vmem_limit_bytes=grant * 2**20),
        cost_estimate=pl.CostEstimate(flops=flops, bytes_accessed=moved, transcendentals=0),
        name=name,
    )(*ins)


def shape(*dims, dtype=bf16):
    return jax.ShapeDtypeStruct(dims, dtype)


def dot(left, right):
    return jnp.dot(left, right, preferred_element_type=f32)


def contract(left, right, axis_left, axis_right):
    dims = (((axis_left,), (axis_right,)), ((), ()))
    return lax.dot_general(left, right, dims, preferred_element_type=f32)


def split(value):
    high = value.astype(bf16)
    return high, (value - high.astype(f32)).astype(bf16)


def product(left, right):
    return dot(left[0], right[0]) + (dot(left[0], right[1]) + dot(left[1], right[0]))


def block(wide):
    size = wide.shape[1] // 2
    real, imag = wide[:, :size], wide[:, size:]
    return jnp.concatenate([wide, jnp.concatenate([-imag, real], axis=1)], axis=0)


def both_of(pair, form):
    return form(pair[0]), form(pair[1])


def couple(rows_h, rows_s, shift_real, shift_imag):
    margin = rows_s.astype(f32)
    real = (rows_h.astype(f32) - shift_real * margin).astype(bf16)
    imag = (-shift_imag * margin).astype(bf16)
    return real, imag


def invert_body(shift, pivot_h, pivot_s, inverse):
    size = pivot_h.shape[0]
    shift_real, shift_imag = shift[:, 0:1], shift[:, 1:2]
    margin = pivot_s[...].astype(f32)
    real = pivot_h[...].astype(f32) - shift_real * margin
    imag = -shift_imag * margin
    on_diag = lax.broadcasted_iota(jnp.int32, (size, size), 0) == lax.broadcasted_iota(
        jnp.int32, (size, size), 1
    )

    def scales(axis):
        diag_real = jnp.sum(jnp.where(on_diag, real, 0.0), axis=axis, keepdims=True)
        diag_imag = jnp.sum(jnp.where(on_diag, imag, 0.0), axis=axis, keepdims=True)
        denom = diag_real * diag_real + diag_imag * diag_imag
        return diag_real / denom, -diag_imag / denom

    col_real, col_imag = scales(0)
    err_real = jnp.where(on_diag, 0.0, imag * col_imag - real * col_real)
    err_imag = jnp.where(on_diag, 0.0, -(real * col_imag + imag * col_real))
    one = jnp.concatenate([jnp.where(on_diag, 1.0, 0.0), jnp.zeros((size, size), f32)], axis=1)
    err = jnp.concatenate([err_real, err_imag], axis=1)
    err_pair = split(err)
    err2 = product(err_pair, both_of(err_pair, block))
    err2_pair = split(err2)
    square = both_of(err2_pair, block)
    err3 = product(err_pair, square)
    err4_pair = split(product(err2_pair, square))
    first = one + err + err2 + err3
    fourth = both_of(err4_pair, block)
    second = first + product(split(first), fourth)
    err8_pair = split(product(err4_pair, fourth))
    total = second + product(split(second), both_of(err8_pair, block))
    sum_real, sum_imag = total[:, :size], total[:, size:]
    row_real, row_imag = scales(1)
    inv_real = row_real * sum_real - row_imag * sum_imag
    inv_imag = row_real * sum_imag + row_imag * sum_real
    inverse[0], inverse[1] = split(jnp.concatenate([inv_real, inv_imag], axis=1))


def solve(rows_h, rows_s, shift, inverse):
    coupling = jnp.concatenate(couple(rows_h, rows_s, shift[:, 0:1], shift[:, 1:2]), axis=1)
    return (dot(coupling, block(inverse[0])) + dot(coupling, block(inverse[1]))).astype(bf16)


def pack_body(panel_h, panel_s, front_h, front_s, out, panels, fronts, buffer, sems):
    half = panels.shape[1] // 2
    share, size = fronts.shape[1], out.shape[2]
    shares = panels.shape[1] // share
    at = pl.ds(pl.multiple_of(lax.axis_index("col") * 2 * half, 2 * half), 2 * half)
    of = pl.ds(pl.multiple_of(lax.rem(lax.axis_index("pole"), shares) * share, share), share)
    loads = [
        pltpu.make_async_copy(panel_h.at[at], panels.at[0], sems.at[0]),
        pltpu.make_async_copy(panel_s.at[at], panels.at[1], sems.at[1]),
        pltpu.make_async_copy(front_h.at[of], fronts.at[0], sems.at[2]),
        pltpu.make_async_copy(front_s.at[of], fronts.at[1], sems.at[3]),
    ]
    panel_rows, front_rows = pl.ds(0, 2 * half), pl.ds(2 * half, 2 * share)
    stores = [
        pltpu.make_async_copy(buffer.at[:, rows], out.at[:, rows], sems.at[4 + index])
        for index, rows in enumerate((panel_rows, front_rows))
    ]
    for load in loads:
        load.start()
    loads[0].wait()
    loads[1].wait()
    for row in range(out.shape[0]):
        core = row % 2
        for part in range(2):
            low = part * half
            buffer[row, low : low + half] = panels[part, core * half : (core + 1) * half]
    stores[0].start()
    loads[2].wait()
    loads[3].wait()
    for row in range(out.shape[0]):
        for part in range(2):
            low = 2 * half + part * share
            buffer[row, low : low + share] = fronts[part, :, row * size : (row + 1) * size]
    stores[1].start()
    for store in stores:
        store.wait()


def solve_body(shift, received, inverse, solved, up, down):
    strips, rows, size = received.shape
    half = solved.shape[0] // strips
    rows_h = received[:, :half].reshape(strips * half, size)
    rows_s = received[:, half : 2 * half].reshape(strips * half, size)
    solved[...] = solve(rows_h, rows_s, shift, inverse)
    up[...] = received[: up.shape[0], 2 * half :]
    down[...] = received[strips - down.shape[0] :, 2 * half :]


def ordered(mine, other):
    low = lax.rem(lax.axis_index("row"), 2) == 0
    return jnp.where(low, mine, other), jnp.where(low, other, mine)


def fold(member, out, at):
    pieces = out.shape[0]
    half = out.shape[1] // 2
    cols = 2 * member.shape[1] // 128
    low_lane = lax.broadcasted_iota(jnp.int32, (half, 128), 1) < 64
    for pole in range(pieces // cols):
        for pair in range(cols // 2):
            rows = pole * 2 * half
            top = member[rows : rows + half, pair * 128 : pair * 128 + 128]
            bottom = member[rows + half : rows + 2 * half, pair * 128 : pair * 128 + 128]
            even = jnp.where(low_lane, top, pltpu.roll(bottom, 64, 1))
            odd = jnp.where(low_lane, pltpu.roll(top, 64, 1), bottom)
            poles = pieces // cols
            out[2 * pair * poles + pole, at : at + half] = even.astype(out.dtype)
            out[(2 * pair + 1) * poles + pole, at : at + half] = odd.astype(out.dtype)


def half_column(solved, ancestor, core):
    strips, half, size = ancestor.shape[1], ancestor.shape[2] // 2, ancestor.shape[3]
    at = pl.ds(pl.multiple_of(core * half, half), half)
    rows = solved[...]
    by_real = contract(rows, ancestor[0, :, at, :].reshape(strips * half, size), 0, 0)
    by_imag = contract(rows, ancestor[1, :, at, :].reshape(strips * half, size), 0, 0)
    return by_real[:size] - by_imag[size:], by_real[size:] + by_imag[:size]


def own_column_body(
    shift, weight, panel_h, panel_s, inverse, mine, ancestor, part, right, base
):
    size = part.shape[1]
    part[:size], part[size:] = half_column(mine, ancestor, lax.rem(lax.axis_index("row"), 2))
    solved = solve(panel_h[...], panel_s[...], shift, inverse)
    right[:size] = solved[:, :size]
    right[size:] = solved[:, size:]
    whole = inverse[0].astype(f32) + inverse[1].astype(f32)
    density = weight[:, 0:1] * whole[:, size:] + weight[:, 1:2] * whole[:, :size]
    first_device = (lax.axis_index("row") == 0) & (lax.axis_index("col") == 0)
    base[...] = jnp.where(first_device, density.T, 0.0)


def column_body(weight, other, ancestor, part, right, base, out, buffer, sems):
    size = part.shape[1]
    half = out.shape[1] // 2
    part_real, part_imag = half_column(other, ancestor, 1 - lax.rem(lax.axis_index("row"), 2))
    part_real += part[:size]
    part_imag += part[size:]
    stores = [
        pltpu.make_async_copy(buffer.at[:, rows], out.at[:, rows], sems.at[index])
        for index, rows in enumerate((pl.ds(0, half), pl.ds(half, half)))
    ]
    weight_real, weight_imag = weight[:, 0:1], weight[:, 1:2]
    density = -(weight_real * part_imag + weight_imag * part_real)
    fold(density, buffer, 0)
    stores[0].start()
    twin = -(weight_real * part_real - weight_imag * part_imag)
    high, low = split(jnp.concatenate([density, twin], axis=1))
    pivot = base[...] - (dot(high, right[...]) + dot(low, right[...]))
    fold(pivot, buffer, half)
    stores[1].start()
    for store in stores:
        store.wait()


def sums_body(parts, spread, rows):
    half, width = parts.shape[1] // 2, rows.shape[1]
    total = jnp.sum(parts[...].astype(f32), axis=0)
    rows[:half] = total[:half, :width]
    rows[half:] = total[:half, width:]
    spread[...] = jnp.broadcast_to(total[None, half:].astype(spread.dtype), spread.shape)


def pivot_body(parts, out):
    half = parts.shape[1]
    width = 64
    cols = out.shape[1] // width
    total = jnp.sum(parts[...].astype(f32).reshape(-1, cols, half, 128), axis=0)
    for index in range(128 // width):
        lanes = slice(index * width, (index + 1) * width)
        strips = [total[col][:, lanes] for col in range(cols)]
        out[index * half : (index + 1) * half] = jnp.concatenate(strips, axis=1)


def update_body(shift, pattern, panel_h, panel_s, mine, other, out, mask):
    here = lax.broadcasted_iota(jnp.int32, pattern.shape, 1) == lax.axis_index("row")
    column = jnp.sum(jnp.where(here, pattern[...], 0).astype(f32), axis=1, keepdims=True)
    mask[...] = jnp.broadcast_to(column, mask.shape)
    strips, rows = out.shape[0], out.shape[1] * out.shape[2]
    half = mine.shape[0] // strips
    group = 4
    top, bottom = ordered(mine[...], other[...])
    real, imag = couple(panel_h[...], panel_s[...], shift[:, 0:1], shift[:, 1:2])
    wide = jnp.concatenate(
        [jnp.concatenate([real, -imag], axis=1), jnp.concatenate([imag, real], axis=1)], axis=0
    )
    for first in range(0, strips, group):
        solved = jnp.concatenate(
            [
                member[strip * half : (strip + 1) * half]
                for strip in range(first, first + group)
                for member in (top, bottom)
            ],
            axis=0,
        )
        update = contract(solved, wide, 1, 1)
        out[first : first + group] = update.reshape((group,) + out.shape[1:])


def relay_body(up, down, from_below, from_above, below, above):
    more = up.shape[0]
    less = more // 3
    half = more - less
    below[:less] = down[half:]
    below[less:] = from_below[:half]
    above[:less] = up[:less]
    above[less:] = from_above[less:]


def schur_tiles(shift, mask, update, members, buffer, out, sems):
    strips, count, share, size = out.shape[1:]
    pole = lax.axis_index("pole")
    shift_real, shift_imag = shift[:, 0:1], shift[:, 1:2]
    copies = []
    for member, start, length, step, first in members:
        at = lax.rem(pole + count + step, count)
        for index in range(length):
            strip = first + index
            here = mask[strip : strip + 1, :]
            margin = here * member[start + index, share:].astype(f32)
            real = here * member[start + index, :share].astype(f32) - shift_real * margin
            buffer[0, strip, at] = (real - update[strip, at, :, :size]).astype(bf16)
            buffer[1, strip, at] = (-shift_imag * margin - update[strip, at, :, size:]).astype(bf16)
        where = (slice(None), pl.ds(first, length), at)
        copies.append(pltpu.make_async_copy(buffer.at[where], out.at[where], sems.at[len(copies)]))
        copies[-1].start()
    for copy in copies:
        copy.wait()


def schur_first_body(shift, mask, update, up, down, from_below, from_above, out, buffer, sems):
    more, less = up.shape[0], out.shape[1] - up.shape[0]
    members = (
        (up, 0, more, 0, 0),
        (down, more - less, less, 0, more),
        (from_below, 0, more, -1, 0),
        (from_above, 0, more, 1, less),
    )
    schur_tiles(shift, mask, update, members, buffer, out, sems)


def schur_last_body(shift, mask, update, below, above, begun, out, buffer, sems):
    del begun
    half = out.shape[1] // 2
    less = below.shape[0] - half
    members = (
        (below, 0, less, -1, 2 * half - less),
        (below, less, half, -2, 0),
        (above, 0, less, 1, 0),
        (above, less, half, 2, half),
    )
    schur_tiles(shift, mask, update, members, buffer, out, sems)


def shards(
    front_h,
    front_s,
    panel_h,
    panel_s,
    pivot_h,
    pivot_s,
    pole_shift,
    pole_weight,
    pattern,
    ancestor_inverse,
):
    row_count = lax.axis_size("row")
    col_count = lax.axis_size("col")
    pole_count = lax.axis_size("pole")
    col_index = lax.axis_index("col")
    size = pivot_h.shape[0]
    width = size // col_count
    piece = size // pole_count
    half = width // 2
    neighbour = [(i, i ^ 1) for i in range(row_count)]

    quarters = 4
    share = width // quarters

    (sent,) = pl.pallas_call(
        pack_body,
        out_shape=[shape(row_count, width + 2 * share, size)],
        in_specs=[pl.BlockSpec(memory_space=pl.ANY)] * 4,
        out_specs=[pl.BlockSpec(memory_space=pl.ANY)],
        scratch_shapes=[
            pltpu.VMEM((2, width, size), bf16),
            pltpu.VMEM((2, share, row_count * size), bf16),
            pltpu.VMEM((row_count, width + 2 * share, size), bf16),
            pltpu.SemaphoreType.DMA((6,)),
        ],
        cost_estimate=pl.CostEstimate(flops=0, bytes_accessed=2**20, transcendentals=0),
        name="pack",
    )(panel_h, panel_s, front_h, front_s)
    received = lax.all_to_all(sent, "row", split_axis=0, concat_axis=0, tiled=True)

    (inverse,) = call(
        invert_body,
        [shape(2, size, 2 * size)],
        [pole_shift, pivot_h, pivot_s],
        6 * 4 * 3 * 2 * size**3,
        "pivot_inverse",
    )
    less = row_count // 4
    more = row_count - less
    mine, up, down = call(
        solve_body,
        [shape(row_count * half, 2 * size)] + [shape(more, 2 * share, size)] * 2,
        [pole_shift, received, inverse],
        2 * 8 * row_count * half * size * size,
        "solved_rows",
    )
    other = lax.ppermute(mine, "row", neighbour)
    ancestor = ancestor_inverse.reshape(2, row_count, width, size)
    part, right, base = call(
        own_column_body,
        [
            shape(2 * size, size, dtype=f32),
            shape(2 * size, size),
            shape(size, size, dtype=f32),
        ],
        [pole_shift, pole_weight, panel_h, panel_s, inverse, mine, ancestor],
        4 * row_count * width * size * size + 2 * 8 * size**3,
        "own_column",
    )
    folded = (col_count * pole_count, piece, 128)
    (both,) = pl.pallas_call(
        column_body,
        out_shape=[shape(*folded)],
        in_specs=[VMEM] * 6,
        out_specs=[pl.BlockSpec(memory_space=pl.ANY)],
        scratch_shapes=[pltpu.VMEM(folded, bf16), pltpu.SemaphoreType.DMA((2,))],
        compiler_params=pltpu.CompilerParams(vmem_limit_bytes=16 * 2**20),
        cost_estimate=pl.CostEstimate(
            flops=4 * row_count * width * size * size, bytes_accessed=2 * 2**20, transcendentals=0
        ),
        name="column",
    )(pole_weight, other, ancestor, part, right, base)

    onward = [(i, (i + 1) % pole_count) for i in range(pole_count)]
    back = [(i, (i - 1) % pole_count) for i in range(pole_count)]
    up, down, both = lax.optimization_barrier((up, down, both))
    from_below = lax.ppermute(up, "pole", onward)
    from_above = lax.ppermute(down, "pole", back)

    both = lax.all_to_all(both, ("col", "pole"), split_axis=0, concat_axis=0, tiled=True)
    spread, rows_out = call(
        sums_body,
        [
            shape(row_count * col_count, piece // 2, 128),
            shape(piece, width, dtype=f32),
        ],
        [both],
        0,
        "sums",
    )
    below, above = call(
        relay_body,
        [shape(more, 2 * share, size)] * 2,
        [up, down, from_below, from_above],
        10**11,
        "relay",
    )
    below = lax.ppermute(below, "pole", onward)
    above = lax.ppermute(above, "pole", back)
    spread = lax.all_to_all(spread, ("row", "col"), split_axis=0, concat_axis=0, tiled=True)
    (pivot_out,) = call(pivot_body, [shape(piece, size, dtype=f32)], [spread], 0, "pivot")

    update, mask = call(
        update_body,
        [
            shape(row_count, quarters, share, 2 * size, dtype=f32),
            shape(row_count, size, dtype=f32),
        ],
        [pole_shift, pattern, panel_h, panel_s, mine, other],
        8 * row_count * width * size * size,
        "update",
    )

    def tiles(body, ins, name, begun=()):
        tile = shape(2, row_count, quarters, share, size)
        return pl.pallas_call(
            body,
            out_shape=tile,
            in_specs=[VMEM] * len(ins) + [pl.BlockSpec(memory_space=pl.ANY)] * len(begun),
            out_specs=pl.BlockSpec(memory_space=pl.ANY),
            input_output_aliases={len(ins): 0} if begun else {},
            scratch_shapes=[pltpu.VMEM(tile.shape, bf16), pltpu.SemaphoreType.DMA((4,))],
            compiler_params=pltpu.CompilerParams(vmem_limit_bytes=16 * 2**20),
            cost_estimate=pl.CostEstimate(flops=0, bytes_accessed=3 * 2**20, transcendentals=0),
            name=name,
        )(*ins, *begun)

    fixed = [pole_shift, mask, update]
    schur = tiles(schur_first_body, fixed + [up, down, from_below, from_above], "schur_first")
    schur = tiles(schur_last_body, fixed + [below, above], "schur_last", (schur,))
    return (schur.reshape(1, 2, row_count, 1, width, size), rows_out.T, pivot_out.T)


def solution(mesh):
    in_specs = (
        P(("row", "col"), None),
        P(("row", "col"), None),
        P("row", None),
        P("row", None),
        P(),
        P(),
        P("pole", None),
        P("pole", None),
        P(),
        P("pole", None, None, "col", None, "row"),
    )
    out_specs = (
        P("pole", None, None, "col", None, "row"),
        P(("row", "col"), "pole"),
        P(None, "pole"),
    )
    return jax.shard_map(shards, mesh=mesh, in_specs=in_specs, out_specs=out_specs, check_vma=False)
```

```python
import functools

import jax
import jax.numpy as jnp
from jax import lax
from jax.experimental import pallas as pl
from jax.experimental.pallas import tpu as pltpu
from jax.sharding import PartitionSpec as P

bf16 = jnp.bfloat16
f32 = jnp.float32
VMEM = pl.BlockSpec(memory_space=pltpu.VMEM)


def call(body, outs, ins, flops, name, grant=16):
    moved = sum(x.size * x.dtype.itemsize for x in list(ins) + list(outs))
    return pl.pallas_call(
        body,
        out_shape=outs,
        in_specs=[VMEM] * len(ins),
        out_specs=[VMEM] * len(outs),
        compiler_params=pltpu.CompilerParams(vmem_limit_bytes=grant * 2**20),
        cost_estimate=pl.CostEstimate(flops=flops, bytes_accessed=moved, transcendentals=0),
        name=name,
    )(*ins)


def shape(*dims, dtype=bf16):
    return jax.ShapeDtypeStruct(dims, dtype)


def dot(left, right):
    return jnp.dot(left, right, preferred_element_type=f32)


def contract(left, right, axis_left, axis_right):
    dims = (((axis_left,), (axis_right,)), ((), ()))
    return lax.dot_general(left, right, dims, preferred_element_type=f32)


def split(value):
    high = value.astype(bf16)
    return high, (value - high.astype(f32)).astype(bf16)


def product(left, right):
    return dot(left[0], right[0]) + (dot(left[0], right[1]) + dot(left[1], right[0]))


def block(wide):
    size = wide.shape[1] // 2
    real, imag = wide[:, :size], wide[:, size:]
    return jnp.concatenate([wide, jnp.concatenate([-imag, real], axis=1)], axis=0)


def both_of(pair, form):
    return form(pair[0]), form(pair[1])


def couple(rows_h, rows_s, shift_real, shift_imag):
    margin = rows_s.astype(f32)
    real = (rows_h.astype(f32) - shift_real * margin).astype(bf16)
    imag = (-shift_imag * margin).astype(bf16)
    return real, imag


def invert_body(shift, pivot_h, pivot_s, inverse):
    size = pivot_h.shape[0]
    shift_real, shift_imag = shift[:, 0:1], shift[:, 1:2]
    margin = pivot_s[...].astype(f32)
    real = pivot_h[...].astype(f32) - shift_real * margin
    imag = -shift_imag * margin
    on_diag = lax.broadcasted_iota(jnp.int32, (size, size), 0) == lax.broadcasted_iota(
        jnp.int32, (size, size), 1
    )

    def scales(axis):
        diag_real = jnp.sum(jnp.where(on_diag, real, 0.0), axis=axis, keepdims=True)
        diag_imag = jnp.sum(jnp.where(on_diag, imag, 0.0), axis=axis, keepdims=True)
        denom = diag_real * diag_real + diag_imag * diag_imag
        return diag_real / denom, -diag_imag / denom

    col_real, col_imag = scales(0)
    err_real = jnp.where(on_diag, 0.0, imag * col_imag - real * col_real)
    err_imag = jnp.where(on_diag, 0.0, -(real * col_imag + imag * col_real))
    one = jnp.concatenate([jnp.where(on_diag, 1.0, 0.0), jnp.zeros((size, size), f32)], axis=1)
    err = jnp.concatenate([err_real, err_imag], axis=1)
    err_pair = split(err)
    err2 = product(err_pair, both_of(err_pair, block))
    err2_pair = split(err2)
    square = both_of(err2_pair, block)
    err3 = product(err_pair, square)
    err4_pair = split(product(err2_pair, square))
    first = one + err + err2 + err3
    fourth = both_of(err4_pair, block)
    second = first + product(split(first), fourth)
    err8_pair = split(product(err4_pair, fourth))
    total = second + product(split(second), both_of(err8_pair, block))
    sum_real, sum_imag = total[:, :size], total[:, size:]
    row_real, row_imag = scales(1)
    inv_real = row_real * sum_real - row_imag * sum_imag
    inv_imag = row_real * sum_imag + row_imag * sum_real
    inverse[0], inverse[1] = split(jnp.concatenate([inv_real, inv_imag], axis=1))


def solve(rows_h, rows_s, shift, inverse):
    coupling = jnp.concatenate(couple(rows_h, rows_s, shift[:, 0:1], shift[:, 1:2]), axis=1)
    return (dot(coupling, block(inverse[0])) + dot(coupling, block(inverse[1]))).astype(bf16)


def pack_body(panel_h, panel_s, front_h, front_s, out, panels, fronts, buffer, sems):
    half = panels.shape[1] // 2
    share, size = fronts.shape[1], out.shape[2]
    shares = panels.shape[1] // share
    at = pl.ds(pl.multiple_of(lax.axis_index("col") * 2 * half, 2 * half), 2 * half)
    of = pl.ds(pl.multiple_of(lax.rem(lax.axis_index("pole"), shares) * share, share), share)
    loads = [
        pltpu.make_async_copy(panel_h.at[at], panels.at[0], sems.at[0]),
        pltpu.make_async_copy(panel_s.at[at], panels.at[1], sems.at[1]),
        pltpu.make_async_copy(front_h.at[of], fronts.at[0], sems.at[2]),
        pltpu.make_async_copy(front_s.at[of], fronts.at[1], sems.at[3]),
    ]
    panel_rows, front_rows = pl.ds(0, 2 * half), pl.ds(2 * half, 2 * share)
    stores = [
        pltpu.make_async_copy(buffer.at[:, rows], out.at[:, rows], sems.at[4 + index])
        for index, rows in enumerate((panel_rows, front_rows))
    ]
    for load in loads:
        load.start()
    loads[0].wait()
    loads[1].wait()
    for row in range(out.shape[0]):
        core = row % 2
        for part in range(2):
            low = part * half
            buffer[row, low : low + half] = panels[part, core * half : (core + 1) * half]
    stores[0].start()
    loads[2].wait()
    loads[3].wait()
    for row in range(out.shape[0]):
        for part in range(2):
            low = 2 * half + part * share
            buffer[row, low : low + share] = fronts[part, :, row * size : (row + 1) * size]
    stores[1].start()
    for store in stores:
        store.wait()


def solve_body(shift, received, inverse, solved, up, down):
    strips, rows, size = received.shape
    half = solved.shape[0] // strips
    rows_h = received[:, :half].reshape(strips * half, size)
    rows_s = received[:, half : 2 * half].reshape(strips * half, size)
    solved[...] = solve(rows_h, rows_s, shift, inverse)
    up[...] = received[: up.shape[0], 2 * half :]
    down[...] = received[strips - down.shape[0] :, 2 * half :]


def ordered(mine, other):
    low = lax.rem(lax.axis_index("row"), 2) == 0
    return jnp.where(low, mine, other), jnp.where(low, other, mine)


def fold(member, out, at):
    pieces = out.shape[0]
    half = out.shape[1] // 2
    cols = 2 * member.shape[1] // 128
    low_lane = lax.broadcasted_iota(jnp.int32, (half, 128), 1) < 64
    for pole in range(pieces // cols):
        for pair in range(cols // 2):
            rows = pole * 2 * half
            top = member[rows : rows + half, pair * 128 : pair * 128 + 128]
            bottom = member[rows + half : rows + 2 * half, pair * 128 : pair * 128 + 128]
            even = jnp.where(low_lane, top, pltpu.roll(bottom, 64, 1))
            odd = jnp.where(low_lane, pltpu.roll(top, 64, 1), bottom)
            poles = pieces // cols
            out[2 * pair * poles + pole, at : at + half] = even.astype(out.dtype)
            out[(2 * pair + 1) * poles + pole, at : at + half] = odd.astype(out.dtype)


def half_column(solved, ancestor, core):
    strips, half, size = ancestor.shape[1], ancestor.shape[2] // 2, ancestor.shape[3]
    at = pl.ds(pl.multiple_of(core * half, half), half)
    rows = solved[...]
    by_real = contract(rows, ancestor[0, :, at, :].reshape(strips * half, size), 0, 0)
    by_imag = contract(rows, ancestor[1, :, at, :].reshape(strips * half, size), 0, 0)
    return by_real[:size] - by_imag[size:], by_real[size:] + by_imag[:size]


def own_column_body(
    shift, weight, panel_h, panel_s, inverse, mine, ancestor, part, right, base
):
    size = part.shape[1]
    part[:size], part[size:] = half_column(mine, ancestor, lax.rem(lax.axis_index("row"), 2))
    solved = solve(panel_h[...], panel_s[...], shift, inverse)
    right[:size] = solved[:, :size]
    right[size:] = solved[:, size:]
    whole = inverse[0].astype(f32) + inverse[1].astype(f32)
    density = weight[:, 0:1] * whole[:, size:] + weight[:, 1:2] * whole[:, :size]
    first_device = (lax.axis_index("row") == 0) & (lax.axis_index("col") == 0)
    base[...] = jnp.where(first_device, density.T, 0.0)


def column_body(weight, other, ancestor, part, right, base, out, buffer, sems):
    size = part.shape[1]
    half = out.shape[1] // 2
    part_real, part_imag = half_column(other, ancestor, 1 - lax.rem(lax.axis_index("row"), 2))
    part_real += part[:size]
    part_imag += part[size:]
    stores = [
        pltpu.make_async_copy(buffer.at[:, rows], out.at[:, rows], sems.at[index])
        for index, rows in enumerate((pl.ds(0, half), pl.ds(half, half)))
    ]
    weight_real, weight_imag = weight[:, 0:1], weight[:, 1:2]
    density = -(weight_real * part_imag + weight_imag * part_real)
    fold(density, buffer, 0)
    stores[0].start()
    twin = -(weight_real * part_real - weight_imag * part_imag)
    high, low = split(jnp.concatenate([density, twin], axis=1))
    pivot = base[...] - (dot(high, right[...]) + dot(low, right[...]))
    fold(pivot, buffer, half)
    stores[1].start()
    for store in stores:
        store.wait()


def sums_body(parts, spread, rows):
    half, width = parts.shape[1] // 2, rows.shape[1]
    total = jnp.sum(parts[...].astype(f32), axis=0)
    rows[:half] = total[:half, :width]
    rows[half:] = total[:half, width:]
    spread[...] = jnp.broadcast_to(total[None, half:].astype(spread.dtype), spread.shape)


def pivot_body(parts, out):
    half = parts.shape[1]
    width = 64
    cols = out.shape[1] // width
    total = jnp.sum(parts[...].astype(f32).reshape(-1, cols, half, 128), axis=0)
    for index in range(128 // width):
        lanes = slice(index * width, (index + 1) * width)
        strips = [total[col][:, lanes] for col in range(cols)]
        out[index * half : (index + 1) * half] = jnp.concatenate(strips, axis=1)


def update_body(shift, pattern, panel_h, panel_s, mine, other, out, mask):
    here = lax.broadcasted_iota(jnp.int32, pattern.shape, 1) == lax.axis_index("row")
    column = jnp.sum(jnp.where(here, pattern[...], 0).astype(f32), axis=1, keepdims=True)
    mask[...] = jnp.broadcast_to(column, mask.shape)
    strips, rows = out.shape[0], out.shape[1] * out.shape[2]
    half = mine.shape[0] // strips
    group = 4
    top, bottom = ordered(mine[...], other[...])
    real, imag = couple(panel_h[...], panel_s[...], shift[:, 0:1], shift[:, 1:2])
    wide = jnp.concatenate(
        [jnp.concatenate([real, -imag], axis=1), jnp.concatenate([imag, real], axis=1)], axis=0
    )
    for first in range(0, strips, group):
        solved = jnp.concatenate(
            [
                member[strip * half : (strip + 1) * half]
                for strip in range(first, first + group)
                for member in (top, bottom)
            ],
            axis=0,
        )
        update = contract(solved, wide, 1, 1)
        out[first : first + group] = update.reshape((group,) + out.shape[1:])


def relay_body(up, down, from_below, from_above, below, above):
    more = up.shape[0]
    less = below.shape[0] - (below.shape[0] + more) // 3
    half = below.shape[0] - less
    below[:less] = down[more - less :]
    below[less:] = from_below[:half]
    above[:less] = up[:less]
    above[less:] = from_above[more - half :]


def schur_tiles(shift, mask, update, members, buffer, out, sems):
    strips, count, share, size = out.shape[1:]
    pole = lax.axis_index("pole")
    shift_real, shift_imag = shift[:, 0:1], shift[:, 1:2]
    copies = []
    for member, start, length, step, first in members:
        at = lax.rem(pole + count + step, count)
        for index in range(length):
            strip = first + index
            here = mask[strip : strip + 1, :]
            margin = here * member[start + index, share:].astype(f32)
            real = here * member[start + index, :share].astype(f32) - shift_real * margin
            buffer[0, strip, at] = (real - update[strip, at, :, :size]).astype(bf16)
            buffer[1, strip, at] = (-shift_imag * margin - update[strip, at, :, size:]).astype(bf16)
        where = (slice(None), pl.ds(first, length), at)
        copies.append(pltpu.make_async_copy(buffer.at[where], out.at[where], sems.at[len(copies)]))
        copies[-1].start()
    for copy in copies:
        copy.wait()


def schur_first_body(shift, mask, update, up, down, from_below, from_above, out, buffer, sems):
    more, less = up.shape[0], out.shape[1] - up.shape[0]
    members = (
        (up, 0, more, 0, 0),
        (down, more - less, less, 0, more),
        (from_below, 0, more, -1, 0),
        (from_above, 0, more, 1, less),
    )
    schur_tiles(shift, mask, update, members, buffer, out, sems)


def schur_last_body(shift, mask, update, below, above, begun, out, buffer, sems):
    del begun
    half = out.shape[1] // 2
    less = below.shape[0] - half
    members = (
        (below, 0, less, -1, 2 * half - less),
        (below, less, half, -2, 0),
        (above, 0, less, 1, 0),
        (above, less, half, 2, half),
    )
    schur_tiles(shift, mask, update, members, buffer, out, sems)


def shards(
    front_h,
    front_s,
    panel_h,
    panel_s,
    pivot_h,
    pivot_s,
    pole_shift,
    pole_weight,
    pattern,
    ancestor_inverse,
):
    row_count = lax.axis_size("row")
    col_count = lax.axis_size("col")
    pole_count = lax.axis_size("pole")
    col_index = lax.axis_index("col")
    size = pivot_h.shape[0]
    width = size // col_count
    piece = size // pole_count
    half = width // 2
    neighbour = [(i, i ^ 1) for i in range(row_count)]

    quarters = 4
    share = width // quarters

    (sent,) = pl.pallas_call(
        pack_body,
        out_shape=[shape(row_count, width + 2 * share, size)],
        in_specs=[pl.BlockSpec(memory_space=pl.ANY)] * 4,
        out_specs=[pl.BlockSpec(memory_space=pl.ANY)],
        scratch_shapes=[
            pltpu.VMEM((2, width, size), bf16),
            pltpu.VMEM((2, share, row_count * size), bf16),
            pltpu.VMEM((row_count, width + 2 * share, size), bf16),
            pltpu.SemaphoreType.DMA((6,)),
        ],
        cost_estimate=pl.CostEstimate(flops=0, bytes_accessed=2**20, transcendentals=0),
        name="pack",
    )(panel_h, panel_s, front_h, front_s)
    received = lax.all_to_all(sent, "row", split_axis=0, concat_axis=0, tiled=True)

    (inverse,) = call(
        invert_body,
        [shape(2, size, 2 * size)],
        [pole_shift, pivot_h, pivot_s],
        6 * 4 * 3 * 2 * size**3,
        "pivot_inverse",
    )
    less = 3 * row_count // 8
    more = row_count - less
    mine, up, down = call(
        solve_body,
        [shape(row_count * half, 2 * size)] + [shape(more, 2 * share, size)] * 2,
        [pole_shift, received, inverse],
        2 * 8 * row_count * half * size * size,
        "solved_rows",
    )
    other = lax.ppermute(mine, "row", neighbour)
    ancestor = ancestor_inverse.reshape(2, row_count, width, size)
    part, right, base = call(
        own_column_body,
        [
            shape(2 * size, size, dtype=f32),
            shape(2 * size, size),
            shape(size, size, dtype=f32),
        ],
        [pole_shift, pole_weight, panel_h, panel_s, inverse, mine, ancestor],
        4 * row_count * width * size * size + 2 * 8 * size**3,
        "own_column",
    )
    folded = (col_count * pole_count, piece, 128)
    (both,) = pl.pallas_call(
        column_body,
        out_shape=[shape(*folded)],
        in_specs=[VMEM] * 6,
        out_specs=[pl.BlockSpec(memory_space=pl.ANY)],
        scratch_shapes=[pltpu.VMEM(folded, bf16), pltpu.SemaphoreType.DMA((2,))],
        compiler_params=pltpu.CompilerParams(vmem_limit_bytes=16 * 2**20),
        cost_estimate=pl.CostEstimate(
            flops=4 * row_count * width * size * size, bytes_accessed=2 * 2**20, transcendentals=0
        ),
        name="column",
    )(pole_weight, other, ancestor, part, right, base)

    onward = [(i, (i + 1) % pole_count) for i in range(pole_count)]
    back = [(i, (i - 1) % pole_count) for i in range(pole_count)]
    up, down, both = lax.optimization_barrier((up, down, both))
    from_below = lax.ppermute(up, "pole", onward)
    from_above = lax.ppermute(down, "pole", back)

    both = lax.all_to_all(both, ("col", "pole"), split_axis=0, concat_axis=0, tiled=True)
    spread, rows_out = call(
        sums_body,
        [
            shape(row_count * col_count, piece // 2, 128),
            shape(piece, width, dtype=f32),
        ],
        [both],
        0,
        "sums",
    )
    below, above = call(
        relay_body,
        [shape(less + row_count // 2, 2 * share, size)] * 2,
        [up, down, from_below, from_above],
        10**11,
        "relay",
    )
    below = lax.ppermute(below, "pole", onward)
    above = lax.ppermute(above, "pole", back)
    spread = lax.all_to_all(spread, ("row", "col"), split_axis=0, concat_axis=0, tiled=True)
    (pivot_out,) = call(pivot_body, [shape(piece, size, dtype=f32)], [spread], 0, "pivot")

    update, mask = call(
        update_body,
        [
            shape(row_count, quarters, share, 2 * size, dtype=f32),
            shape(row_count, size, dtype=f32),
        ],
        [pole_shift, pattern, panel_h, panel_s, mine, other],
        8 * row_count * width * size * size,
        "update",
    )

    def tiles(body, ins, name, begun=()):
        tile = shape(2, row_count, quarters, share, size)
        return pl.pallas_call(
            body,
            out_shape=tile,
            in_specs=[VMEM] * len(ins) + [pl.BlockSpec(memory_space=pl.ANY)] * len(begun),
            out_specs=pl.BlockSpec(memory_space=pl.ANY),
            input_output_aliases={len(ins): 0} if begun else {},
            scratch_shapes=[pltpu.VMEM(tile.shape, bf16), pltpu.SemaphoreType.DMA((4,))],
            compiler_params=pltpu.CompilerParams(vmem_limit_bytes=16 * 2**20),
            cost_estimate=pl.CostEstimate(flops=0, bytes_accessed=3 * 2**20, transcendentals=0),
            name=name,
        )(*ins, *begun)

    fixed = [pole_shift, mask, update]
    schur = tiles(schur_first_body, fixed + [up, down, from_below, from_above], "schur_first")
    schur = tiles(schur_last_body, fixed + [below, above], "schur_last", (schur,))
    return (schur.reshape(1, 2, row_count, 1, width, size), rows_out.T, pivot_out.T)


def solution(mesh):
    in_specs = (
        P(("row", "col"), None),
        P(("row", "col"), None),
        P("row", None),
        P("row", None),
        P(),
        P(),
        P("pole", None),
        P("pole", None),
        P(),
        P("pole", None, None, "col", None, "row"),
    )
    out_specs = (
        P("pole", None, None, "col", None, "row"),
        P(("row", "col"), "pole"),
        P(None, "pole"),
    )
    return jax.shard_map(shards, mesh=mesh, in_specs=in_specs, out_specs=out_specs, check_vma=False)
```

```python
import functools

import jax
import jax.numpy as jnp
from jax import lax
from jax.experimental import pallas as pl
from jax.experimental.pallas import tpu as pltpu
from jax.sharding import PartitionSpec as P

bf16 = jnp.bfloat16
f32 = jnp.float32
VMEM = pl.BlockSpec(memory_space=pltpu.VMEM)


def call(body, outs, ins, flops, name, grant=16):
    moved = sum(x.size * x.dtype.itemsize for x in list(ins) + list(outs))
    return pl.pallas_call(
        body,
        out_shape=outs,
        in_specs=[VMEM] * len(ins),
        out_specs=[VMEM] * len(outs),
        compiler_params=pltpu.CompilerParams(vmem_limit_bytes=grant * 2**20),
        cost_estimate=pl.CostEstimate(flops=flops, bytes_accessed=moved, transcendentals=0),
        name=name,
    )(*ins)


def shape(*dims, dtype=bf16):
    return jax.ShapeDtypeStruct(dims, dtype)


def dot(left, right):
    return jnp.dot(left, right, preferred_element_type=f32)


def contract(left, right, axis_left, axis_right):
    dims = (((axis_left,), (axis_right,)), ((), ()))
    return lax.dot_general(left, right, dims, preferred_element_type=f32)


def split(value):
    high = value.astype(bf16)
    return high, (value - high.astype(f32)).astype(bf16)


def product(left, right):
    return dot(left[0], right[0]) + (dot(left[0], right[1]) + dot(left[1], right[0]))


def block(wide):
    size = wide.shape[1] // 2
    real, imag = wide[:, :size], wide[:, size:]
    return jnp.concatenate([wide, jnp.concatenate([-imag, real], axis=1)], axis=0)


def both_of(pair, form):
    return form(pair[0]), form(pair[1])


def couple(rows_h, rows_s, shift_real, shift_imag):
    margin = rows_s.astype(f32)
    real = (rows_h.astype(f32) - shift_real * margin).astype(bf16)
    imag = (-shift_imag * margin).astype(bf16)
    return real, imag


def invert_body(shift, pivot_h, pivot_s, inverse):
    size = pivot_h.shape[0]
    shift_real, shift_imag = shift[:, 0:1], shift[:, 1:2]
    margin = pivot_s[...].astype(f32)
    real = pivot_h[...].astype(f32) - shift_real * margin
    imag = -shift_imag * margin
    on_diag = lax.broadcasted_iota(jnp.int32, (size, size), 0) == lax.broadcasted_iota(
        jnp.int32, (size, size), 1
    )

    def scales(axis):
        diag_real = jnp.sum(jnp.where(on_diag, real, 0.0), axis=axis, keepdims=True)
        diag_imag = jnp.sum(jnp.where(on_diag, imag, 0.0), axis=axis, keepdims=True)
        denom = diag_real * diag_real + diag_imag * diag_imag
        return diag_real / denom, -diag_imag / denom

    col_real, col_imag = scales(0)
    err_real = jnp.where(on_diag, 0.0, imag * col_imag - real * col_real)
    err_imag = jnp.where(on_diag, 0.0, -(real * col_imag + imag * col_real))
    one = jnp.concatenate([jnp.where(on_diag, 1.0, 0.0), jnp.zeros((size, size), f32)], axis=1)
    err = jnp.concatenate([err_real, err_imag], axis=1)
    err_pair = split(err)
    err2 = product(err_pair, both_of(err_pair, block))
    err2_pair = split(err2)
    square = both_of(err2_pair, block)
    err3 = product(err_pair, square)
    err4_pair = split(product(err2_pair, square))
    first = one + err + err2 + err3
    fourth = both_of(err4_pair, block)
    second = first + product(split(first), fourth)
    err8_pair = split(product(err4_pair, fourth))
    total = second + product(split(second), both_of(err8_pair, block))
    sum_real, sum_imag = total[:, :size], total[:, size:]
    row_real, row_imag = scales(1)
    inv_real = row_real * sum_real - row_imag * sum_imag
    inv_imag = row_real * sum_imag + row_imag * sum_real
    inverse[0], inverse[1] = split(jnp.concatenate([inv_real, inv_imag], axis=1))


def solve(rows_h, rows_s, shift, inverse):
    coupling = jnp.concatenate(couple(rows_h, rows_s, shift[:, 0:1], shift[:, 1:2]), axis=1)
    return (dot(coupling, block(inverse[0])) + dot(coupling, block(inverse[1]))).astype(bf16)


def pack_body(panel_h, panel_s, front_h, front_s, out, panels, fronts, buffer, sems):
    half = panels.shape[1] // 2
    share, size = fronts.shape[1], out.shape[2]
    shares = panels.shape[1] // share
    at = pl.ds(pl.multiple_of(lax.axis_index("col") * 2 * half, 2 * half), 2 * half)
    of = pl.ds(pl.multiple_of(lax.rem(lax.axis_index("pole"), shares) * share, share), share)
    loads = [
        pltpu.make_async_copy(panel_h.at[at], panels.at[0], sems.at[0]),
        pltpu.make_async_copy(panel_s.at[at], panels.at[1], sems.at[1]),
        pltpu.make_async_copy(front_h.at[of], fronts.at[0], sems.at[2]),
        pltpu.make_async_copy(front_s.at[of], fronts.at[1], sems.at[3]),
    ]
    rows = out.shape[0] // 2
    stores = []

    def send(first, low, height):
        where = (pl.ds(first, rows), pl.ds(low, height))
        stores.append(
            pltpu.make_async_copy(buffer.at[where], out.at[where], sems.at[4 + len(stores)])
        )
        stores[-1].start()

    for load in loads:
        load.start()
    loads[0].wait()
    loads[1].wait()
    for first in (0, rows):
        for row in range(first, first + rows):
            core = row % 2
            for part in range(2):
                low = part * half
                buffer[row, low : low + half] = panels[part, core * half : (core + 1) * half]
        send(first, 0, 2 * half)
    loads[2].wait()
    loads[3].wait()
    for first in (0, rows):
        for row in range(first, first + rows):
            for part in range(2):
                low = 2 * half + part * share
                buffer[row, low : low + share] = fronts[part, :, row * size : (row + 1) * size]
        send(first, 2 * half, 2 * share)
    for store in stores:
        store.wait()


def solve_body(shift, received, inverse, solved, up, down):
    strips, rows, size = received.shape
    half = solved.shape[0] // strips
    rows_h = received[:, :half].reshape(strips * half, size)
    rows_s = received[:, half : 2 * half].reshape(strips * half, size)
    solved[...] = solve(rows_h, rows_s, shift, inverse)
    up[...] = received[: up.shape[0], 2 * half :]
    down[...] = received[strips - down.shape[0] :, 2 * half :]


def ordered(mine, other):
    low = lax.rem(lax.axis_index("row"), 2) == 0
    return jnp.where(low, mine, other), jnp.where(low, other, mine)


def fold(member, out, at):
    pieces = out.shape[0]
    half = out.shape[1] // 2
    cols = 2 * member.shape[1] // 128
    low_lane = lax.broadcasted_iota(jnp.int32, (half, 128), 1) < 64
    for pole in range(pieces // cols):
        for pair in range(cols // 2):
            rows = pole * 2 * half
            top = member[rows : rows + half, pair * 128 : pair * 128 + 128]
            bottom = member[rows + half : rows + 2 * half, pair * 128 : pair * 128 + 128]
            even = jnp.where(low_lane, top, pltpu.roll(bottom, 64, 1))
            odd = jnp.where(low_lane, pltpu.roll(top, 64, 1), bottom)
            poles = pieces // cols
            out[2 * pair * poles + pole, at : at + half] = even.astype(out.dtype)
            out[(2 * pair + 1) * poles + pole, at : at + half] = odd.astype(out.dtype)


def half_column(solved, ancestor, core):
    strips, half, size = ancestor.shape[1], ancestor.shape[2] // 2, ancestor.shape[3]
    at = pl.ds(pl.multiple_of(core * half, half), half)
    rows = solved[...]
    by_real = contract(rows, ancestor[0, :, at, :].reshape(strips * half, size), 0, 0)
    by_imag = contract(rows, ancestor[1, :, at, :].reshape(strips * half, size), 0, 0)
    return by_real[:size] - by_imag[size:], by_real[size:] + by_imag[:size]


def own_column_body(
    shift, weight, panel_h, panel_s, inverse, mine, ancestor, part, right, base
):
    size = part.shape[1]
    part[:size], part[size:] = half_column(mine, ancestor, lax.rem(lax.axis_index("row"), 2))
    solved = solve(panel_h[...], panel_s[...], shift, inverse)
    right[:size] = solved[:, :size]
    right[size:] = solved[:, size:]
    whole = inverse[0].astype(f32) + inverse[1].astype(f32)
    density = weight[:, 0:1] * whole[:, size:] + weight[:, 1:2] * whole[:, :size]
    first_device = (lax.axis_index("row") == 0) & (lax.axis_index("col") == 0)
    base[...] = jnp.where(first_device, density.T, 0.0)


def column_body(weight, other, ancestor, part, right, base, out, buffer, sems):
    size = part.shape[1]
    half = out.shape[1] // 2
    part_real, part_imag = half_column(other, ancestor, 1 - lax.rem(lax.axis_index("row"), 2))
    part_real += part[:size]
    part_imag += part[size:]
    stores = [
        pltpu.make_async_copy(buffer.at[:, rows], out.at[:, rows], sems.at[index])
        for index, rows in enumerate((pl.ds(0, half), pl.ds(half, half)))
    ]
    weight_real, weight_imag = weight[:, 0:1], weight[:, 1:2]
    density = -(weight_real * part_imag + weight_imag * part_real)
    fold(density, buffer, 0)
    stores[0].start()
    twin = -(weight_real * part_real - weight_imag * part_imag)
    high, low = split(jnp.concatenate([density, twin], axis=1))
    pivot = base[...] - (dot(high, right[...]) + dot(low, right[...]))
    fold(pivot, buffer, half)
    stores[1].start()
    for store in stores:
        store.wait()


def sums_body(parts, spread, rows, copies, shares, sems):
    half, width = parts.shape[1] // 2, rows.shape[1]
    total = jnp.sum(parts[:, half:].astype(f32), axis=0)
    copies[...] = jnp.broadcast_to(total[None].astype(copies.dtype), copies.shape)
    stores = [
        pltpu.make_async_copy(copies, spread, sems.at[0]),
        pltpu.make_async_copy(shares, rows, sems.at[1]),
    ]
    stores[0].start()
    total = jnp.sum(parts[:, :half].astype(f32), axis=0)
    shares[:half] = total[:, :width]
    shares[half:] = total[:, width:]
    stores[1].start()
    for store in stores:
        store.wait()


def pivot_body(parts, out):
    half = parts.shape[1]
    width = 64
    cols = out.shape[1] // width
    total = jnp.sum(parts[...].astype(f32).reshape(-1, cols, half, 128), axis=0)
    for index in range(128 // width):
        lanes = slice(index * width, (index + 1) * width)
        strips = [total[col][:, lanes] for col in range(cols)]
        out[index * half : (index + 1) * half] = jnp.concatenate(strips, axis=1)


def update_body(shift, pattern, panel_h, panel_s, mine, other, out, mask):
    here = lax.broadcasted_iota(jnp.int32, pattern.shape, 1) == lax.axis_index("row")
    column = jnp.sum(jnp.where(here, pattern[...], 0).astype(f32), axis=1, keepdims=True)
    mask[...] = jnp.broadcast_to(column, mask.shape)
    strips, rows = out.shape[0], out.shape[1] * out.shape[2]
    half = mine.shape[0] // strips
    group = 4
    top, bottom = ordered(mine[...], other[...])
    real, imag = couple(panel_h[...], panel_s[...], shift[:, 0:1], shift[:, 1:2])
    wide = jnp.concatenate(
        [jnp.concatenate([real, -imag], axis=1), jnp.concatenate([imag, real], axis=1)], axis=0
    )
    for first in range(0, strips, group):
        solved = jnp.concatenate(
            [
                member[strip * half : (strip + 1) * half]
                for strip in range(first, first + group)
                for member in (top, bottom)
            ],
            axis=0,
        )
        update = contract(solved, wide, 1, 1)
        out[first : first + group] = update.reshape((group,) + out.shape[1:])


def relay_body(up, down, from_below, from_above, below, above):
    more = up.shape[0]
    less = below.shape[0] - (below.shape[0] + more) // 3
    half = below.shape[0] - less
    below[:less] = down[more - less :]
    below[less:] = from_below[:half]
    above[:less] = up[:less]
    above[less:] = from_above[more - half :]


def schur_tiles(shift, mask, update, members, buffer, out, sems):
    strips, count, share, size = out.shape[1:]
    pole = lax.axis_index("pole")
    shift_real, shift_imag = shift[:, 0:1], shift[:, 1:2]
    copies = []
    for member, start, length, step, first in members:
        at = lax.rem(pole + count + step, count)
        for index in range(length):
            strip = first + index
            here = mask[strip : strip + 1, :]
            margin = here * member[start + index, share:].astype(f32)
            real = here * member[start + index, :share].astype(f32) - shift_real * margin
            buffer[0, strip, at] = (real - update[strip, at, :, :size]).astype(bf16)
            buffer[1, strip, at] = (-shift_imag * margin - update[strip, at, :, size:]).astype(bf16)
        where = (slice(None), pl.ds(first, length), at)
        copies.append(pltpu.make_async_copy(buffer.at[where], out.at[where], sems.at[len(copies)]))
        copies[-1].start()
    for copy in copies:
        copy.wait()


def schur_first_body(shift, mask, update, up, down, from_below, from_above, out, buffer, sems):
    more, less = up.shape[0], out.shape[1] - up.shape[0]
    members = (
        (up, 0, more, 0, 0),
        (down, more - less, less, 0, more),
        (from_below, 0, more, -1, 0),
        (from_above, 0, more, 1, less),
    )
    schur_tiles(shift, mask, update, members, buffer, out, sems)


def schur_last_body(shift, mask, update, below, above, begun, out, buffer, sems):
    del begun
    half = out.shape[1] // 2
    less = below.shape[0] - half
    members = (
        (below, 0, less, -1, 2 * half - less),
        (below, less, half, -2, 0),
        (above, 0, less, 1, 0),
        (above, less, half, 2, half),
    )
    schur_tiles(shift, mask, update, members, buffer, out, sems)


def shards(
    front_h,
    front_s,
    panel_h,
    panel_s,
    pivot_h,
    pivot_s,
    pole_shift,
    pole_weight,
    pattern,
    ancestor_inverse,
):
    row_count = lax.axis_size("row")
    col_count = lax.axis_size("col")
    pole_count = lax.axis_size("pole")
    col_index = lax.axis_index("col")
    size = pivot_h.shape[0]
    width = size // col_count
    piece = size // pole_count
    half = width // 2
    neighbour = [(i, i ^ 1) for i in range(row_count)]

    quarters = 4
    share = width // quarters

    (sent,) = pl.pallas_call(
        pack_body,
        out_shape=[shape(row_count, width + 2 * share, size)],
        in_specs=[pl.BlockSpec(memory_space=pl.ANY)] * 4,
        out_specs=[pl.BlockSpec(memory_space=pl.ANY)],
        scratch_shapes=[
            pltpu.VMEM((2, width, size), bf16),
            pltpu.VMEM((2, share, row_count * size), bf16),
            pltpu.VMEM((row_count, width + 2 * share, size), bf16),
            pltpu.SemaphoreType.DMA((8,)),
        ],
        cost_estimate=pl.CostEstimate(flops=0, bytes_accessed=2**20, transcendentals=0),
        name="pack",
    )(panel_h, panel_s, front_h, front_s)
    received = lax.all_to_all(sent, "row", split_axis=0, concat_axis=0, tiled=True)

    (inverse,) = call(
        invert_body,
        [shape(2, size, 2 * size)],
        [pole_shift, pivot_h, pivot_s],
        6 * 4 * 3 * 2 * size**3,
        "pivot_inverse",
    )
    less = 3 * row_count // 8
    more = row_count - less
    mine, up, down = call(
        solve_body,
        [shape(row_count * half, 2 * size)] + [shape(more, 2 * share, size)] * 2,
        [pole_shift, received, inverse],
        2 * 8 * row_count * half * size * size,
        "solved_rows",
    )
    other = lax.ppermute(mine, "row", neighbour)
    ancestor = ancestor_inverse.reshape(2, row_count, width, size)
    part, right, base = call(
        own_column_body,
        [
            shape(2 * size, size, dtype=f32),
            shape(2 * size, size),
            shape(size, size, dtype=f32),
        ],
        [pole_shift, pole_weight, panel_h, panel_s, inverse, mine, ancestor],
        4 * row_count * width * size * size + 2 * 8 * size**3,
        "own_column",
    )
    folded = (col_count * pole_count, piece, 128)
    (both,) = pl.pallas_call(
        column_body,
        out_shape=[shape(*folded)],
        in_specs=[VMEM] * 6,
        out_specs=[pl.BlockSpec(memory_space=pl.ANY)],
        scratch_shapes=[pltpu.VMEM(folded, bf16), pltpu.SemaphoreType.DMA((2,))],
        compiler_params=pltpu.CompilerParams(vmem_limit_bytes=16 * 2**20),
        cost_estimate=pl.CostEstimate(
            flops=4 * row_count * width * size * size, bytes_accessed=2 * 2**20, transcendentals=0
        ),
        name="column",
    )(pole_weight, other, ancestor, part, right, base)

    onward = [(i, (i + 1) % pole_count) for i in range(pole_count)]
    back = [(i, (i - 1) % pole_count) for i in range(pole_count)]
    up, down, both = lax.optimization_barrier((up, down, both))
    from_below = lax.ppermute(up, "pole", onward)
    from_above = lax.ppermute(down, "pole", back)

    both = lax.all_to_all(both, ("col", "pole"), split_axis=0, concat_axis=0, tiled=True)
    sums = [
        shape(row_count * col_count, piece // 2, 128),
        shape(piece, width, dtype=f32),
    ]
    spread, rows_out = pl.pallas_call(
        sums_body,
        out_shape=sums,
        in_specs=[VMEM],
        out_specs=[pl.BlockSpec(memory_space=pl.ANY)] * 2,
        scratch_shapes=[pltpu.VMEM(x.shape, x.dtype) for x in sums]
        + [pltpu.SemaphoreType.DMA((2,))],
        compiler_params=pltpu.CompilerParams(vmem_limit_bytes=16 * 2**20),
        cost_estimate=pl.CostEstimate(flops=0, bytes_accessed=2**19, transcendentals=0),
        name="sums",
    )(both)
    below, above = call(
        relay_body,
        [shape(less + row_count // 2, 2 * share, size)] * 2,
        [up, down, from_below, from_above],
        10**11,
        "relay",
    )
    below = lax.ppermute(below, "pole", onward)
    above = lax.ppermute(above, "pole", back)
    spread = lax.all_to_all(spread, ("row", "col"), split_axis=0, concat_axis=0, tiled=True)
    (pivot_out,) = call(pivot_body, [shape(piece, size, dtype=f32)], [spread], 0, "pivot")

    update, mask = call(
        update_body,
        [
            shape(row_count, quarters, share, 2 * size, dtype=f32),
            shape(row_count, size, dtype=f32),
        ],
        [pole_shift, pattern, panel_h, panel_s, mine, other],
        8 * row_count * width * size * size,
        "update",
    )

    def tiles(body, ins, name, begun=()):
        tile = shape(2, row_count, quarters, share, size)
        return pl.pallas_call(
            body,
            out_shape=tile,
            in_specs=[VMEM] * len(ins) + [pl.BlockSpec(memory_space=pl.ANY)] * len(begun),
            out_specs=pl.BlockSpec(memory_space=pl.ANY),
            input_output_aliases={len(ins): 0} if begun else {},
            scratch_shapes=[pltpu.VMEM(tile.shape, bf16), pltpu.SemaphoreType.DMA((4,))],
            compiler_params=pltpu.CompilerParams(vmem_limit_bytes=16 * 2**20),
            cost_estimate=pl.CostEstimate(flops=0, bytes_accessed=3 * 2**20, transcendentals=0),
            name=name,
        )(*ins, *begun)

    fixed = [pole_shift, mask, update]
    schur = tiles(schur_first_body, fixed + [up, down, from_below, from_above], "schur_first")
    schur = tiles(schur_last_body, fixed + [below, above], "schur_last", (schur,))
    return (schur.reshape(1, 2, row_count, 1, width, size), rows_out.T, pivot_out.T)


def solution(mesh):
    in_specs = (
        P(("row", "col"), None),
        P(("row", "col"), None),
        P("row", None),
        P("row", None),
        P(),
        P(),
        P("pole", None),
        P("pole", None),
        P(),
        P("pole", None, None, "col", None, "row"),
    )
    out_specs = (
        P("pole", None, None, "col", None, "row"),
        P(("row", "col"), "pole"),
        P(None, "pole"),
    )
    return jax.shard_map(shards, mesh=mesh, in_specs=in_specs, out_specs=out_specs, check_vma=False)
```
